768 devices in a mesh: dp: 96 (over x, z, core), mp: 8 (over y).
Axes of the slice: x: 4, y: 8, z: 12, core: 2. Of those that a mesh axis runs over, the one named last changes fastest.
Arguments:
- hidden_rows: bfloat16 [49152, 2048], P('dp'), may hold values from -8 to 8
- lengths: int32 [96], P('dp'), may hold values from 256 to 512, as said below
- pair_order: int32 [96], replicated, may hold values from 0 to 95, each once
- gain_attn: float32 [2048], replicated, may hold values from 0.1 to 1.9
- w_query: bfloat16 [2048, 2048], P(None, 'mp')
- key_weight: bfloat16 [2048, 512], P(None, 'mp'), may hold values from -0.125 to 0.125
- value_weight: bfloat16 [2048, 512], P(None, 'mp'), may hold values from -0.125 to 0.125
- w_out: bfloat16 [2048, 2048], P('mp'), may hold values from -0.125 to 0.125
- gain_final: float32 [2048], replicated, may hold values from 0.1 to 1.9
- w_head: float32 [2048], replicated, may hold values from -1.5 to 1.5
Outputs:
- loss: float32 [], replicated
- rewards: float32 [96], replicated
- grad_out_proj: float32 [2048, 2048], P(None, 'mp')
- grad_head: float32 [2048], P('mp')
- grad_gain: float32 [2048], P('mp')
The draws below stay inside these ranges and needn't reach their ends.
Inputs may be any that keep to these rules, and one draw needn't show every extreme that they name: The one entry of `lengths` on a data shard is the length of the sequence packed from that shard's first row on. `pair_order`: entries 2p and 2p+1 name the chosen and the rejected sequence of pair p; every sequence is named once.
All inputs are finite; a program needn't handle non-finite values.
Results may differ from the reference program's by a relative error of at most 0.009.
The reference program's roundings to bfloat16 on the way count: a program that leaves them out, or rounds other values in their place, can miss the bound.
Values may be sent and summed in bfloat16 or wider, within the bound.
No kernel may reach another device: no remote copies, remote signals or barrier semaphores. Data moves between devices by JAX's collectives and lax.ppermute only.
A program may use at most 32 MiB of HBM per device.

```python
import jax
import jax.numpy as jnp
from jax import lax

MODEL_WIDTH = 2048
QUERY_HEADS = 32
KEY_VALUE_HEADS = 8
HEAD_SIZE = 64
SHARD_TOKEN_ROWS = 512
SEQ_DEV = 1
LMAX = 512
LMIN = 256
TOKENS = 49152
SEQS_ALL = 96
N_DP = 96
N_MP = 8


def common_direction(key):
    return jnp.clip(jax.random.normal(key, (MODEL_WIDTH,), jnp.float32), -4.0, 4.0)


def draw_hidden_rows(key, part):
    direction = common_direction(key)
    key = jax.random.fold_in(key, 13)
    sign_key, noise_key = jax.random.split(key, 2)
    pair_bits = jax.random.randint(sign_key, (TOKENS // 2, 1), 0, 2, dtype=jnp.int32)
    pair_signs = (2 * pair_bits - 1).astype(jnp.float32)
    signs = jnp.concatenate([pair_signs, -pair_signs], axis=1).reshape(TOKENS, 1)
    noise = jnp.clip(jax.random.normal(noise_key, (TOKENS, MODEL_WIDTH), jnp.float32), -4.0, 4.0)
    rows = 1.5 * signs * direction[None, :] + noise
    return jnp.clip(rows, -8.0, 8.0).astype(jnp.bfloat16)


def draw_w_head(key, part):
    direction = common_direction(key)
    key = jax.random.fold_in(key, 17)
    own = jnp.clip(jax.random.normal(key, (MODEL_WIDTH,), jnp.float32), -4.0, 4.0)
    return jnp.clip(0.25 * (0.9 * direction + 0.44 * own), -1.5, 1.5)


def draw_lengths(key, part):
    key = jax.random.fold_in(key, 7)
    drawn = jax.random.randint(key, (SEQS_ALL,), LMIN, LMAX + 1, dtype=jnp.int32)
    return drawn.at[0].set(LMAX).at[1].set(LMIN)


def draw_w_query(key, part):
    key = jax.random.fold_in(key, 11)
    base = jax.random.normal(key, (MODEL_WIDTH, QUERY_HEADS * HEAD_SIZE), jnp.float32) * MODEL_WIDTH ** (-0.5)
    return base.astype(jnp.bfloat16)


def block_scale(key, dims, pieces, smallest, high):
    factor_of, own = 1.0, jax.random.fold_in(key, 6)
    for axis_at, blocks in pieces:
        draws = jnp.exp(jax.random.uniform(jax.random.fold_in(own, axis_at), (blocks,), jnp.float32, smallest / len(pieces), high / len(pieces)))
        factor_of = factor_of * jnp.repeat(draws, dims[axis_at] // blocks).reshape([-1 if axis == axis_at else 1 for axis in range(len(dims))])
    return factor_of


def centred(rng, dims, scale, most, pieces=(), kind=jnp.bfloat16):
    values = jax.random.normal(rng, dims, jnp.float32) * scale
    if len(pieces) > 0:
        values = block_scale(rng, dims, pieces, -0.22, 0.18) * values
    return jnp.clip(values, min=-most, max=most).astype(kind)


def setup_inputs(seed: int = 0) -> dict:
    splits = jax.random.split(jax.random.key(seed), 11)
    return {
        "hidden_rows": draw_hidden_rows(jax.random.fold_in(splits[10], 71), 0),
        "lengths": draw_lengths(jax.random.fold_in(splits[10], 71), 0),
        "pair_order": jax.random.permutation(splits[2], SEQS_ALL).astype(jnp.int32),
        "gain_attn": jnp.clip(1.0 + 0.18 * jax.random.normal(splits[3], (MODEL_WIDTH,), jnp.float32), 0.1, 1.9),
        "w_query": draw_w_query(jax.random.fold_in(splits[10], 71), 0),
        "key_weight": centred(splits[5], (MODEL_WIDTH, KEY_VALUE_HEADS * HEAD_SIZE), MODEL_WIDTH ** -0.5, 0.125, ((1, 8),)),
        "value_weight": centred(splits[6], (MODEL_WIDTH, KEY_VALUE_HEADS * HEAD_SIZE), MODEL_WIDTH ** -0.5, 0.125, ((1, 8),)),
        "w_out": centred(splits[7], (QUERY_HEADS * HEAD_SIZE, MODEL_WIDTH), (QUERY_HEADS * HEAD_SIZE) ** -0.5, 0.125, ((0, 8),)),
        "gain_final": jnp.clip(1.0 + 0.18 * jax.random.normal(splits[8], (MODEL_WIDTH,), jnp.float32), 0.1, 1.9),
        "w_head": draw_w_head(jax.random.fold_in(splits[10], 71), 0),
    }


EPS = 1e-05
THETA = 500000.0

def positions_of(lens, rows):
    ends = jnp.cumsum(lens).astype(jnp.int32)
    starts = (ends - lens).astype(jnp.int32)
    row_ids = jnp.arange(rows, dtype=jnp.int32)
    inside = (row_ids[:, None] >= starts[None, :]) & (row_ids[:, None] < ends[None, :])
    member = inside.astype(jnp.int32)
    segment = lax.optimization_barrier(jnp.sum((row_ids[:, None] >= ends[None, :]).astype(jnp.int32), axis=1))
    offset = lax.optimization_barrier(jnp.sum(member * starts[None, :], axis=1)) + (1 - lax.optimization_barrier(jnp.sum(member, axis=1))) * ends[-1]
    return (segment, (row_ids - offset).astype(jnp.int32), member)

def rope_tables(positions):
    half = HEAD_SIZE // 2
    freq = THETA ** (-jnp.arange(half, dtype=jnp.float32) * 2.0 / HEAD_SIZE)
    angle = positions.astype(jnp.float32)[:, None] * freq[None, :]
    return (jnp.cos(angle), jnp.sin(angle))

def rotate(vecs, cosine, sine):
    half = vecs.shape[-1] // 2
    first = vecs[..., :half]
    second = vecs[..., half:]
    cos_b = cosine[:, None, :]
    sin_b = sine[:, None, :]
    return jnp.concatenate([first * cos_b - second * sin_b, second * cos_b + first * sin_b], axis=-1)

def reference(hidden_rows, lengths, pair_order, gain_attn, w_query, key_weight, value_weight, w_out, gain_final, w_head):
    shard_rows = hidden_rows.reshape(N_DP, SHARD_TOKEN_ROWS, MODEL_WIDTH)
    shard_lengths = lengths.reshape(N_DP, SEQ_DEV)
    head_group = QUERY_HEADS // KEY_VALUE_HEADS
    cols = QUERY_HEADS * HEAD_SIZE // N_MP

    def forward(item):
        rows_in, lens = item
        segment, positions, member = positions_of(lens, SHARD_TOKEN_ROWS)
        x32 = rows_in.astype(jnp.float32)
        normalized_rows = (x32 * lax.rsqrt(lax.optimization_barrier(jnp.mean(x32 * x32, axis=1, keepdims=True)) + EPS) * gain_attn).astype(jnp.bfloat16)
        cosine, sine = rope_tables(positions)
        query = jnp.dot(normalized_rows, w_query, preferred_element_type=jnp.float32).reshape(SHARD_TOKEN_ROWS, QUERY_HEADS, HEAD_SIZE)
        query = rotate(query, cosine, sine).astype(jnp.bfloat16)
        key_vectors = jnp.dot(normalized_rows, key_weight, preferred_element_type=jnp.float32).reshape(SHARD_TOKEN_ROWS, KEY_VALUE_HEADS, HEAD_SIZE)
        key_vectors = rotate(key_vectors, cosine, sine).astype(jnp.bfloat16)
        value_rows = jnp.dot(normalized_rows, value_weight, preferred_element_type=jnp.float32).astype(jnp.bfloat16).reshape(SHARD_TOKEN_ROWS, KEY_VALUE_HEADS, HEAD_SIZE)
        key_rep = jnp.repeat(key_vectors, head_group, axis=1)
        value_rep = jnp.repeat(value_rows, head_group, axis=1)
        scores = jnp.einsum('qhd,khd->hqk', query.astype(jnp.float32), key_rep.astype(jnp.float32)) * HEAD_SIZE ** (-0.5)
        row_ids = jnp.arange(SHARD_TOKEN_ROWS, dtype=jnp.int32)
        allowed = (segment[:, None] == segment[None, :]) & (row_ids[None, :] <= row_ids[:, None])
        scores = jnp.where(allowed[None], scores, -1e+30)
        top = lax.optimization_barrier(jnp.max(scores, axis=2, keepdims=True))
        weights = jnp.exp(scores - top)
        probs = (weights / lax.optimization_barrier(jnp.sum(weights, axis=2, keepdims=True))).astype(jnp.bfloat16)
        mixed = jnp.einsum('hqk,khd->qhd', probs.astype(jnp.float32), value_rep.astype(jnp.float32))
        mixed = mixed.astype(jnp.bfloat16).reshape(SHARD_TOKEN_ROWS, QUERY_HEADS * HEAD_SIZE)
        partials = jnp.einsum('rgc,gcd->grd', mixed.reshape(SHARD_TOKEN_ROWS, N_MP, cols).astype(jnp.float32), w_out.reshape(N_MP, cols, MODEL_WIDTH).astype(jnp.float32))
        rounded = lax.optimization_barrier(partials.astype(jnp.bfloat16))
        attended = lax.optimization_barrier(jnp.sum(rounded.astype(jnp.float32), axis=0))
        resid = x32 + attended
        scale = lax.rsqrt(lax.optimization_barrier(jnp.mean(resid * resid, axis=1)) + EPS)
        unit = resid * scale[:, None]
        row_score = lax.optimization_barrier(jnp.sum(unit * gain_final * w_head, axis=1))
        part = lax.optimization_barrier(jnp.sum(member.astype(jnp.float32) * row_score[:, None], axis=0)) / lens.astype(jnp.float32)
        return (part, mixed, unit, scale)
    parts, mixed_all, unit_all, scale_all = lax.map(forward, (shard_rows, shard_lengths))
    rewards = parts.reshape(SEQS_ALL)
    picked = rewards[pair_order].reshape(SEQS_ALL // 2, 2)
    margin = picked[:, 0] - picked[:, 1]
    loss = jnp.sum(jax.nn.softplus(-margin))
    sig = jax.nn.sigmoid(-margin)
    per_pos = jnp.stack([-sig, sig], axis=1).reshape(SEQS_ALL)
    dreward = jnp.zeros((SEQS_ALL,), jnp.float32).at[pair_order].set(per_pos)
    coef_all = dreward.reshape(N_DP, SEQ_DEV) / shard_lengths.astype(jnp.float32)

    def backward(carry, item):
        grad_sum, pooled = carry
        mixed, unit, scale, coef, lens = item
        _, _, member = positions_of(lens, SHARD_TOKEN_ROWS)
        row_coef = lax.optimization_barrier(jnp.sum(member.astype(jnp.float32) * coef[None, :], axis=1))
        dunit = row_coef[:, None] * (w_head * gain_final)[None, :]
        inner = lax.optimization_barrier(jnp.mean(dunit * unit, axis=1))
        dresid = scale[:, None] * (dunit - unit * inner[:, None])
        grad_sum = grad_sum + jnp.dot(mixed.astype(jnp.float32).T, dresid, preferred_element_type=jnp.float32, precision=lax.Precision.HIGHEST)
        pooled = pooled + lax.optimization_barrier(jnp.sum(row_coef[:, None] * unit, axis=0))
        return ((grad_sum, pooled), None)
    start = (jnp.zeros((QUERY_HEADS * HEAD_SIZE, MODEL_WIDTH), jnp.float32), jnp.zeros((MODEL_WIDTH,), jnp.float32))
    (grad_out_proj, pooled), _ = lax.scan(backward, start, (mixed_all, unit_all, scale_all, coef_all, shard_lengths))
    return (loss, rewards, grad_out_proj, gain_final * pooled, w_head * pooled)
```

```python
import jax
import jax.numpy as jnp
from jax import lax
from jax.sharding import PartitionSpec as P

QUERY_HEADS = 32
KEY_VALUE_HEADS = 8
HEAD_SIZE = 64
NX, NZ, NCORE = 4, 12, 2


EPS = 1e-05
THETA = 500000.0


def positions_of(lens, rows):
    ends = jnp.cumsum(lens)
    starts = ends - lens
    row_ids = jnp.arange(rows, dtype=jnp.int32)
    inside = (row_ids[:, None] >= starts[None, :]) & (row_ids[:, None] < ends[None, :])
    member = inside.astype(jnp.int32)
    segment = jnp.sum((row_ids[:, None] >= ends[None, :]).astype(jnp.int32), axis=1)
    offset = jnp.sum(member * starts[None, :], axis=1) + (1 - jnp.sum(member, axis=1)) * ends[-1]
    return (segment, row_ids - offset, member)


def rope_tables(positions):
    half = HEAD_SIZE // 2
    freq = THETA ** (-jnp.arange(half, dtype=jnp.float32) * 2.0 / HEAD_SIZE)
    angle = positions.astype(jnp.float32)[:, None] * freq[None, :]
    return (jnp.cos(angle), jnp.sin(angle))


def rotate(vecs, cosine, sine):
    half = vecs.shape[-1] // 2
    first = vecs[..., :half]
    second = vecs[..., half:]
    cos_b = cosine[:, None, :]
    sin_b = sine[:, None, :]
    return jnp.concatenate(
        [first * cos_b - second * sin_b, second * cos_b + first * sin_b], axis=-1
    )


def dp_groups():
    near = [[(x * NZ + z) * NCORE + c for x in range(NX) for c in range(NCORE)] for z in range(NZ)]
    far = [[(x * NZ + z) * NCORE + c for z in range(NZ)] for x in range(NX) for c in range(NCORE)]
    return near, far


def swap(parts, groups):
    return lax.all_to_all(parts, "dp", 0, 0, tiled=True, axis_index_groups=groups)


def body(
    hidden_rows,
    lengths,
    pair_order,
    gain_attn,
    w_query,
    key_weight,
    value_weight,
    w_out,
    gain_final,
    w_head,
):
    rows, width = hidden_rows.shape
    q_heads = w_query.shape[1] // HEAD_SIZE
    kv_heads = key_weight.shape[1] // HEAD_SIZE
    head_group = QUERY_HEADS // KEY_VALUE_HEADS
    n_mp = lax.axis_size("mp")
    n_dp = lax.axis_size("dp")
    my_part = lax.axis_index("mp")
    feat = width // n_mp
    near, far = dp_groups()
    w_cols = lax.all_to_all(w_out, "mp", split_axis=1, concat_axis=0, tiled=True)
    segment, positions, member_int = positions_of(lengths, rows)
    member = member_int.astype(jnp.float32)[:, 0]
    lens_f = lengths.astype(jnp.float32)
    x32 = hidden_rows.astype(jnp.float32)
    normalized_rows = (
        x32 * lax.rsqrt(jnp.mean(x32 * x32, axis=1, keepdims=True) + EPS) * gain_attn
    ).astype(jnp.bfloat16)
    cosine, sine = rope_tables(positions)
    query = jnp.dot(normalized_rows, w_query, preferred_element_type=jnp.float32).reshape(
        rows, q_heads, HEAD_SIZE
    )
    query = rotate(query, cosine, sine).astype(jnp.bfloat16)
    key_vectors = jnp.dot(normalized_rows, key_weight, preferred_element_type=jnp.float32).reshape(
        rows, kv_heads, HEAD_SIZE
    )
    key_vectors = rotate(key_vectors, cosine, sine).astype(jnp.bfloat16)
    value_rows = (
        jnp.dot(normalized_rows, value_weight, preferred_element_type=jnp.float32)
        .astype(jnp.bfloat16)
        .reshape(rows, kv_heads, HEAD_SIZE)
    )
    key_rep = jnp.repeat(key_vectors, head_group, axis=1)
    value_rep = jnp.repeat(value_rows, head_group, axis=1)
    row_ids = jnp.arange(rows, dtype=jnp.int32)
    scores = jnp.einsum(
        "qhd,khd->hqk", query, key_rep, preferred_element_type=jnp.float32
    ) * HEAD_SIZE ** (-0.5)
    allowed = (segment[:, None] == segment[None, :]) & (row_ids[None, :] <= row_ids[:, None])
    scores = jnp.where(allowed[None], scores, -1e30)
    top = jnp.max(scores, axis=2, keepdims=True)
    weights = jnp.exp(scores - top)
    probs = (weights / jnp.sum(weights, axis=2, keepdims=True)).astype(jnp.bfloat16)
    mixed = jnp.einsum("hqk,khd->qhd", probs, value_rep, preferred_element_type=jnp.float32)
    mixed = mixed.astype(jnp.bfloat16).reshape(rows, q_heads * HEAD_SIZE)

    mixed_all = lax.all_gather(mixed, "mp", axis=0, tiled=False)
    partials = jnp.einsum(
        "grc,gcd->grd",
        mixed_all,
        w_cols.reshape(n_mp, q_heads * HEAD_SIZE, feat),
        preferred_element_type=jnp.float32,
    ).astype(jnp.bfloat16)
    attended = jnp.sum(partials.astype(jnp.float32), axis=0)
    x_cols = lax.dynamic_slice_in_dim(hidden_rows, my_part * feat, feat, 1).astype(jnp.float32)
    gain_share = lax.dynamic_slice_in_dim(gain_final, my_part * feat, feat, 0)
    head_share = lax.dynamic_slice_in_dim(w_head, my_part * feat, feat, 0)
    both = gain_share * head_share
    resid = x_cols + attended
    stats = jnp.stack([jnp.sum(resid * resid, axis=1), jnp.sum(resid * both, axis=1)])
    stats = lax.all_to_all(
        jnp.broadcast_to(stats[None], (n_mp,) + stats.shape), "mp", 0, 0, tiled=True
    )
    stats = jnp.sum(stats, axis=0)
    scale = lax.rsqrt(stats[0] / width + EPS)
    row_score = stats[1] * scale
    my_reward = jnp.sum(member * row_score) / lens_f[0]
    rewards = lax.all_to_all(
        jnp.broadcast_to(my_reward, (n_dp, 1, 128)), "dp", 0, 0, tiled=True
    )[:, 0, 0]

    unit = resid * scale[:, None]
    weight = member / lens_f[0]
    dresid = (weight * scale)[:, None] * (both[None, :] - unit * (row_score / width)[:, None])
    grad_block = jnp.einsum(
        "grc,rd->gcd", mixed_all, dresid.astype(jnp.bfloat16), preferred_element_type=jnp.float32
    ).reshape(width, feat)
    pooled_block = jnp.sum(weight[:, None] * unit, axis=0)
    near_n, far_n = NX * NCORE, NZ
    piece = -(-(width + 1) // (near_n * far_n * 8)) * 8
    total_rows = piece * near_n * far_n
    block = jnp.concatenate(
        [
            grad_block.astype(jnp.bfloat16),
            jnp.pad(pooled_block[None], ((0, total_rows - width - 1), (0, 0))).astype(jnp.bfloat16),
        ],
        axis=0,
    )
    got = swap(block.reshape(near_n, far_n * piece, feat), near)

    total_seqs = rewards.shape[0]
    picked = rewards[pair_order].reshape(total_seqs // 2, 2)
    margin = picked[:, 0] - picked[:, 1]
    loss = jnp.sum(jax.nn.softplus(-margin))
    sig = jax.nn.sigmoid(-margin)
    per_pos = jnp.stack([-sig, sig], axis=1).reshape(total_seqs)
    dreward = jnp.zeros((total_seqs,), jnp.float32).at[pair_order].set(per_pos)
    my_z = (lax.axis_index("dp") // NCORE) % NZ
    near_dreward = lax.dynamic_slice_in_dim(dreward.reshape(NX, NZ, NCORE), my_z, 1, 1).reshape(near_n)
    summed = jnp.sum(got.astype(jnp.float32) * near_dreward[:, None, None], axis=0)
    got = swap(summed.astype(jnp.bfloat16).reshape(far_n, piece, feat), far)
    mine = jnp.sum(got.astype(jnp.float32), axis=0).astype(jnp.bfloat16)
    got = swap(jnp.broadcast_to(mine[None], (far_n, piece, feat)), far)
    got = swap(jnp.broadcast_to(got.reshape(1, far_n * piece, feat), (near_n, far_n * piece, feat)), near)
    got = got.reshape(total_rows, feat).astype(jnp.float32)
    grad_out_proj = got[:width]
    pooled = got[width]
    return (loss, rewards, grad_out_proj, gain_share * pooled, head_share * pooled)


def solution(mesh):
    placed = (
        P("dp", None),
        P("dp"),
        P(),
        P(),
        P(None, "mp"),
        P(None, "mp"),
        P(None, "mp"),
        P("mp", None),
        P(),
        P(),
    )
    return jax.shard_map(
        body,
        mesh=mesh,
        in_specs=placed,
        out_specs=(P(), P(), P(None, "mp"), P("mp"), P("mp")),
        check_vma=False,
    )
```

```python
import jax
import jax.numpy as jnp
from jax import lax
from jax.sharding import PartitionSpec as P

QUERY_HEADS = 32
KEY_VALUE_HEADS = 8
HEAD_SIZE = 64
NX, NZ, NCORE = 4, 12, 2


EPS = 1e-05
THETA = 500000.0


def positions_of(lens, rows):
    ends = jnp.cumsum(lens)
    starts = ends - lens
    row_ids = jnp.arange(rows, dtype=jnp.int32)
    inside = (row_ids[:, None] >= starts[None, :]) & (row_ids[:, None] < ends[None, :])
    member = inside.astype(jnp.int32)
    segment = jnp.sum((row_ids[:, None] >= ends[None, :]).astype(jnp.int32), axis=1)
    offset = jnp.sum(member * starts[None, :], axis=1) + (1 - jnp.sum(member, axis=1)) * ends[-1]
    return (segment, row_ids - offset, member)


def rope_tables(positions):
    half = HEAD_SIZE // 2
    freq = THETA ** (-jnp.arange(half, dtype=jnp.float32) * 2.0 / HEAD_SIZE)
    angle = positions.astype(jnp.float32)[:, None] * freq[None, :]
    return (jnp.cos(angle), jnp.sin(angle))


def rotate(vecs, cosine, sine):
    half = vecs.shape[-1] // 2
    first = vecs[..., :half]
    second = vecs[..., half:]
    cos_b = cosine[:, None, :]
    sin_b = sine[:, None, :]
    return jnp.concatenate(
        [first * cos_b - second * sin_b, second * cos_b + first * sin_b], axis=-1
    )


def device_of(x, z, core):
    return (x * NZ + z) * NCORE + core


def dp_groups():
    along_x = [[device_of(x, z, c) for x in range(NX)] for z in range(NZ) for c in range(NCORE)]
    along_z = [[device_of(x, z, c) for z in range(NZ)] for x in range(NX) for c in range(NCORE)]
    return along_x, along_z


def swap(parts, groups):
    return lax.all_to_all(parts, "dp", 0, 0, tiled=True, axis_index_groups=groups)


def to_sibling(x):
    pairs = [(i, i ^ 1) for i in range(NX * NZ * NCORE)]
    return lax.ppermute(x, "dp", pairs)


def body(
    hidden_rows,
    lengths,
    pair_order,
    gain_attn,
    w_query,
    key_weight,
    value_weight,
    w_out,
    gain_final,
    w_head,
):
    rows, width = hidden_rows.shape
    q_heads = w_query.shape[1] // HEAD_SIZE
    kv_heads = key_weight.shape[1] // HEAD_SIZE
    head_group = QUERY_HEADS // KEY_VALUE_HEADS
    n_mp = lax.axis_size("mp")
    n_dp = lax.axis_size("dp")
    my_part = lax.axis_index("mp")
    feat = width // n_mp
    along_x, along_z = dp_groups()
    core = lax.axis_index("dp") % NCORE
    half_rows = w_out.shape[0] // NCORE
    w_half = lax.dynamic_slice_in_dim(w_out, core * half_rows, half_rows, 0)
    w_half = lax.all_to_all(
        w_half.reshape(half_rows, n_mp, feat).swapaxes(0, 1), "mp", 0, 0, tiled=True
    )
    segment, positions, member_int = positions_of(lengths, rows)
    member = member_int.astype(jnp.float32)[:, 0]
    lens_f = lengths.astype(jnp.float32)
    x32 = hidden_rows.astype(jnp.float32)
    normalized_rows = (
        x32 * lax.rsqrt(jnp.mean(x32 * x32, axis=1, keepdims=True) + EPS) * gain_attn
    ).astype(jnp.bfloat16)
    cosine, sine = rope_tables(positions)
    query = jnp.dot(normalized_rows, w_query, preferred_element_type=jnp.float32).reshape(
        rows, q_heads, HEAD_SIZE
    )
    query = rotate(query, cosine, sine).astype(jnp.bfloat16)
    key_vectors = jnp.dot(normalized_rows, key_weight, preferred_element_type=jnp.float32).reshape(
        rows, kv_heads, HEAD_SIZE
    )
    key_vectors = rotate(key_vectors, cosine, sine).astype(jnp.bfloat16)
    value_rows = (
        jnp.dot(normalized_rows, value_weight, preferred_element_type=jnp.float32)
        .astype(jnp.bfloat16)
        .reshape(rows, kv_heads, HEAD_SIZE)
    )
    key_rep = jnp.repeat(key_vectors, head_group, axis=1)
    value_rep = jnp.repeat(value_rows, head_group, axis=1)
    row_ids = jnp.arange(rows, dtype=jnp.int32)
    scores = jnp.einsum(
        "qhd,khd->hqk", query, key_rep, preferred_element_type=jnp.float32
    ) * HEAD_SIZE ** (-0.5)
    allowed = (segment[:, None] == segment[None, :]) & (row_ids[None, :] <= row_ids[:, None])
    scores = jnp.where(allowed[None], scores, -1e30)
    top = jnp.max(scores, axis=2, keepdims=True)
    weights = jnp.exp(scores - top)
    probs = (weights / jnp.sum(weights, axis=2, keepdims=True)).astype(jnp.bfloat16)
    mixed = jnp.einsum("hqk,khd->qhd", probs, value_rep, preferred_element_type=jnp.float32)
    mixed = mixed.astype(jnp.bfloat16).reshape(rows, q_heads * HEAD_SIZE)

    mixed, w_half = lax.optimization_barrier((mixed, w_half))
    w_other = to_sibling(w_half)
    w_cols = jnp.concatenate(
        [jnp.where(core == 0, w_half, w_other), jnp.where(core == 0, w_other, w_half)], axis=1
    )

    mixed_all = lax.all_gather(mixed, "mp", axis=0, tiled=False)
    partials = jnp.einsum(
        "grc,gcd->grd",
        mixed_all,
        w_cols,
        preferred_element_type=jnp.float32,
    ).astype(jnp.bfloat16)
    attended = jnp.sum(partials.astype(jnp.float32), axis=0)
    x_cols = lax.dynamic_slice_in_dim(hidden_rows, my_part * feat, feat, 1).astype(jnp.float32)
    gain_share = lax.dynamic_slice_in_dim(gain_final, my_part * feat, feat, 0)
    head_share = lax.dynamic_slice_in_dim(w_head, my_part * feat, feat, 0)
    both = gain_share * head_share
    resid = x_cols + attended
    stats = jnp.stack([jnp.sum(resid * resid, axis=1), jnp.sum(resid * both, axis=1)])
    stats = lax.all_to_all(
        jnp.broadcast_to(stats[None], (n_mp,) + stats.shape), "mp", 0, 0, tiled=True
    )
    stats = jnp.sum(stats, axis=0)
    scale = lax.rsqrt(stats[0] / width + EPS)
    row_score = stats[1] * scale
    my_reward = jnp.sum(member * row_score) / lens_f[0]
    rewards = lax.all_to_all(
        jnp.broadcast_to(my_reward, (n_dp, 1, 128)), "dp", 0, 0, tiled=True
    )[:, 0, 0]

    unit = resid * scale[:, None]
    weight = member / lens_f[0]
    dresid = (weight * scale)[:, None] * (both[None, :] - unit * (row_score / width)[:, None])
    grad_block = jnp.einsum(
        "grc,rd->gcd", mixed_all, dresid.astype(jnp.bfloat16), preferred_element_type=jnp.float32
    ).reshape(width, feat)
    pooled_block = jnp.sum(weight[:, None] * unit, axis=0)
    half = width // NCORE
    piece = -(-(half + 1) // (NX * NZ * 8)) * 8
    half_ext = piece * NX * NZ
    extra = jnp.pad(pooled_block[None], ((0, half_ext - half - 1), (0, 0))).astype(jnp.bfloat16)
    grad_block = grad_block.astype(jnp.bfloat16).reshape(NCORE, half, feat)
    keep = jnp.concatenate([lax.dynamic_index_in_dim(grad_block, core, 0, False), extra], axis=0)
    send = jnp.concatenate([lax.dynamic_index_in_dim(grad_block, 1 - core, 0, False), extra], axis=0)
    got = to_sibling(send)

    total_seqs = rewards.shape[0]
    picked = rewards[pair_order].reshape(total_seqs // 2, 2)
    margin = picked[:, 0] - picked[:, 1]
    loss = jnp.sum(jax.nn.softplus(-margin))
    sig = jax.nn.sigmoid(-margin)
    per_pos = jnp.stack([-sig, sig], axis=1).reshape(total_seqs)
    dreward = jnp.zeros((total_seqs,), jnp.float32).at[pair_order].set(per_pos)
    me = lax.axis_index("dp")
    own = lax.dynamic_index_in_dim(dreward, me, 0, False)
    sib = lax.dynamic_index_in_dim(dreward, me ^ 1, 0, False)
    summed = keep.astype(jnp.float32) * own + got.astype(jnp.float32) * sib
    got = swap(summed.astype(jnp.bfloat16).reshape(NX, NZ * piece, feat), along_x)
    summed = jnp.sum(got.astype(jnp.float32), axis=0).astype(jnp.bfloat16)
    got = swap(summed.reshape(NZ, piece, feat), along_z)
    mine = jnp.sum(got.astype(jnp.float32), axis=0).astype(jnp.bfloat16)
    got = swap(jnp.broadcast_to(mine[None], (NZ, piece, feat)), along_z)
    got = swap(jnp.broadcast_to(got.reshape(1, NZ * piece, feat), (NX, NZ * piece, feat)), along_x)
    got = got.reshape(half_ext, feat)
    other = to_sibling(got)
    lower = jnp.where(core == 0, got, other)
    upper = jnp.where(core == 0, other, got)
    grad_out_proj = jnp.concatenate([lower[:half], upper[:half]], axis=0).astype(jnp.float32)
    pooled = got[half].astype(jnp.float32)
    return (loss, rewards, grad_out_proj, gain_share * pooled, head_share * pooled)


def solution(mesh):
    placed = (
        P("dp", None),
        P("dp"),
        P(),
        P(),
        P(None, "mp"),
        P(None, "mp"),
        P(None, "mp"),
        P("mp", None),
        P(),
        P(),
    )
    return jax.shard_map(
        body,
        mesh=mesh,
        in_specs=placed,
        out_specs=(P(), P(), P(None, "mp"), P("mp"), P("mp")),
        check_vma=False,
    )
```

```python
import functools

import jax
import jax.numpy as jnp
from jax import lax
from jax.experimental import pallas as pl
from jax.experimental.pallas import tpu as pltpu
from jax.sharding import PartitionSpec as P

QUERY_HEADS = 32
KEY_VALUE_HEADS = 8
HEAD_SIZE = 64
NX, NZ, NCORE = 4, 12, 2
NEAR = NX * NCORE

EPS = 1e-05
THETA = 500000.0
LANES = 128
F32 = jnp.float32
BF16 = jnp.bfloat16


def device_of(x, z, core):
    return (x * NZ + z) * NCORE + core


def dp_groups():
    along_x = [[device_of(x, z, c) for x in range(NX)] for z in range(NZ) for c in range(NCORE)]
    along_z = [[device_of(x, z, c) for z in range(NZ)] for x in range(NX) for c in range(NCORE)]
    near = [[device_of(x, z, c) for x in range(NX) for c in range(NCORE)] for z in range(NZ)]
    return along_x, along_z, near


def swap(parts, groups):
    return lax.all_to_all(parts, "dp", 0, 0, tiled=True, axis_index_groups=groups)


def to_sibling(x):
    pairs = [(i, i ^ 1) for i in range(NX * NZ * NCORE)]
    return lax.ppermute(x, "dp", pairs)


def dot(a, b, a_dim, b_dim, precision=None):
    return lax.dot_general(
        a, b, (((a_dim,), (b_dim,)), ((), ())), preferred_element_type=F32, precision=precision
    )


def rope_tables(positions):
    half = HEAD_SIZE // 2
    freq = THETA ** (-jnp.arange(half, dtype=F32) * 2.0 / HEAD_SIZE)
    angle = positions.astype(F32)[:, None] * jnp.tile(freq, LANES // half)[None, :]
    sign = jnp.tile(jnp.repeat(jnp.array([-1.0, 1.0], F32), half), LANES // HEAD_SIZE)
    return jnp.cos(angle), jnp.sin(angle) * sign[None, :]


def front_kernel(lens, x_ref, gain_ref, wq_ref, wk_ref, wv_ref, cos_ref, sin_ref, out_ref, k_ref, v_ref):
    step = pl.program_id(0)
    rows = x_ref.shape[0]
    x = x_ref[...].astype(F32)
    inv = lax.rsqrt(jnp.mean(x * x, axis=1, keepdims=True) + EPS)
    normed = (x * inv * gain_ref[...]).astype(BF16)
    cosine, sine = cos_ref[...], sin_ref[...]
    lane = lax.broadcasted_iota(jnp.int32, (rows, LANES), 1)
    first_half = (lane % HEAD_SIZE) < HEAD_SIZE // 2
    low = lane < HEAD_SIZE

    def rotate(t):
        partner = jnp.where(
            first_half, pltpu.roll(t, LANES - HEAD_SIZE // 2, 1), pltpu.roll(t, HEAD_SIZE // 2, 1)
        )
        return t * cosine + partner * sine

    query = dot(normed, wq_ref[...], 1, 0)
    key = dot(normed, wk_ref[...], 1, 0)
    value = dot(normed, wv_ref[...], 1, 0)
    key = rotate(jnp.concatenate([key, key], axis=1))
    value = jnp.concatenate([value, value], axis=1)
    here = pl.ds(pl.multiple_of(step * rows, rows), rows)
    k_ref[0, here, :] = jnp.where(low, key, 0.0).astype(BF16)
    k_ref[1, here, :] = jnp.where(low, 0.0, key).astype(BF16)
    v_ref[0, here, :] = jnp.where(low, value, 0.0).astype(BF16)
    v_ref[1, here, :] = jnp.where(low, 0.0, value).astype(BF16)
    pairs = query.shape[1] // LANES
    turned = [rotate(query[:, p * LANES : (p + 1) * LANES]).astype(BF16) for p in range(pairs)]
    used = lens[0]

    def attend(first, cols):
        row = first + lax.broadcasted_iota(jnp.int32, (rows, cols), 0)
        col = lax.broadcasted_iota(jnp.int32, (rows, cols), 1)
        allowed = (col <= row) & ((row >= used) == (col >= used))
        for p in range(pairs):
            total = jnp.zeros((rows, LANES), F32)
            for e in range(LANES // HEAD_SIZE):
                scores = dot(turned[p], k_ref[e, :cols, :], 1, 1) * HEAD_SIZE ** (-0.5)
                scores = jnp.where(allowed, scores, -1e30)
                top = jnp.max(scores, axis=1, keepdims=True)
                weights = jnp.exp(scores - top)
                probs = weights * (1.0 / jnp.sum(weights, axis=1, keepdims=True))
                total = total + dot(probs.astype(BF16), v_ref[e, :cols, :], 1, 0)
            out_ref[:, p * LANES : (p + 1) * LANES] = total.astype(BF16)

    for s in range(k_ref.shape[1] // rows):
        @pl.when(step == s)
        def _(s=s):
            attend(s * rows, (s + 1) * rows)


def front(hidden_rows, lengths, gain_attn, w_query, key_weight, value_weight):
    rows, width = hidden_rows.shape
    row = jnp.arange(rows, dtype=jnp.int32)
    cosine, sine = rope_tables(row - jnp.where(row >= lengths[0], lengths[0], 0))
    block = rows // 2
    whole = lambda a: pl.BlockSpec(a.shape, lambda i, s: (0, 0))
    by_rows = lambda cols: pl.BlockSpec((block, cols), lambda i, s: (i, 0))
    gain = gain_attn[None]
    return pl.pallas_call(
        front_kernel,
        out_shape=jax.ShapeDtypeStruct((rows, w_query.shape[1]), BF16),
        grid_spec=pltpu.PrefetchScalarGridSpec(
            num_scalar_prefetch=1,
            grid=(rows // block,),
            in_specs=[
                by_rows(width),
                whole(gain),
                whole(w_query),
                whole(key_weight),
                whole(value_weight),
                by_rows(LANES),
                by_rows(LANES),
            ],
            out_specs=by_rows(w_query.shape[1]),
            scratch_shapes=[pltpu.VMEM((2, rows, LANES), BF16), pltpu.VMEM((2, rows, LANES), BF16)],
        ),
        compiler_params=pltpu.CompilerParams(vmem_limit_bytes=48 * 2**20),
        cost_estimate=pl.CostEstimate(flops=1500000000, bytes_accessed=4000000, transcendentals=800000),
        name="front",
    )(lengths, hidden_rows, gain, w_query, key_weight, value_weight, cosine, sine)


def project_kernel(place, mixed_ref, w_ref, x_ref, gain_ref, head_ref, resid_ref, stats_ref):
    step = pl.program_id(0)
    groups = mixed_ref.shape[0]
    rows, feat = resid_ref.shape

    @pl.when(step == 0)
    def _():
        resid_ref[...] = x_ref[...].astype(F32)

    total = jnp.zeros((rows, feat), F32)
    for g in range(groups):
        weight = w_ref[:, g].reshape(-1, feat)
        total = total + dot(mixed_ref[g], weight, 1, 0).astype(BF16).astype(F32)
    resid_ref[...] += total

    @pl.when(step == pl.num_programs(0) - 1)
    def _():
        resid = resid_ref[...]
        both = gain_ref[...] * head_ref[...]
        squares = dot(jnp.ones((8, feat), F32), resid * resid, 1, 1, lax.Precision.HIGHEST)
        scores = dot(jnp.broadcast_to(both, (8, feat)), resid, 1, 1, lax.Precision.HIGHEST)
        pair = jnp.concatenate([squares[:1], scores[:1]], axis=0)
        stats_ref[...] = jnp.broadcast_to(pair[None], stats_ref.shape)


def project(place, mixed_all, w_parts, hidden_rows, gain_final, w_head):
    n_mp, rows, heads = mixed_all.shape
    feat = w_parts.shape[-1]
    step = 2
    share = pl.BlockSpec((1, feat), lambda i, s: (0, s[0]))
    return pl.pallas_call(
        project_kernel,
        out_shape=(
            jax.ShapeDtypeStruct((rows, feat), F32),
            jax.ShapeDtypeStruct((n_mp, 2, rows), F32),
        ),
        grid_spec=pltpu.PrefetchScalarGridSpec(
            num_scalar_prefetch=1,
            grid=(n_mp // step,),
            in_specs=[
                pl.BlockSpec((step, rows, heads), lambda i, s: (i, 0, 0)),
                pl.BlockSpec(
                    (w_parts.shape[0], step, w_parts.shape[2], feat), lambda i, s: (0, i, 0, 0)
                ),
                pl.BlockSpec((rows, feat), lambda i, s: (0, s[0])),
                share,
                share,
            ],
            out_specs=(
                pl.BlockSpec((rows, feat), lambda i, s: (0, 0)),
                pl.BlockSpec((n_mp, 2, rows), lambda i, s: (0, 0, 0)),
            ),
        ),
        compiler_params=pltpu.CompilerParams(vmem_limit_bytes=48 * 2**20),
        cost_estimate=pl.CostEstimate(flops=550000000, bytes_accessed=4000000, transcendentals=0),
        name="project",
    )(place, mixed_all, w_parts, hidden_rows, gain_final[None], w_head[None])


def row_terms(stats, used, width):
    sums = stats[0]
    for part in range(1, stats.shape[0]):
        sums = sums + stats[part]
    scale = lax.rsqrt(sums[:1] / width + EPS)
    score = sums[1:2] * scale
    row = lax.broadcasted_iota(jnp.int32, scale.shape, 1)
    inside = row < used
    return scale, score, inside


def reward_kernel(width, lens, stats_ref, out_ref):
    _, score, inside = row_terms(stats_ref, lens[0], width)
    total = jnp.sum(jnp.where(inside, score, 0.0), axis=1, keepdims=True)
    reward = total / lens[0].astype(F32)
    out_ref[...] = jnp.broadcast_to(reward[None], out_ref.shape)


def reward_of(lengths, stats, width, n_dp):
    return pl.pallas_call(
        functools.partial(reward_kernel, width),
        out_shape=jax.ShapeDtypeStruct((n_dp, 1, LANES), F32),
        grid_spec=pltpu.PrefetchScalarGridSpec(
            num_scalar_prefetch=1,
            grid=(1,),
            in_specs=[pl.BlockSpec(stats.shape, lambda i, s: (0, 0, 0))],
            out_specs=pl.BlockSpec((n_dp, 1, LANES), lambda i, s: (0, 0, 0)),
        ),
        cost_estimate=pl.CostEstimate(flops=10000, bytes_accessed=90000, transcendentals=512),
        name="reward",
    )(lengths, stats)


def gradient_kernel(width, place, stats_ref, resid_ref, gain_ref, head_ref, mixed_ref, send_ref, keep_ref, d_ref, p_ref):
    step = pl.program_id(0)
    groups, rows, heads = mixed_ref.shape
    feat = resid_ref.shape[1]
    half = groups * heads

    @pl.when(step == 0)
    def _():
        used = place[2]
        scale, score, inside = row_terms(stats_ref, used, width)
        weight = jnp.where(inside, scale, 0.0) / used.astype(F32)
        minus = weight * scale * score * (1.0 / width)
        plus = jnp.broadcast_to(weight, (LANES, rows)).T
        minus = jnp.broadcast_to(minus, (LANES, rows)).T
        both = gain_ref[...] * head_ref[...]
        for part in range(feat // LANES):
            at = slice(part * LANES, (part + 1) * LANES)
            resid = resid_ref[:, at]
            d_ref[:, at] = (plus * both[:, at] - minus * resid).astype(BF16)
            pooled = jnp.sum(plus * resid, axis=0, keepdims=True)
            p_ref[:, at] = jnp.broadcast_to(pooled, (8, LANES))

    def fill(out_ref):
        for g in range(groups):
            out_ref[g * heads : (g + 1) * heads, :] = dot(mixed_ref[g], d_ref[...], 0, 0).astype(BF16)
        extra = out_ref.shape[0] - half
        first = lax.broadcasted_iota(jnp.int32, (extra, feat), 0) == 0
        out_ref[half:, :] = jnp.where(first, p_ref[:1, :], 0.0).astype(BF16)

    @pl.when(step == 0)
    def _():
        fill(send_ref)

    @pl.when(step == 1)
    def _():
        fill(keep_ref)


def gradient_halves(place, stats, resid, gain_final, w_head, mixed_all, half_ext):
    n_mp, rows, heads = mixed_all.shape
    feat = resid.shape[1]
    width = gain_final.shape[0]
    share = pl.BlockSpec((1, feat), lambda i, s: (0, s[0]))
    half = jax.ShapeDtypeStruct((half_ext, feat), BF16)
    half_spec = pl.BlockSpec((half_ext, feat), lambda i, s: (0, 0))
    return pl.pallas_call(
        functools.partial(gradient_kernel, width),
        out_shape=(half, half),
        grid_spec=pltpu.PrefetchScalarGridSpec(
            num_scalar_prefetch=1,
            grid=(NCORE,),
            in_specs=[
                pl.BlockSpec(stats.shape, lambda i, s: (0, 0, 0)),
                pl.BlockSpec(resid.shape, lambda i, s: (0, 0)),
                share,
                share,
                pl.BlockSpec((n_mp // NCORE, rows, heads), lambda i, s: (i * s[1] + (1 - i) * (1 - s[1]), 0, 0)),
            ],
            out_specs=(half_spec, half_spec),
            scratch_shapes=[pltpu.VMEM((rows, feat), BF16), pltpu.VMEM((8, feat), F32)],
        ),
        compiler_params=pltpu.CompilerParams(vmem_limit_bytes=48 * 2**20),
        cost_estimate=pl.CostEstimate(flops=550000000, bytes_accessed=4000000, transcendentals=0),
        name="gradient",
    )(place, stats, resid, gain_final[None], w_head[None], mixed_all)


def weigh_kernel(place, rewards_ref, order_ref, keep_ref, got_ref, out_ref, margin_ref):
    seqs = rewards_ref.shape[0]
    rewards = rewards_ref[...].reshape(seqs, LANES)
    order = order_ref[...]
    seq = lax.broadcasted_iota(jnp.int32, (seqs, LANES), 0)
    picked = jnp.sum(jnp.where(seq == order, rewards, 0.0), axis=0, keepdims=True)
    lane = lax.broadcasted_iota(jnp.int32, (1, LANES), 1)
    chosen = lane % 2 == 0
    partner = jnp.where(chosen, pltpu.roll(picked, LANES - 1, 1), pltpu.roll(picked, 1, 1))
    margin = jnp.where(chosen, picked - partner, partner - picked)
    sig = 1.0 / (1.0 + jnp.exp(margin))
    dreward = jnp.where(chosen, -sig, sig)
    me = place[3]
    own = jnp.sum(jnp.where(order == me, dreward, 0.0), axis=1, keepdims=True)
    sib = jnp.sum(jnp.where(order == (me ^ 1), dreward, 0.0), axis=1, keepdims=True)
    out_ref[...] = (keep_ref[...].astype(F32) * own + got_ref[...].astype(F32) * sib).astype(BF16)
    margin_ref[...] = margin


def weigh(place, rewards, order, keep, got):
    flat = lambda a: pl.BlockSpec(a.shape, lambda i, s: (0,) * len(a.shape))
    return pl.pallas_call(
        weigh_kernel,
        out_shape=(
            jax.ShapeDtypeStruct(keep.shape, BF16),
            jax.ShapeDtypeStruct((1, LANES), F32),
        ),
        grid_spec=pltpu.PrefetchScalarGridSpec(
            num_scalar_prefetch=1,
            grid=(1,),
            in_specs=[flat(rewards), flat(order), flat(keep), flat(got)],
            out_specs=(flat(keep), pl.BlockSpec((1, LANES), lambda i, s: (0, 0))),
        ),
        cost_estimate=pl.CostEstimate(flops=1000000, bytes_accessed=2000000, transcendentals=128),
        name="weigh",
    )(place, rewards, order, keep, got)


def finish_kernel(half, place, mine_ref, other_ref, gain_ref, head_ref, grad_ref, ghead_ref, ggain_ref):
    step = pl.program_id(0)

    @pl.when(step == place[1])
    def _():
        grad_ref[...] = mine_ref[:half, :].astype(F32)

    @pl.when(step != place[1])
    def _():
        grad_ref[...] = other_ref[:half, :].astype(F32)

    pooled = mine_ref[half : half + 16, :].astype(F32)[:1]
    ghead_ref[...] = gain_ref[...] * pooled
    ggain_ref[...] = head_ref[...] * pooled


def finish(place, mine, other, gain_final, w_head, half):
    feat = mine.shape[1]
    flat = pl.BlockSpec(mine.shape, lambda i, s: (0, 0))
    share = pl.BlockSpec((1, feat), lambda i, s: (0, s[0]))
    line = pl.BlockSpec((1, feat), lambda i, s: (0, 0))
    return pl.pallas_call(
        functools.partial(finish_kernel, half),
        out_shape=(
            jax.ShapeDtypeStruct((NCORE * half, feat), F32),
            jax.ShapeDtypeStruct((1, feat), F32),
            jax.ShapeDtypeStruct((1, feat), F32),
        ),
        grid_spec=pltpu.PrefetchScalarGridSpec(
            num_scalar_prefetch=1,
            grid=(NCORE,),
            in_specs=[flat, flat, share, share],
            out_specs=(pl.BlockSpec((half, feat), lambda i, s: (i, 0)), line, line),
        ),
        cost_estimate=pl.CostEstimate(flops=1000000, bytes_accessed=4000000, transcendentals=0),
        name="finish",
    )(place, mine, other, gain_final[None], w_head[None])


def body(
    hidden_rows,
    lengths,
    pair_order,
    gain_attn,
    w_query,
    key_weight,
    value_weight,
    w_out,
    gain_final,
    w_head,
):
    rows, width = hidden_rows.shape
    n_mp = lax.axis_size("mp")
    n_dp = lax.axis_size("dp")
    feat = width // n_mp
    me = lax.axis_index("dp").astype(jnp.int32)
    core = me % NCORE
    along_x, along_z, near = dp_groups()
    place = jnp.stack([lax.axis_index("mp").astype(jnp.int32), core, lengths[0], me])

    mixed = front(hidden_rows, lengths, gain_attn, w_query, key_weight, value_weight)

    mixed, w_out = lax.optimization_barrier((mixed, w_out))
    mixed_all = lax.all_gather(mixed, "mp", axis=0, tiled=False)
    piece_rows = w_out.shape[0] // NEAR
    my_near = (me // (NZ * NCORE)) * NCORE + core
    w_piece = lax.dynamic_slice_in_dim(w_out, my_near * piece_rows, piece_rows, 0)
    w_piece = w_piece.reshape(piece_rows, n_mp, feat).swapaxes(0, 1)
    w_piece = lax.all_to_all(w_piece, "mp", 0, 0, tiled=True)
    w_parts = swap(jnp.broadcast_to(w_piece[None], (NEAR,) + w_piece.shape), near)

    resid, stats = project(place, mixed_all, w_parts, hidden_rows, gain_final, w_head)
    stats = lax.all_to_all(stats, "mp", 0, 0, tiled=True)
    rewards = lax.all_to_all(reward_of(lengths, stats, width, n_dp), "dp", 0, 0, tiled=True)

    half = width // NCORE
    piece = -(-(half + 1) // (NX * NZ * 8)) * 8
    half_ext = piece * NX * NZ
    send, keep = gradient_halves(place, stats, resid, gain_final, w_head, mixed_all, half_ext)
    got = to_sibling(send)
    seqs = pair_order.shape[0]
    order = jnp.pad(pair_order, (0, LANES - seqs), constant_values=-1)[None]
    summed, margin = weigh(place, rewards, order, keep, got)
    loss = jnp.sum(jax.nn.softplus(-margin[0, :seqs:2]))

    got = swap(summed.reshape(NX, NZ * piece, feat), along_x)
    summed = jnp.sum(got.astype(F32), axis=0).astype(BF16)
    got = swap(summed.reshape(NZ, piece, feat), along_z)
    mine = jnp.sum(got.astype(F32), axis=0).astype(BF16)
    got = swap(jnp.broadcast_to(mine[None], (NZ, piece, feat)), along_z)
    got = swap(jnp.broadcast_to(got.reshape(1, NZ * piece, feat), (NX, NZ * piece, feat)), along_x)
    got = got.reshape(half_ext, feat)
    other = to_sibling(got)
    grad_out_proj, grad_head, grad_gain = finish(place, got, other, gain_final, w_head, half)
    return (loss, rewards[:, 0, 0], grad_out_proj, grad_head[0], grad_gain[0])


def solution(mesh):
    placed = (
        P("dp", None),
        P("dp"),
        P(),
        P(),
        P(None, "mp"),
        P(None, "mp"),
        P(None, "mp"),
        P("mp", None),
        P(),
        P(),
    )
    return jax.shard_map(
        body,
        mesh=mesh,
        in_specs=placed,
        out_specs=(P(), P(), P(None, "mp"), P("mp"), P("mp")),
        check_vma=False,
    )
```

```python
import functools

import jax
import jax.numpy as jnp
import numpy as np
from jax import lax
from jax.experimental import pallas as pl
from jax.experimental.pallas import tpu as pltpu
from jax.sharding import PartitionSpec as P

QUERY_HEADS = 32
KEY_VALUE_HEADS = 8
HEAD_SIZE = 64
NX, NZ, NCORE = 4, 12, 2
NEAR = NX * NCORE

EPS = 1e-05
THETA = 500000.0
LANES = 128
F32 = jnp.float32
BF16 = jnp.bfloat16


def device_of(x, z, core):
    return (x * NZ + z) * NCORE + core


def dp_groups():
    along_x = [[device_of(x, z, c) for x in range(NX)] for z in range(NZ) for c in range(NCORE)]
    along_z = [[device_of(x, z, c) for z in range(NZ)] for x in range(NX) for c in range(NCORE)]
    near = [[device_of(x, z, c) for x in range(NX) for c in range(NCORE)] for z in range(NZ)]
    return along_x, along_z, near


def swap(parts, groups):
    return lax.all_to_all(parts, "dp", 0, 0, tiled=True, axis_index_groups=groups)


def to_sibling(x):
    pairs = [(i, i ^ 1) for i in range(NX * NZ * NCORE)]
    return lax.ppermute(x, "dp", pairs)


def dot(a, b, a_dim, b_dim, precision=None):
    return lax.dot_general(
        a, b, (((a_dim,), (b_dim,)), ((), ())), preferred_element_type=F32, precision=precision
    )


def rope_tables(positions):
    half = HEAD_SIZE // 2
    freq = np.tile(THETA ** (-np.arange(half) * 2.0 / HEAD_SIZE), LANES // half).astype(np.float32)
    sign = np.tile(np.repeat([-1.0, 1.0], half), LANES // HEAD_SIZE).astype(np.float32)
    angle = positions.astype(F32)[:, None] * freq[None, :]
    return jnp.cos(angle), jnp.sin(angle) * sign[None, :]


def front_kernel(lens, x_ref, gain_ref, wq_ref, wk_ref, wv_ref, cos_ref, sin_ref, out_ref, k_ref, v_ref):
    step = pl.program_id(0)
    rows = x_ref.shape[0]
    x = x_ref[...].astype(F32)
    inv = lax.rsqrt(jnp.mean(x * x, axis=1, keepdims=True) + EPS)
    normed = (x * inv * gain_ref[...]).astype(BF16)
    cosine, sine = cos_ref[...], sin_ref[...]
    lane = lax.broadcasted_iota(jnp.int32, (rows, LANES), 1)
    first_half = (lane % HEAD_SIZE) < HEAD_SIZE // 2
    low = lane < HEAD_SIZE

    def rotate(t):
        partner = jnp.where(
            first_half, pltpu.roll(t, LANES - HEAD_SIZE // 2, 1), pltpu.roll(t, HEAD_SIZE // 2, 1)
        )
        return t * cosine + partner * sine

    query = dot(normed, wq_ref[...], 1, 0)
    key = dot(normed, wk_ref[...], 1, 1)
    value = dot(normed, wv_ref[...], 1, 1)
    key = rotate(jnp.concatenate([key, key], axis=1))
    value = jnp.concatenate([value, value], axis=1)
    here = pl.ds(pl.multiple_of(step * rows, rows), rows)
    k_ref[0, here, :] = jnp.where(low, key, 0.0).astype(BF16)
    k_ref[1, here, :] = jnp.where(low, 0.0, key).astype(BF16)
    v_ref[0, here, :] = jnp.where(low, value, 0.0).astype(BF16)
    v_ref[1, here, :] = jnp.where(low, 0.0, value).astype(BF16)
    pairs = query.shape[1] // LANES
    turned = [rotate(query[:, p * LANES : (p + 1) * LANES]).astype(BF16) for p in range(pairs)]
    used = lens[0]

    def attend(first, cols):
        row = first + lax.broadcasted_iota(jnp.int32, (rows, cols), 0)
        col = lax.broadcasted_iota(jnp.int32, (rows, cols), 1)
        allowed = (col <= row) & ((row >= used) == (col >= used))
        for p in range(pairs):
            total = jnp.zeros((rows, LANES), F32)
            for e in range(LANES // HEAD_SIZE):
                scores = dot(turned[p], k_ref[e, :cols, :], 1, 1) * HEAD_SIZE ** (-0.5)
                scores = jnp.where(allowed, scores, -1e30)
                top = jnp.max(scores, axis=1, keepdims=True)
                weights = jnp.exp(scores - top)
                probs = weights * (1.0 / jnp.sum(weights, axis=1, keepdims=True))
                total = total + dot(probs.astype(BF16), v_ref[e, :cols, :], 1, 0)
            out_ref[:, p * LANES : (p + 1) * LANES] = total.astype(BF16)

    for s in range(k_ref.shape[1] // rows):
        @pl.when(step == s)
        def _(s=s):
            attend(s * rows, (s + 1) * rows)


def front(hidden_rows, lengths, gain_attn, w_query, key_weight, value_weight):
    rows, width = hidden_rows.shape
    row = jnp.arange(rows, dtype=jnp.int32)
    cosine, sine = rope_tables(row - jnp.where(row >= lengths[0], lengths[0], 0))
    block = rows // 2
    whole = lambda a: pl.BlockSpec(a.shape, lambda i, s: (0, 0))
    by_rows = lambda cols: pl.BlockSpec((block, cols), lambda i, s: (i, 0))
    gain = gain_attn[None]
    key_weight, value_weight = key_weight.T, value_weight.T
    return pl.pallas_call(
        front_kernel,
        out_shape=jax.ShapeDtypeStruct((rows, w_query.shape[1]), BF16),
        grid_spec=pltpu.PrefetchScalarGridSpec(
            num_scalar_prefetch=1,
            grid=(rows // block,),
            in_specs=[
                by_rows(width),
                whole(gain),
                whole(w_query),
                whole(key_weight),
                whole(value_weight),
                by_rows(LANES),
                by_rows(LANES),
            ],
            out_specs=by_rows(w_query.shape[1]),
            scratch_shapes=[pltpu.VMEM((2, rows, LANES), BF16), pltpu.VMEM((2, rows, LANES), BF16)],
        ),
        compiler_params=pltpu.CompilerParams(vmem_limit_bytes=58 * 2**20),
        cost_estimate=pl.CostEstimate(flops=1500000000, bytes_accessed=4000000, transcendentals=800000),
        name="front",
    )(lengths, hidden_rows, gain, w_query, key_weight, value_weight, cosine, sine)


def project_kernel(place, mixed_ref, w_ref, x_ref, gain_ref, head_ref, resid_ref, stats_ref):
    step = pl.program_id(0)
    groups = mixed_ref.shape[0]
    rows, feat = resid_ref.shape

    @pl.when(step == 0)
    def _():
        resid_ref[...] = x_ref[...].astype(F32)

    total = jnp.zeros((rows, feat), F32)
    for g in range(groups):
        weight = w_ref[:, g].reshape(-1, feat)
        total = total + dot(mixed_ref[g], weight, 1, 0).astype(BF16).astype(F32)
    resid_ref[...] += total

    @pl.when(step == pl.num_programs(0) - 1)
    def _():
        resid = resid_ref[...]
        both = gain_ref[...] * head_ref[...]
        squares = dot(jnp.ones((8, feat), F32), resid * resid, 1, 1, lax.Precision.HIGHEST)
        scores = dot(jnp.broadcast_to(both, (8, feat)), resid, 1, 1, lax.Precision.HIGHEST)
        pair = jnp.concatenate([squares[:1], scores[:1]], axis=0)
        stats_ref[...] = jnp.broadcast_to(pair[None], stats_ref.shape)


def project(place, mixed_all, w_parts, hidden_rows, gain_final, w_head):
    n_mp, rows, heads = mixed_all.shape
    feat = w_parts.shape[-1]
    step = 2
    share = pl.BlockSpec((1, feat), lambda i, s: (0, s[0]))
    return pl.pallas_call(
        project_kernel,
        out_shape=(
            jax.ShapeDtypeStruct((rows, feat), F32),
            jax.ShapeDtypeStruct((n_mp, 2, rows), F32),
        ),
        grid_spec=pltpu.PrefetchScalarGridSpec(
            num_scalar_prefetch=1,
            grid=(n_mp // step,),
            in_specs=[
                pl.BlockSpec((step, rows, heads), lambda i, s: (i, 0, 0)),
                pl.BlockSpec(
                    (w_parts.shape[0], step, w_parts.shape[2], feat), lambda i, s: (0, i, 0, 0)
                ),
                pl.BlockSpec((rows, feat), lambda i, s: (0, s[0])),
                share,
                share,
            ],
            out_specs=(
                pl.BlockSpec((rows, feat), lambda i, s: (0, 0)),
                pl.BlockSpec((n_mp, 2, rows), lambda i, s: (0, 0, 0)),
            ),
        ),
        compiler_params=pltpu.CompilerParams(vmem_limit_bytes=58 * 2**20),
        cost_estimate=pl.CostEstimate(flops=550000000, bytes_accessed=4000000, transcendentals=0),
        name="project",
    )(place, mixed_all, w_parts, hidden_rows, gain_final[None], w_head[None])


def row_terms(stats, used, width):
    sums = stats[0]
    for part in range(1, stats.shape[0]):
        sums = sums + stats[part]
    scale = lax.rsqrt(sums[:1] / width + EPS)
    score = sums[1:2] * scale
    row = lax.broadcasted_iota(jnp.int32, scale.shape, 1)
    inside = row < used
    return scale, score, inside


def reward_kernel(width, lens, stats_ref, out_ref):
    _, score, inside = row_terms(stats_ref, lens[0], width)
    total = jnp.sum(jnp.where(inside, score, 0.0), axis=1, keepdims=True)
    reward = total / lens[0].astype(F32)
    out_ref[...] = jnp.broadcast_to(reward[None], out_ref.shape)


def reward_of(lengths, stats, width, n_dp):
    return pl.pallas_call(
        functools.partial(reward_kernel, width),
        out_shape=jax.ShapeDtypeStruct((n_dp, 1, LANES), F32),
        grid_spec=pltpu.PrefetchScalarGridSpec(
            num_scalar_prefetch=1,
            grid=(1,),
            in_specs=[pl.BlockSpec(stats.shape, lambda i, s: (0, 0, 0))],
            out_specs=pl.BlockSpec((n_dp, 1, LANES), lambda i, s: (0, 0, 0)),
        ),
        compiler_params=pltpu.CompilerParams(vmem_limit_bytes=16 * 2**20),
        cost_estimate=pl.CostEstimate(flops=10000, bytes_accessed=90000, transcendentals=512),
        name="reward",
    )(lengths, stats)


def gradient_kernel(width, place, stats_ref, resid_ref, gain_ref, head_ref, mixed_ref, send_ref, keep_ref, d_ref, p_ref):
    step = pl.program_id(0)
    groups, rows, heads = mixed_ref.shape
    feat = resid_ref.shape[1]
    half = groups * heads

    @pl.when(step == 0)
    def _():
        used = place[2]
        scale, score, inside = row_terms(stats_ref, used, width)
        weight = jnp.where(inside, scale, 0.0) / used.astype(F32)
        minus = weight * scale * score * (1.0 / width)
        plus = jnp.broadcast_to(weight, (LANES, rows)).T
        minus = jnp.broadcast_to(minus, (LANES, rows)).T
        both = gain_ref[...] * head_ref[...]
        for part in range(feat // LANES):
            at = slice(part * LANES, (part + 1) * LANES)
            resid = resid_ref[:, at]
            d_ref[:, at] = (plus * both[:, at] - minus * resid).astype(BF16)
            pooled = jnp.sum(plus * resid, axis=0, keepdims=True)
            p_ref[:, at] = jnp.broadcast_to(pooled, (8, LANES))

    def fill(out_ref):
        for g in range(groups):
            out_ref[g * heads : (g + 1) * heads, :] = dot(mixed_ref[g], d_ref[...], 0, 0).astype(BF16)
        extra = out_ref.shape[0] - half
        first = lax.broadcasted_iota(jnp.int32, (extra, feat), 0) == 0
        out_ref[half:, :] = jnp.where(first, p_ref[:1, :], 0.0).astype(BF16)

    @pl.when(step == 0)
    def _():
        fill(send_ref)

    @pl.when(step == 1)
    def _():
        fill(keep_ref)


def gradient_halves(place, stats, resid, gain_final, w_head, mixed_all, half_ext):
    n_mp, rows, heads = mixed_all.shape
    feat = resid.shape[1]
    width = gain_final.shape[0]
    share = pl.BlockSpec((1, feat), lambda i, s: (0, s[0]))
    half = jax.ShapeDtypeStruct((half_ext, feat), BF16)
    half_spec = pl.BlockSpec((half_ext, feat), lambda i, s: (0, 0))
    return pl.pallas_call(
        functools.partial(gradient_kernel, width),
        out_shape=(half, half),
        grid_spec=pltpu.PrefetchScalarGridSpec(
            num_scalar_prefetch=1,
            grid=(NCORE,),
            in_specs=[
                pl.BlockSpec(stats.shape, lambda i, s: (0, 0, 0)),
                pl.BlockSpec(resid.shape, lambda i, s: (0, 0)),
                share,
                share,
                pl.BlockSpec((n_mp // NCORE, rows, heads), lambda i, s: (i * s[1] + (1 - i) * (1 - s[1]), 0, 0)),
            ],
            out_specs=(half_spec, half_spec),
            scratch_shapes=[pltpu.VMEM((rows, feat), BF16), pltpu.VMEM((8, feat), F32)],
        ),
        compiler_params=pltpu.CompilerParams(vmem_limit_bytes=48 * 2**20),
        cost_estimate=pl.CostEstimate(flops=550000000, bytes_accessed=4000000, transcendentals=0),
        name="gradient",
    )(place, stats, resid, gain_final[None], w_head[None], mixed_all)


def weigh_kernel(place, rewards_ref, order_ref, keep_ref, got_ref, out_ref, margin_ref, row_ref):
    seqs = rewards_ref.shape[0]
    rewards = rewards_ref[...].reshape(seqs, LANES)
    order = order_ref[...]
    seq = lax.broadcasted_iota(jnp.int32, (seqs, LANES), 0)
    picked = jnp.sum(jnp.where(seq == order, rewards, 0.0), axis=0, keepdims=True)
    lane = lax.broadcasted_iota(jnp.int32, (1, LANES), 1)
    chosen = lane % 2 == 0
    partner = jnp.where(chosen, pltpu.roll(picked, LANES - 1, 1), pltpu.roll(picked, 1, 1))
    margin = jnp.where(chosen, picked - partner, partner - picked)
    sig = 1.0 / (1.0 + jnp.exp(margin))
    dreward = jnp.where(chosen, -sig, sig)
    me = place[3]
    own = jnp.sum(jnp.where(order == me, dreward, 0.0), axis=1, keepdims=True)
    sib = jnp.sum(jnp.where(order == (me ^ 1), dreward, 0.0), axis=1, keepdims=True)
    out_ref[...] = (keep_ref[...].astype(F32) * own + got_ref[...].astype(F32) * sib).astype(BF16)
    margin_ref[...] = margin
    at = lax.broadcasted_iota(jnp.int32, (seqs, LANES), 1)
    row_ref[...] = jnp.sum(jnp.where(seq == at, rewards, 0.0), axis=0, keepdims=True)


def weigh(place, rewards, order, keep, got):
    flat = lambda a: pl.BlockSpec(a.shape, lambda i, s: (0,) * len(a.shape))
    return pl.pallas_call(
        weigh_kernel,
        out_shape=(
            jax.ShapeDtypeStruct(keep.shape, BF16),
            jax.ShapeDtypeStruct((1, LANES), F32),
            jax.ShapeDtypeStruct((1, LANES), F32),
        ),
        grid_spec=pltpu.PrefetchScalarGridSpec(
            num_scalar_prefetch=1,
            grid=(1,),
            in_specs=[flat(rewards), flat(order), flat(keep), flat(got)],
            out_specs=(flat(keep),) + (pl.BlockSpec((1, LANES), lambda i, s: (0, 0)),) * 2,
        ),
        compiler_params=pltpu.CompilerParams(vmem_limit_bytes=16 * 2**20),
        cost_estimate=pl.CostEstimate(flops=1000000, bytes_accessed=2000000, transcendentals=128),
        name="weigh",
    )(place, rewards, order, keep, got)


def finish_kernel(half, place, mine_ref, other_ref, gain_ref, head_ref, grad_ref, ghead_ref, ggain_ref):
    step = pl.program_id(0)

    @pl.when(step == place[1])
    def _():
        grad_ref[...] = mine_ref[:half, :].astype(F32)

    @pl.when(step != place[1])
    def _():
        grad_ref[...] = other_ref[:half, :].astype(F32)

    pooled = mine_ref[half : half + 16, :].astype(F32)[:1]
    ghead_ref[...] = gain_ref[...] * pooled
    ggain_ref[...] = head_ref[...] * pooled


def finish(place, mine, other, gain_final, w_head, half):
    feat = mine.shape[1]
    flat = pl.BlockSpec(mine.shape, lambda i, s: (0, 0))
    share = pl.BlockSpec((1, feat), lambda i, s: (0, s[0]))
    line = pl.BlockSpec((1, feat), lambda i, s: (0, 0))
    return pl.pallas_call(
        functools.partial(finish_kernel, half),
        out_shape=(
            jax.ShapeDtypeStruct((NCORE * half, feat), F32),
            jax.ShapeDtypeStruct((1, feat), F32),
            jax.ShapeDtypeStruct((1, feat), F32),
        ),
        grid_spec=pltpu.PrefetchScalarGridSpec(
            num_scalar_prefetch=1,
            grid=(NCORE,),
            in_specs=[flat, flat, share, share],
            out_specs=(pl.BlockSpec((half, feat), lambda i, s: (i, 0)), line, line),
        ),
        compiler_params=pltpu.CompilerParams(vmem_limit_bytes=16 * 2**20),
        cost_estimate=pl.CostEstimate(flops=1000000, bytes_accessed=4000000, transcendentals=0),
        name="finish",
    )(place, mine, other, gain_final[None], w_head[None])


def body(
    hidden_rows,
    lengths,
    pair_order,
    gain_attn,
    w_query,
    key_weight,
    value_weight,
    w_out,
    gain_final,
    w_head,
):
    rows, width = hidden_rows.shape
    n_mp = lax.axis_size("mp")
    n_dp = lax.axis_size("dp")
    feat = width // n_mp
    me = lax.axis_index("dp").astype(jnp.int32)
    core = me % NCORE
    along_x, along_z, near = dp_groups()
    place = jnp.stack([lax.axis_index("mp").astype(jnp.int32), core, lengths[0], me])

    mixed = front(hidden_rows, lengths, gain_attn, w_query, key_weight, value_weight)

    mixed, w_out = lax.optimization_barrier((mixed, w_out))
    mixed_all = lax.all_gather(mixed, "mp", axis=0, tiled=False)
    piece_rows = w_out.shape[0] // NEAR
    my_near = (me // (NZ * NCORE)) * NCORE + core
    w_piece = lax.dynamic_slice_in_dim(w_out, my_near * piece_rows, piece_rows, 0)
    w_piece = w_piece.reshape(piece_rows, n_mp, feat).swapaxes(0, 1)
    w_piece = lax.all_to_all(w_piece, "mp", 0, 0, tiled=True)
    w_parts = swap(jnp.broadcast_to(w_piece[None], (NEAR,) + w_piece.shape), near)

    resid, stats = project(place, mixed_all, w_parts, hidden_rows, gain_final, w_head)
    stats = lax.all_to_all(stats, "mp", 0, 0, tiled=True)
    reward, stats = lax.optimization_barrier((reward_of(lengths, stats, width, n_dp), stats))
    rewards = lax.all_to_all(reward, "dp", 0, 0, tiled=True)

    half = width // NCORE
    piece = -(-(half + 1) // (NX * NZ * 8)) * 8
    half_ext = piece * NX * NZ
    send, keep = gradient_halves(place, stats, resid, gain_final, w_head, mixed_all, half_ext)
    got = to_sibling(send)
    seqs = pair_order.shape[0]
    order = jnp.pad(pair_order, (0, LANES - seqs), constant_values=-1)[None]
    summed, margin, reward_row = weigh(place, rewards, order, keep, got)
    loss = jnp.sum(jax.nn.softplus(-margin[0, :seqs:2]))

    got = swap(summed.reshape(NX, NZ * piece, feat), along_x)
    summed = jnp.sum(got.astype(F32), axis=0).astype(BF16)
    got = swap(summed.reshape(NZ, piece, feat), along_z)
    mine = jnp.sum(got.astype(F32), axis=0).astype(BF16)
    got = swap(jnp.broadcast_to(mine[None], (NZ, piece, feat)), along_z)
    got = swap(jnp.broadcast_to(got.reshape(1, NZ * piece, feat), (NX, NZ * piece, feat)), along_x)
    got = got.reshape(half_ext, feat)
    other = to_sibling(got)
    grad_out_proj, grad_head, grad_gain = finish(place, got, other, gain_final, w_head, half)
    return (loss, reward_row[0, :seqs], grad_out_proj, grad_head[0], grad_gain[0])


def solution(mesh):
    placed = (
        P("dp", None),
        P("dp"),
        P(),
        P(),
        P(None, "mp"),
        P(None, "mp"),
        P(None, "mp"),
        P("mp", None),
        P(),
        P(),
    )
    return jax.shard_map(
        body,
        mesh=mesh,
        in_specs=placed,
        out_specs=(P(), P(), P(None, "mp"), P("mp"), P("mp")),
        check_vma=False,
    )
```

```python
import functools

import jax
import jax.numpy as jnp
import numpy as np
from jax import lax
from jax.experimental import pallas as pl
from jax.experimental.pallas import tpu as pltpu
from jax.sharding import PartitionSpec as P

QUERY_HEADS = 32
KEY_VALUE_HEADS = 8
HEAD_SIZE = 64
NX, NZ, NCORE = 4, 12, 2
NEAR = NX * NCORE

EPS = 1e-05
THETA = 500000.0
LANES = 128
F32 = jnp.float32
BF16 = jnp.bfloat16


def device_of(x, z, core):
    return (x * NZ + z) * NCORE + core


def dp_groups():
    along_x = [[device_of(x, z, c) for x in range(NX)] for z in range(NZ) for c in range(NCORE)]
    along_z = [[device_of(x, z, c) for z in range(NZ)] for x in range(NX) for c in range(NCORE)]
    near = [[device_of(x, z, c) for x in range(NX) for c in range(NCORE)] for z in range(NZ)]
    return along_x, along_z, near


def swap(parts, groups):
    return lax.all_to_all(parts, "dp", 0, 0, tiled=True, axis_index_groups=groups)


def to_sibling(x):
    pairs = [(i, i ^ 1) for i in range(NX * NZ * NCORE)]
    return lax.ppermute(x, "dp", pairs)


def dot(a, b, a_dim, b_dim, precision=None):
    return lax.dot_general(
        a, b, (((a_dim,), (b_dim,)), ((), ())), preferred_element_type=F32, precision=precision
    )


def rope_tables(positions):
    half = HEAD_SIZE // 2
    freq = np.tile(THETA ** (-np.arange(half) * 2.0 / HEAD_SIZE), LANES // half).astype(np.float32)
    sign = np.tile(np.repeat([-1.0, 1.0], half), LANES // HEAD_SIZE).astype(np.float32)
    angle = positions.astype(F32)[:, None] * freq[None, :]
    return jnp.cos(angle), jnp.sin(angle) * sign[None, :]


def front_kernel(lens, x_ref, gain_ref, wq_ref, wk_ref, wv_ref, cos_ref, sin_ref, out_ref, k_ref, v_ref):
    step = pl.program_id(0)
    rows = x_ref.shape[0]
    x = x_ref[...].astype(F32)
    inv = lax.rsqrt(jnp.mean(x * x, axis=1, keepdims=True) + EPS)
    normed = (x * inv * gain_ref[...]).astype(BF16)
    cosine, sine = cos_ref[...], sin_ref[...]
    lane = lax.broadcasted_iota(jnp.int32, (rows, LANES), 1)
    first_half = (lane % HEAD_SIZE) < HEAD_SIZE // 2
    low = lane < HEAD_SIZE

    def rotate(t):
        partner = jnp.where(
            first_half, pltpu.roll(t, LANES - HEAD_SIZE // 2, 1), pltpu.roll(t, HEAD_SIZE // 2, 1)
        )
        return t * cosine + partner * sine

    query = dot(normed, wq_ref[...], 1, 0)
    key = dot(normed, wk_ref[...], 1, 1)
    value = dot(normed, wv_ref[...], 1, 1)
    key = rotate(jnp.concatenate([key, key], axis=1))
    value = jnp.concatenate([value, value], axis=1)
    here = pl.ds(pl.multiple_of(step * rows, rows), rows)
    k_ref[0, here, :] = jnp.where(low, key, 0.0).astype(BF16)
    k_ref[1, here, :] = jnp.where(low, 0.0, key).astype(BF16)
    v_ref[0, here, :] = jnp.where(low, value, 0.0).astype(BF16)
    v_ref[1, here, :] = jnp.where(low, 0.0, value).astype(BF16)
    pairs = query.shape[1] // LANES
    turned = [rotate(query[:, p * LANES : (p + 1) * LANES]).astype(BF16) for p in range(pairs)]
    used = lens[0]

    def attend(first, cols):
        row = first + lax.broadcasted_iota(jnp.int32, (rows, cols), 0)
        col = lax.broadcasted_iota(jnp.int32, (rows, cols), 1)
        allowed = (col <= row) & ((row >= used) == (col >= used))
        for p in range(pairs):
            total = jnp.zeros((rows, LANES), F32)
            for e in range(LANES // HEAD_SIZE):
                scores = dot(turned[p], k_ref[e, :cols, :], 1, 1) * HEAD_SIZE ** (-0.5)
                scores = jnp.where(allowed, scores, -1e30)
                top = jnp.max(scores, axis=1, keepdims=True)
                weights = jnp.exp(scores - top)
                probs = weights * (1.0 / jnp.sum(weights, axis=1, keepdims=True))
                total = total + dot(probs.astype(BF16), v_ref[e, :cols, :], 1, 0)
            out_ref[:, p * LANES : (p + 1) * LANES] = total.astype(BF16)

    for s in range(k_ref.shape[1] // rows):
        @pl.when(step == s)
        def _(s=s):
            attend(s * rows, (s + 1) * rows)


def front(hidden_rows, lengths, gain_attn, w_query, key_weight, value_weight):
    rows, width = hidden_rows.shape
    row = jnp.arange(rows, dtype=jnp.int32)
    cosine, sine = rope_tables(row - jnp.where(row >= lengths[0], lengths[0], 0))
    block = rows // 2
    whole = lambda a: pl.BlockSpec(a.shape, lambda i, s: (0, 0))
    by_rows = lambda cols: pl.BlockSpec((block, cols), lambda i, s: (i, 0))
    gain = gain_attn[None]
    key_weight, value_weight = key_weight.T, value_weight.T
    return pl.pallas_call(
        front_kernel,
        out_shape=jax.ShapeDtypeStruct((rows, w_query.shape[1]), BF16),
        grid_spec=pltpu.PrefetchScalarGridSpec(
            num_scalar_prefetch=1,
            grid=(rows // block,),
            in_specs=[
                by_rows(width),
                whole(gain),
                whole(w_query),
                whole(key_weight),
                whole(value_weight),
                by_rows(LANES),
                by_rows(LANES),
            ],
            out_specs=by_rows(w_query.shape[1]),
            scratch_shapes=[pltpu.VMEM((2, rows, LANES), BF16), pltpu.VMEM((2, rows, LANES), BF16)],
        ),
        compiler_params=pltpu.CompilerParams(vmem_limit_bytes=48 * 2**20),
        cost_estimate=pl.CostEstimate(flops=1500000000, bytes_accessed=4000000, transcendentals=800000),
        name="front",
    )(lengths, hidden_rows, gain, w_query, key_weight, value_weight, cosine, sine)


def project_kernel(place, mixed_hbm, w_ref, x_ref, gain_ref, head_ref, resid_ref, stats_ref, mixed_ref, sems):
    groups = mixed_ref.shape[0]
    rows, feat = resid_ref.shape
    copies = [pltpu.make_async_copy(mixed_hbm.at[g], mixed_ref.at[g], sems.at[g]) for g in range(groups)]
    for copy in copies:
        copy.start()
    resid_ref[...] = x_ref[...].astype(F32)
    for g in range(groups):
        copies[g].wait()
        weight = w_ref[:, g].reshape(-1, feat)
        resid_ref[...] += dot(mixed_ref[g], weight, 1, 0).astype(BF16).astype(F32)
    resid = resid_ref[...]
    both = gain_ref[...] * head_ref[...]
    squares = dot(jnp.ones((8, feat), F32), resid * resid, 1, 1, lax.Precision.HIGHEST)
    scores = dot(jnp.broadcast_to(both, (8, feat)), resid, 1, 1, lax.Precision.HIGHEST)
    pair = jnp.concatenate([squares[:1], scores[:1]], axis=0)
    stats_ref[...] = jnp.broadcast_to(pair[None], stats_ref.shape)


def project(place, mixed_all, w_parts, x_cols, gain_final, w_head):
    n_mp, rows, heads = mixed_all.shape
    feat = w_parts.shape[-1]
    share = pl.BlockSpec((1, feat), lambda i, s: (0, s[0]))
    flat = lambda a: pl.BlockSpec(a.shape, lambda i, s: (0,) * len(a.shape))
    return pl.pallas_call(
        project_kernel,
        out_shape=(
            jax.ShapeDtypeStruct((rows, feat), F32),
            jax.ShapeDtypeStruct((n_mp, 2, rows), F32),
        ),
        grid_spec=pltpu.PrefetchScalarGridSpec(
            num_scalar_prefetch=1,
            grid=(1,),
            in_specs=[
                pl.BlockSpec(memory_space=pltpu.HBM),
                flat(w_parts),
                flat(x_cols),
                share,
                share,
            ],
            out_specs=(
                pl.BlockSpec((rows, feat), lambda i, s: (0, 0)),
                pl.BlockSpec((n_mp, 2, rows), lambda i, s: (0, 0, 0)),
            ),
            scratch_shapes=[
                pltpu.VMEM(mixed_all.shape, BF16),
                pltpu.SemaphoreType.DMA((n_mp,)),
            ],
        ),
        compiler_params=pltpu.CompilerParams(vmem_limit_bytes=32 * 2**20),
        cost_estimate=pl.CostEstimate(flops=550000000, bytes_accessed=4000000, transcendentals=0),
        name="project",
    )(place, mixed_all, w_parts, x_cols, gain_final[None], w_head[None])


def row_terms(stats, used, width):
    sums = stats[0]
    for part in range(1, stats.shape[0]):
        sums = sums + stats[part]
    scale = lax.rsqrt(sums[:1] / width + EPS)
    score = sums[1:2] * scale
    row = lax.broadcasted_iota(jnp.int32, scale.shape, 1)
    inside = row < used
    return scale, score, inside


def reward_kernel(width, lens, stats_ref, out_ref):
    _, score, inside = row_terms(stats_ref, lens[0], width)
    total = jnp.sum(jnp.where(inside, score, 0.0), axis=1, keepdims=True)
    reward = total / lens[0].astype(F32)
    out_ref[...] = jnp.broadcast_to(reward[None], out_ref.shape)


def reward_of(lengths, stats, width, n_dp):
    return pl.pallas_call(
        functools.partial(reward_kernel, width),
        out_shape=jax.ShapeDtypeStruct((n_dp, 1, LANES), F32),
        grid_spec=pltpu.PrefetchScalarGridSpec(
            num_scalar_prefetch=1,
            grid=(1,),
            in_specs=[pl.BlockSpec(stats.shape, lambda i, s: (0, 0, 0))],
            out_specs=pl.BlockSpec((n_dp, 1, LANES), lambda i, s: (0, 0, 0)),
        ),
        compiler_params=pltpu.CompilerParams(vmem_limit_bytes=16 * 2**20),
        cost_estimate=pl.CostEstimate(flops=10000, bytes_accessed=90000, transcendentals=512),
        name="reward",
    )(lengths, stats)


def gradient_kernel(width, place, stats_ref, resid_ref, gain_ref, head_ref, mixed_ref, send_ref, keep_ref, d_ref, p_ref):
    step = pl.program_id(0)
    groups, rows, heads = mixed_ref.shape
    feat = resid_ref.shape[1]
    half = groups * heads

    @pl.when(step == 0)
    def _():
        used = place[2]
        scale, score, inside = row_terms(stats_ref, used, width)
        weight = jnp.where(inside, scale, 0.0) / used.astype(F32)
        minus = weight * scale * score * (1.0 / width)
        plus = jnp.broadcast_to(weight, (LANES, rows)).T
        minus = jnp.broadcast_to(minus, (LANES, rows)).T
        both = gain_ref[...] * head_ref[...]
        for part in range(feat // LANES):
            at = slice(part * LANES, (part + 1) * LANES)
            resid = resid_ref[:, at]
            d_ref[:, at] = (plus * both[:, at] - minus * resid).astype(BF16)
            pooled = jnp.sum(plus * resid, axis=0, keepdims=True)
            p_ref[:, at] = jnp.broadcast_to(pooled, (8, LANES))

    def fill(out_ref):
        for g in range(groups):
            out_ref[g * heads : (g + 1) * heads, :] = dot(mixed_ref[g], d_ref[...], 0, 0).astype(BF16)
        extra = out_ref.shape[0] - half
        first = lax.broadcasted_iota(jnp.int32, (extra, feat), 0) == 0
        out_ref[half:, :] = jnp.where(first, p_ref[:1, :], 0.0).astype(BF16)

    @pl.when(step == 0)
    def _():
        fill(send_ref)

    @pl.when(step == 1)
    def _():
        fill(keep_ref)


def gradient_halves(place, stats, resid, gain_final, w_head, mixed_all, half_ext):
    n_mp, rows, heads = mixed_all.shape
    feat = resid.shape[1]
    width = gain_final.shape[0]
    share = pl.BlockSpec((1, feat), lambda i, s: (0, s[0]))
    half = jax.ShapeDtypeStruct((half_ext, feat), BF16)
    half_spec = pl.BlockSpec((half_ext, feat), lambda i, s: (0, 0))
    return pl.pallas_call(
        functools.partial(gradient_kernel, width),
        out_shape=(half, half),
        grid_spec=pltpu.PrefetchScalarGridSpec(
            num_scalar_prefetch=1,
            grid=(NCORE,),
            in_specs=[
                pl.BlockSpec(stats.shape, lambda i, s: (0, 0, 0)),
                pl.BlockSpec(resid.shape, lambda i, s: (0, 0)),
                share,
                share,
                pl.BlockSpec((n_mp // NCORE, rows, heads), lambda i, s: (i * s[1] + (1 - i) * (1 - s[1]), 0, 0)),
            ],
            out_specs=(half_spec, half_spec),
            scratch_shapes=[pltpu.VMEM((rows, feat), BF16), pltpu.VMEM((8, feat), F32)],
        ),
        compiler_params=pltpu.CompilerParams(vmem_limit_bytes=58 * 2**20),
        cost_estimate=pl.CostEstimate(flops=550000000, bytes_accessed=4000000, transcendentals=0),
        name="gradient",
    )(place, stats, resid, gain_final[None], w_head[None], mixed_all)


def pairs_kernel(place, rewards_ref, order_ref, coef_ref, margin_ref, row_ref):
    seqs = rewards_ref.shape[0]
    rewards = rewards_ref[...].reshape(seqs, LANES)
    order = order_ref[...]
    seq = lax.broadcasted_iota(jnp.int32, (seqs, LANES), 0)
    picked = jnp.sum(jnp.where(seq == order, rewards, 0.0), axis=0, keepdims=True)
    lane = lax.broadcasted_iota(jnp.int32, (1, LANES), 1)
    chosen = lane % 2 == 0
    partner = jnp.where(chosen, pltpu.roll(picked, LANES - 1, 1), pltpu.roll(picked, 1, 1))
    margin = jnp.where(chosen, picked - partner, partner - picked)
    sig = 1.0 / (1.0 + jnp.exp(margin))
    dreward = jnp.where(chosen, -sig, sig)
    me = place[3]
    own = jnp.sum(jnp.where(order == me, dreward, 0.0), axis=1, keepdims=True)
    sib = jnp.sum(jnp.where(order == (me ^ 1), dreward, 0.0), axis=1, keepdims=True)
    row = lax.broadcasted_iota(jnp.int32, coef_ref.shape, 0)
    coef_ref[...] = jnp.where(row == 0, own, sib)
    margin_ref[...] = margin
    at = lax.broadcasted_iota(jnp.int32, (seqs, LANES), 1)
    row_ref[...] = jnp.sum(jnp.where(seq == at, rewards, 0.0), axis=0, keepdims=True)


def pair_weights(place, rewards, order):
    flat = lambda shape: pl.BlockSpec(shape, lambda i, s: (0,) * len(shape))
    line = jax.ShapeDtypeStruct((1, LANES), F32)
    return pl.pallas_call(
        pairs_kernel,
        out_shape=(jax.ShapeDtypeStruct((8, LANES), F32), line, line),
        grid_spec=pltpu.PrefetchScalarGridSpec(
            num_scalar_prefetch=1,
            grid=(1,),
            in_specs=[flat(rewards.shape), flat(order.shape)],
            out_specs=(flat((8, LANES)), flat((1, LANES)), flat((1, LANES))),
        ),
        compiler_params=pltpu.CompilerParams(vmem_limit_bytes=16 * 2**20),
        cost_estimate=pl.CostEstimate(flops=1000000, bytes_accessed=60000000, transcendentals=128),
        name="pairs",
    )(place, rewards, order)


def weigh_kernel(coef_ref, keep_ref, got_ref, out_ref):
    own = coef_ref[0:1, 0:1]
    sib = coef_ref[1:2, 0:1]
    out_ref[...] = (keep_ref[...].astype(F32) * own + got_ref[...].astype(F32) * sib).astype(BF16)


def weigh(coef, keep, got):
    return pl.pallas_call(
        weigh_kernel,
        out_shape=jax.ShapeDtypeStruct(keep.shape, BF16),
        compiler_params=pltpu.CompilerParams(vmem_limit_bytes=16 * 2**20),
        cost_estimate=pl.CostEstimate(flops=1000000, bytes_accessed=2000000, transcendentals=0),
        name="weigh",
    )(coef, keep, got)


def finish_kernel(half, place, mine_ref, other_ref, gain_ref, head_ref, grad_ref, ghead_ref, ggain_ref):
    step = pl.program_id(0)

    @pl.when(step == place[1])
    def _():
        grad_ref[...] = mine_ref[:half, :].astype(F32)

    @pl.when(step != place[1])
    def _():
        grad_ref[...] = other_ref[:half, :].astype(F32)

    pooled = mine_ref[half : half + 16, :].astype(F32)[:1]
    ghead_ref[...] = gain_ref[...] * pooled
    ggain_ref[...] = head_ref[...] * pooled


def finish(place, mine, other, gain_final, w_head, half):
    feat = mine.shape[1]
    flat = pl.BlockSpec(mine.shape, lambda i, s: (0, 0))
    share = pl.BlockSpec((1, feat), lambda i, s: (0, s[0]))
    line = pl.BlockSpec((1, feat), lambda i, s: (0, 0))
    return pl.pallas_call(
        functools.partial(finish_kernel, half),
        out_shape=(
            jax.ShapeDtypeStruct((NCORE * half, feat), F32),
            jax.ShapeDtypeStruct((1, feat), F32),
            jax.ShapeDtypeStruct((1, feat), F32),
        ),
        grid_spec=pltpu.PrefetchScalarGridSpec(
            num_scalar_prefetch=1,
            grid=(NCORE,),
            in_specs=[flat, flat, share, share],
            out_specs=(pl.BlockSpec((half, feat), lambda i, s: (i, 0)), line, line),
        ),
        compiler_params=pltpu.CompilerParams(vmem_limit_bytes=16 * 2**20),
        cost_estimate=pl.CostEstimate(flops=1000000, bytes_accessed=4000000, transcendentals=0),
        name="finish",
    )(place, mine, other, gain_final[None], w_head[None])


def body(
    hidden_rows,
    lengths,
    pair_order,
    gain_attn,
    w_query,
    key_weight,
    value_weight,
    w_out,
    gain_final,
    w_head,
):
    rows, width = hidden_rows.shape
    n_mp = lax.axis_size("mp")
    n_dp = lax.axis_size("dp")
    feat = width // n_mp
    me = lax.axis_index("dp").astype(jnp.int32)
    core = me % NCORE
    along_x, along_z, near = dp_groups()
    place = jnp.stack([lax.axis_index("mp").astype(jnp.int32), core, lengths[0], me])

    mixed = front(hidden_rows, lengths, gain_attn, w_query, key_weight, value_weight)

    mixed, w_out, hidden_rows = lax.optimization_barrier((mixed, w_out, hidden_rows))
    mixed_all = lax.all_gather(mixed, "mp", axis=0, tiled=False)
    piece_rows = w_out.shape[0] // NEAR
    my_near = (me // (NZ * NCORE)) * NCORE + core
    w_piece = lax.dynamic_slice_in_dim(w_out, my_near * piece_rows, piece_rows, 0)
    w_piece = w_piece.reshape(piece_rows, n_mp, feat).swapaxes(0, 1)
    w_piece = lax.all_to_all(w_piece, "mp", 0, 0, tiled=True)
    w_parts = swap(jnp.broadcast_to(w_piece[None], (NEAR,) + w_piece.shape), near)

    x_cols = lax.dynamic_slice_in_dim(hidden_rows, place[0] * feat, feat, 1)
    resid, stats = project(place, mixed_all, w_parts, x_cols, gain_final, w_head)
    stats = lax.all_to_all(stats, "mp", 0, 0, tiled=True)
    reward, stats = lax.optimization_barrier((reward_of(lengths, stats, width, n_dp), stats))
    rewards = lax.all_to_all(reward, "dp", 0, 0, tiled=True)

    half = width // NCORE
    piece = -(-(half + 1) // (NX * NZ * 8)) * 8
    half_ext = piece * NX * NZ
    send, keep = gradient_halves(place, stats, resid, gain_final, w_head, mixed_all, half_ext)
    send, rewards = lax.optimization_barrier((send, rewards))
    got = to_sibling(send)
    seqs = pair_order.shape[0]
    order = jnp.pad(pair_order, (0, LANES - seqs), constant_values=-1)[None]
    coef, margin, reward_row = pair_weights(place, rewards, order)
    summed = weigh(coef, keep, got)
    loss = jnp.sum(jax.nn.softplus(-margin[0, :seqs:2]))

    got = swap(summed.reshape(NX, NZ * piece, feat), along_x)
    summed = jnp.sum(got.astype(F32), axis=0).astype(BF16)
    got = swap(summed.reshape(NZ, piece, feat), along_z)
    mine = jnp.sum(got.astype(F32), axis=0).astype(BF16)
    got = swap(jnp.broadcast_to(mine[None], (NZ, piece, feat)), along_z)
    got = swap(jnp.broadcast_to(got.reshape(1, NZ * piece, feat), (NX, NZ * piece, feat)), along_x)
    got = got.reshape(half_ext, feat)
    other = to_sibling(got)
    grad_out_proj, grad_head, grad_gain = finish(place, got, other, gain_final, w_head, half)
    return (loss, reward_row[0, :seqs], grad_out_proj, grad_head[0], grad_gain[0])


def solution(mesh):
    placed = (
        P("dp", None),
        P("dp"),
        P(),
        P(),
        P(None, "mp"),
        P(None, "mp"),
        P(None, "mp"),
        P("mp", None),
        P(),
        P(),
    )
    return jax.shard_map(
        body,
        mesh=mesh,
        in_specs=placed,
        out_specs=(P(), P(), P(None, "mp"), P("mp"), P("mp")),
        check_vma=False,
    )
```

```python
import functools

import jax
import jax.numpy as jnp
import numpy as np
from jax import lax
from jax.experimental import pallas as pl
from jax.experimental.pallas import tpu as pltpu
from jax.sharding import PartitionSpec as P

QUERY_HEADS = 32
KEY_VALUE_HEADS = 8
HEAD_SIZE = 64
NX, NZ, NCORE = 4, 12, 2
NEAR = NX * NCORE
ZB = 4

EPS = 1e-05
THETA = 500000.0
LANES = 128
F32 = jnp.float32
BF16 = jnp.bfloat16


def device_of(x, z, core):
    return (x * NZ + z) * NCORE + core


def dp_groups():
    along_x = [[device_of(x, z, c) for x in range(NX)] for z in range(NZ) for c in range(NCORE)]
    columns = [(x, c) for x in range(NX) for c in range(NCORE)]
    close_z = [[device_of(x, b * ZB + z, c) for z in range(ZB)] for x, c in columns for b in range(NZ // ZB)]
    far_z = [[device_of(x, b * ZB + z, c) for b in range(NZ // ZB)] for x, c in columns for z in range(ZB)]
    near = [[device_of(x, z, c) for x in range(NX) for c in range(NCORE)] for z in range(NZ)]
    return along_x, close_z, far_z, near


def swap(parts, groups):
    return lax.all_to_all(parts, "dp", 0, 0, tiled=True, axis_index_groups=groups)


def to_sibling(x):
    pairs = [(i, i ^ 1) for i in range(NX * NZ * NCORE)]
    return lax.ppermute(x, "dp", pairs)


def dot(a, b, a_dim, b_dim, precision=None):
    return lax.dot_general(
        a, b, (((a_dim,), (b_dim,)), ((), ())), preferred_element_type=F32, precision=precision
    )


def front_kernel(lens, x_hbm, gain_ref, wq_hbm, wk_hbm, wv_hbm, freq_ref, out_ref, x_ref, wq_ref, wk_ref, wv_ref, k_ref, v_ref, sems):
    total_rows = x_ref.shape[0]
    blocks = 2
    rows = total_rows // blocks
    copies = [
        pltpu.make_async_copy(x_hbm.at[pl.ds(0, rows)], x_ref.at[pl.ds(0, rows)], sems.at[0]),
        pltpu.make_async_copy(wq_hbm, wq_ref, sems.at[1]),
        pltpu.make_async_copy(wk_hbm, wk_ref, sems.at[2]),
        pltpu.make_async_copy(wv_hbm, wv_ref, sems.at[3]),
        pltpu.make_async_copy(x_hbm.at[pl.ds(rows, rows)], x_ref.at[pl.ds(rows, rows)], sems.at[4]),
    ]
    for copy in copies:
        copy.start()
    used = lens[0]
    lane = lax.broadcasted_iota(jnp.int32, (rows, LANES), 1)
    first_half = (lane % HEAD_SIZE) < HEAD_SIZE // 2
    low = lane < HEAD_SIZE
    gain = gain_ref[...]

    def tables(first):
        row = first + lax.broadcasted_iota(jnp.int32, (rows, LANES), 0)
        position = row - jnp.where(row >= used, used, 0)
        angle = position.astype(F32) * freq_ref[...]
        sine = jnp.sin(angle)
        return jnp.cos(angle), jnp.where(first_half, -sine, sine)

    turns = [tables(i * rows) for i in range(blocks)]

    def rotate(t, turn):
        partner = jnp.where(
            first_half, pltpu.roll(t, LANES - HEAD_SIZE // 2, 1), pltpu.roll(t, HEAD_SIZE // 2, 1)
        )
        return t * turn[0] + partner * turn[1]

    def norm(i):
        x = x_ref[i * rows : (i + 1) * rows, :].astype(F32)
        return (x * lax.rsqrt(jnp.mean(x * x, axis=1, keepdims=True) + EPS) * gain).astype(BF16)

    def attend(query, first, cols):
        row = first + lax.broadcasted_iota(jnp.int32, (rows, cols), 0)
        col = lax.broadcasted_iota(jnp.int32, (rows, cols), 1)
        allowed = (col <= row) & ((row >= used) == (col >= used))
        for p in range(len(query)):
            total = jnp.zeros((rows, LANES), F32)
            for e in range(LANES // HEAD_SIZE):
                scores = dot(query[p], k_ref[e, :cols, :], 1, 1) * HEAD_SIZE ** (-0.5)
                scores = jnp.where(allowed, scores, -1e30)
                top = jnp.max(scores, axis=1, keepdims=True)
                weights = jnp.exp(scores - top)
                probs = weights * (1.0 / jnp.sum(weights, axis=1, keepdims=True))
                total = total + dot(probs.astype(BF16), v_ref[e, :cols, :], 1, 0)
            out_ref[first : first + rows, p * LANES : (p + 1) * LANES] = total.astype(BF16)

    copies[0].wait()
    for i in range(blocks):
        if i == 1:
            copies[4].wait()
        normed = norm(i)
        if i == 0:
            for copy in copies[1:4]:
                copy.wait()
        query = dot(normed, wq_ref[...], 1, 0)
        key = dot(normed, wk_ref[...], 1, 1)
        value = dot(normed, wv_ref[...], 1, 1)
        key = rotate(jnp.concatenate([key, key], axis=1), turns[i])
        value = jnp.concatenate([value, value], axis=1)
        here = slice(i * rows, (i + 1) * rows)
        k_ref[0, here, :] = jnp.where(low, key, 0.0).astype(BF16)
        k_ref[1, here, :] = jnp.where(low, 0.0, key).astype(BF16)
        v_ref[0, here, :] = jnp.where(low, value, 0.0).astype(BF16)
        v_ref[1, here, :] = jnp.where(low, 0.0, value).astype(BF16)
        turned = [
            rotate(query[:, p * LANES : (p + 1) * LANES], turns[i]).astype(BF16)
            for p in range(query.shape[1] // LANES)
        ]
        attend(turned, i * rows, (i + 1) * rows)


def front(hidden_rows, lengths, gain_attn, w_query, key_weight, value_weight):
    rows, width = hidden_rows.shape
    key_weight, value_weight = key_weight.T, value_weight.T
    gain = gain_attn[None]
    half = HEAD_SIZE // 2
    freq = np.tile(THETA ** (-np.arange(half) * 2.0 / HEAD_SIZE), LANES // half).astype(np.float32)[None]
    whole = lambda a: pl.BlockSpec(a.shape, lambda i, s: (0, 0))
    far = pl.BlockSpec(memory_space=pl.ANY)
    return pl.pallas_call(
        front_kernel,
        out_shape=jax.ShapeDtypeStruct((rows, w_query.shape[1]), BF16),
        grid_spec=pltpu.PrefetchScalarGridSpec(
            num_scalar_prefetch=1,
            grid=(1,),
            in_specs=[far, whole(gain), far, far, far, whole(freq)],
            out_specs=pl.BlockSpec((rows, w_query.shape[1]), lambda i, s: (0, 0)),
            scratch_shapes=[
                pltpu.VMEM(hidden_rows.shape, BF16),
                pltpu.VMEM(w_query.shape, BF16),
                pltpu.VMEM(key_weight.shape, BF16),
                pltpu.VMEM(value_weight.shape, BF16),
                pltpu.VMEM((2, rows, LANES), BF16),
                pltpu.VMEM((2, rows, LANES), BF16),
                pltpu.SemaphoreType.DMA((5,)),
            ],
        ),
        compiler_params=pltpu.CompilerParams(vmem_limit_bytes=58 * 2**20),
        cost_estimate=pl.CostEstimate(flops=1500000000, bytes_accessed=4000000, transcendentals=900000),
        name="front",
    )(lengths, hidden_rows, gain, w_query, key_weight, value_weight, jnp.asarray(freq))


def project_kernel(place, mixed_hbm, w_hbm, x_ref, gain_ref, head_ref, resid_ref, stats_ref, mixed_ref, w_ref, sems):
    groups = mixed_ref.shape[0]
    rows, feat = resid_ref.shape
    copies = [pltpu.make_async_copy(mixed_hbm.at[g], mixed_ref.at[g], sems.at[g]) for g in range(groups)]
    weights = pltpu.make_async_copy(w_hbm, w_ref, sems.at[groups])
    copies[0].start()
    weights.start()
    for copy in copies[1:]:
        copy.start()
    resid_ref[...] = x_ref[...].astype(F32)
    weights.wait()
    for g in range(groups):
        copies[g].wait()
        weight = w_ref[:, g].reshape(-1, feat)
        resid_ref[...] += dot(mixed_ref[g], weight, 1, 0).astype(BF16).astype(F32)
    resid = resid_ref[...]
    both = gain_ref[...] * head_ref[...]
    squares = dot(jnp.ones((8, feat), F32), resid * resid, 1, 1, lax.Precision.HIGHEST)
    scores = dot(jnp.broadcast_to(both, (8, feat)), resid, 1, 1, lax.Precision.HIGHEST)
    pair = jnp.concatenate([squares[:1], scores[:1]], axis=0)
    stats_ref[...] = jnp.broadcast_to(pair[None], stats_ref.shape)


def project(place, mixed_all, w_parts, x_cols, gain_final, w_head):
    n_mp, rows, heads = mixed_all.shape
    feat = w_parts.shape[-1]
    share = pl.BlockSpec((1, feat), lambda i, s: (0, s[0]))
    flat = lambda a: pl.BlockSpec(a.shape, lambda i, s: (0,) * len(a.shape))
    return pl.pallas_call(
        project_kernel,
        out_shape=(
            jax.ShapeDtypeStruct((rows, feat), F32),
            jax.ShapeDtypeStruct((n_mp, 2, rows), F32),
        ),
        grid_spec=pltpu.PrefetchScalarGridSpec(
            num_scalar_prefetch=1,
            grid=(1,),
            in_specs=[
                pl.BlockSpec(memory_space=pl.ANY),
                pl.BlockSpec(memory_space=pl.ANY),
                flat(x_cols),
                share,
                share,
            ],
            out_specs=(
                pl.BlockSpec((rows, feat), lambda i, s: (0, 0)),
                pl.BlockSpec((n_mp, 2, rows), lambda i, s: (0, 0, 0)),
            ),
            scratch_shapes=[
                pltpu.VMEM(mixed_all.shape, BF16),
                pltpu.VMEM(w_parts.shape, BF16),
                pltpu.SemaphoreType.DMA((n_mp + 1,)),
            ],
        ),
        compiler_params=pltpu.CompilerParams(vmem_limit_bytes=58 * 2**20),
        cost_estimate=pl.CostEstimate(flops=550000000, bytes_accessed=4000000, transcendentals=0),
        name="project",
    )(place, mixed_all, w_parts, x_cols, gain_final[None], w_head[None])


def row_terms(stats, used, width):
    sums = stats[0]
    for part in range(1, stats.shape[0]):
        sums = sums + stats[part]
    scale = lax.rsqrt(sums[:1] / width + EPS)
    score = sums[1:2] * scale
    row = lax.broadcasted_iota(jnp.int32, scale.shape, 1)
    inside = row < used
    return scale, score, inside


def reward_kernel(width, lens, stats_ref, out_ref):
    _, score, inside = row_terms(stats_ref, lens[0], width)
    total = jnp.sum(jnp.where(inside, score, 0.0), axis=1, keepdims=True)
    reward = total / lens[0].astype(F32)
    out_ref[...] = jnp.broadcast_to(reward[None], out_ref.shape)


def reward_of(lengths, stats, width, n_dp):
    return pl.pallas_call(
        functools.partial(reward_kernel, width),
        out_shape=jax.ShapeDtypeStruct((n_dp, 1, LANES), F32),
        grid_spec=pltpu.PrefetchScalarGridSpec(
            num_scalar_prefetch=1,
            grid=(1,),
            in_specs=[pl.BlockSpec(stats.shape, lambda i, s: (0, 0, 0))],
            out_specs=pl.BlockSpec((n_dp, 1, LANES), lambda i, s: (0, 0, 0)),
        ),
        compiler_params=pltpu.CompilerParams(vmem_limit_bytes=16 * 2**20),
        cost_estimate=pl.CostEstimate(flops=10000, bytes_accessed=90000, transcendentals=512),
        name="reward",
    )(lengths, stats)


def gradient_kernel(width, place, stats_ref, resid_ref, gain_ref, head_ref, mixed_ref, send_ref, keep_ref, d_ref, p_ref):
    step = pl.program_id(0)
    groups, rows, heads = mixed_ref.shape
    feat = resid_ref.shape[1]
    half = groups * heads

    @pl.when(step == 0)
    def _():
        used = place[2]
        scale, score, inside = row_terms(stats_ref, used, width)
        weight = jnp.where(inside, scale, 0.0) / used.astype(F32)
        minus = weight * scale * score * (1.0 / width)
        plus = jnp.broadcast_to(weight, (LANES, rows)).T
        minus = jnp.broadcast_to(minus, (LANES, rows)).T
        both = gain_ref[...] * head_ref[...]
        for part in range(feat // LANES):
            at = slice(part * LANES, (part + 1) * LANES)
            resid = resid_ref[:, at]
            d_ref[:, at] = (plus * both[:, at] - minus * resid).astype(BF16)
            pooled = jnp.sum(plus * resid, axis=0, keepdims=True)
            p_ref[:, at] = jnp.broadcast_to(pooled, (8, LANES))

    def fill(out_ref):
        for g in range(groups):
            out_ref[g * heads : (g + 1) * heads, :] = dot(mixed_ref[g], d_ref[...], 0, 0).astype(BF16)
        extra = out_ref.shape[0] - half
        first = lax.broadcasted_iota(jnp.int32, (extra, feat), 0) == 0
        out_ref[half:, :] = jnp.where(first, p_ref[:1, :], 0.0).astype(BF16)

    @pl.when(step == 0)
    def _():
        fill(send_ref)

    @pl.when(step == 1)
    def _():
        fill(keep_ref)


def gradient_halves(place, stats, resid, gain_final, w_head, mixed_all, half_ext):
    n_mp, rows, heads = mixed_all.shape
    feat = resid.shape[1]
    width = gain_final.shape[0]
    share = pl.BlockSpec((1, feat), lambda i, s: (0, s[0]))
    half = jax.ShapeDtypeStruct((half_ext, feat), BF16)
    half_spec = pl.BlockSpec((half_ext, feat), lambda i, s: (0, 0))
    return pl.pallas_call(
        functools.partial(gradient_kernel, width),
        out_shape=(half, half),
        grid_spec=pltpu.PrefetchScalarGridSpec(
            num_scalar_prefetch=1,
            grid=(NCORE,),
            in_specs=[
                pl.BlockSpec(stats.shape, lambda i, s: (0, 0, 0)),
                pl.BlockSpec(resid.shape, lambda i, s: (0, 0)),
                share,
                share,
                pl.BlockSpec((n_mp // NCORE, rows, heads), lambda i, s: (i * s[1] + (1 - i) * (1 - s[1]), 0, 0)),
            ],
            out_specs=(half_spec, half_spec),
            scratch_shapes=[pltpu.VMEM((rows, feat), BF16), pltpu.VMEM((8, feat), F32)],
        ),
        compiler_params=pltpu.CompilerParams(vmem_limit_bytes=48 * 2**20),
        cost_estimate=pl.CostEstimate(flops=550000000, bytes_accessed=4000000, transcendentals=0),
        name="gradient",
    )(place, stats, resid, gain_final[None], w_head[None], mixed_all)


def weigh_kernel(place, rewards_ref, order_ref, keep_ref, got_ref, out_ref, margin_ref, row_ref):
    seqs = rewards_ref.shape[0]
    rewards = rewards_ref[...].reshape(seqs, LANES)
    order = order_ref[...]
    seq = lax.broadcasted_iota(jnp.int32, (seqs, LANES), 0)
    picked = jnp.sum(jnp.where(seq == order, rewards, 0.0), axis=0, keepdims=True)
    lane = lax.broadcasted_iota(jnp.int32, (1, LANES), 1)
    chosen = lane % 2 == 0
    partner = jnp.where(chosen, pltpu.roll(picked, LANES - 1, 1), pltpu.roll(picked, 1, 1))
    margin = jnp.where(chosen, picked - partner, partner - picked)
    sig = 1.0 / (1.0 + jnp.exp(margin))
    dreward = jnp.where(chosen, -sig, sig)
    me = place[3]
    own = jnp.sum(jnp.where(order == me, dreward, 0.0), axis=1, keepdims=True)
    sib = jnp.sum(jnp.where(order == (me ^ 1), dreward, 0.0), axis=1, keepdims=True)
    out_ref[...] = (keep_ref[...].astype(F32) * own + got_ref[...].astype(F32) * sib).astype(BF16)
    margin_ref[...] = margin
    at = lax.broadcasted_iota(jnp.int32, (seqs, LANES), 1)
    row_ref[...] = jnp.sum(jnp.where(seq == at, rewards, 0.0), axis=0, keepdims=True)


def weigh(place, rewards, order, keep, got):
    flat = lambda a: pl.BlockSpec(a.shape, lambda i, s: (0,) * len(a.shape))
    return pl.pallas_call(
        weigh_kernel,
        out_shape=(
            jax.ShapeDtypeStruct(keep.shape, BF16),
            jax.ShapeDtypeStruct((1, LANES), F32),
            jax.ShapeDtypeStruct((1, LANES), F32),
        ),
        grid_spec=pltpu.PrefetchScalarGridSpec(
            num_scalar_prefetch=1,
            grid=(1,),
            in_specs=[flat(rewards), flat(order), flat(keep), flat(got)],
            out_specs=(flat(keep),) + (pl.BlockSpec((1, LANES), lambda i, s: (0, 0)),) * 2,
        ),
        compiler_params=pltpu.CompilerParams(vmem_limit_bytes=16 * 2**20),
        cost_estimate=pl.CostEstimate(flops=1000000, bytes_accessed=2000000, transcendentals=128),
        name="weigh",
    )(place, rewards, order, keep, got)


def finish_kernel(half, place, mine_ref, other_ref, gain_ref, head_ref, grad_ref, ghead_ref, ggain_ref):
    step = pl.program_id(0)

    @pl.when(step == place[1])
    def _():
        grad_ref[...] = mine_ref[:half, :].astype(F32)

    @pl.when(step != place[1])
    def _():
        grad_ref[...] = other_ref[:half, :].astype(F32)

    pooled = mine_ref[half : half + 16, :].astype(F32)[:1]
    ghead_ref[...] = gain_ref[...] * pooled
    ggain_ref[...] = head_ref[...] * pooled


def finish(place, mine, other, gain_final, w_head, half):
    feat = mine.shape[1]
    flat = pl.BlockSpec(mine.shape, lambda i, s: (0, 0))
    share = pl.BlockSpec((1, feat), lambda i, s: (0, s[0]))
    line = pl.BlockSpec((1, feat), lambda i, s: (0, 0))
    return pl.pallas_call(
        functools.partial(finish_kernel, half),
        out_shape=(
            jax.ShapeDtypeStruct((NCORE * half, feat), F32),
            jax.ShapeDtypeStruct((1, feat), F32),
            jax.ShapeDtypeStruct((1, feat), F32),
        ),
        grid_spec=pltpu.PrefetchScalarGridSpec(
            num_scalar_prefetch=1,
            grid=(NCORE,),
            in_specs=[flat, flat, share, share],
            out_specs=(pl.BlockSpec((half, feat), lambda i, s: (i, 0)), line, line),
        ),
        compiler_params=pltpu.CompilerParams(vmem_limit_bytes=16 * 2**20),
        cost_estimate=pl.CostEstimate(flops=1000000, bytes_accessed=4000000, transcendentals=0),
        name="finish",
    )(place, mine, other, gain_final[None], w_head[None])


def body(
    hidden_rows,
    lengths,
    pair_order,
    gain_attn,
    w_query,
    key_weight,
    value_weight,
    w_out,
    gain_final,
    w_head,
):
    rows, width = hidden_rows.shape
    n_mp = lax.axis_size("mp")
    n_dp = lax.axis_size("dp")
    feat = width // n_mp
    me = lax.axis_index("dp").astype(jnp.int32)
    core = me % NCORE
    along_x, close_z, far_z, near = dp_groups()
    place = jnp.stack([lax.axis_index("mp").astype(jnp.int32), core, lengths[0], me])

    mixed = front(hidden_rows, lengths, gain_attn, w_query, key_weight, value_weight)

    mixed, w_out, hidden_rows = lax.optimization_barrier((mixed, w_out, hidden_rows))
    mixed_all = lax.all_gather(mixed, "mp", axis=0, tiled=False)
    piece_rows = w_out.shape[0] // NEAR
    my_near = (me // (NZ * NCORE)) * NCORE + core
    w_piece = lax.dynamic_slice_in_dim(w_out, my_near * piece_rows, piece_rows, 0)
    w_piece = w_piece.reshape(piece_rows, n_mp, feat).swapaxes(0, 1)
    w_piece = lax.all_to_all(w_piece, "mp", 0, 0, tiled=True)
    w_parts = swap(jnp.broadcast_to(w_piece[None], (NEAR,) + w_piece.shape), near)

    x_cols = lax.dynamic_slice_in_dim(hidden_rows, place[0] * feat, feat, 1)
    resid, stats = project(place, mixed_all, w_parts, x_cols, gain_final, w_head)
    stats = lax.all_to_all(stats, "mp", 0, 0, tiled=True)
    reward, stats = lax.optimization_barrier((reward_of(lengths, stats, width, n_dp), stats))
    rewards = lax.all_to_all(reward, "dp", 0, 0, tiled=True)

    half = width // NCORE
    piece = -(-(half + 16) // (NX * ZB * 8)) * 8
    half_ext = piece * NX * ZB
    send, keep = gradient_halves(place, stats, resid, gain_final, w_head, mixed_all, half_ext)
    got = to_sibling(send)
    seqs = pair_order.shape[0]
    order = jnp.pad(pair_order, (0, LANES - seqs), constant_values=-1)[None]
    summed, margin, reward_row = weigh(place, rewards, order, keep, got)
    loss = jnp.sum(jax.nn.softplus(-margin[0, :seqs:2]))

    got = swap(summed.reshape(NX, ZB * piece, feat), along_x)
    summed = jnp.sum(got.astype(F32), axis=0).astype(BF16)
    got = swap(summed.reshape(ZB, piece, feat), close_z)
    summed = jnp.sum(got.astype(F32), axis=0).astype(BF16)
    got = swap(jnp.broadcast_to(summed[None], (NZ // ZB, piece, feat)), far_z)
    summed = jnp.sum(got.astype(F32), axis=0).astype(BF16)
    got = swap(jnp.broadcast_to(summed[None], (ZB, piece, feat)), close_z)
    got = swap(jnp.broadcast_to(got.reshape(1, ZB * piece, feat), (NX, ZB * piece, feat)), along_x)
    got = got.reshape(half_ext, feat)
    other = to_sibling(got)
    grad_out_proj, grad_head, grad_gain = finish(place, got, other, gain_final, w_head, half)
    return (loss, reward_row[0, :seqs], grad_out_proj, grad_head[0], grad_gain[0])


def solution(mesh):
    placed = (
        P("dp", None),
        P("dp"),
        P(),
        P(),
        P(None, "mp"),
        P(None, "mp"),
        P(None, "mp"),
        P("mp", None),
        P(),
        P(),
    )
    return jax.shard_map(
        body,
        mesh=mesh,
        in_specs=placed,
        out_specs=(P(), P(), P(None, "mp"), P("mp"), P("mp")),
        check_vma=False,
    )
```

```python
import functools

import jax
import jax.numpy as jnp
import numpy as np
from jax import lax
from jax.experimental import pallas as pl
from jax.experimental.pallas import tpu as pltpu
from jax.sharding import PartitionSpec as P

QUERY_HEADS = 32
KEY_VALUE_HEADS = 8
HEAD_SIZE = 64
NX, NZ, NCORE = 4, 12, 2
NEAR = NX * NCORE

EPS = 1e-05
THETA = 500000.0
LANES = 128
F32 = jnp.float32
BF16 = jnp.bfloat16


def device_of(x, z, core):
    return (x * NZ + z) * NCORE + core


def dp_groups():
    along_x = [[device_of(x, z, c) for x in range(NX)] for z in range(NZ) for c in range(NCORE)]
    along_z = [[device_of(x, z, c) for z in range(NZ)] for x in range(NX) for c in range(NCORE)]
    near = [[device_of(x, z, c) for x in range(NX) for c in range(NCORE)] for z in range(NZ)]
    return along_x, along_z, near


def swap(parts, groups):
    return lax.all_to_all(parts, "dp", 0, 0, tiled=True, axis_index_groups=groups)


def to_sibling(x):
    pairs = [(i, i ^ 1) for i in range(NX * NZ * NCORE)]
    return lax.ppermute(x, "dp", pairs)


def dot(a, b, a_dim, b_dim, precision=None):
    return lax.dot_general(
        a, b, (((a_dim,), (b_dim,)), ((), ())), preferred_element_type=F32, precision=precision
    )


def front_kernel(lens, x_hbm, gain_ref, wq_hbm, wk_hbm, wv_hbm, freq_ref, out_ref, x_ref, wq_ref, wk_ref, wv_ref, k_ref, v_ref, sems):
    total_rows = x_ref.shape[0]
    blocks = 2
    rows = total_rows // blocks
    copies = [
        pltpu.make_async_copy(x_hbm.at[pl.ds(0, rows)], x_ref.at[pl.ds(0, rows)], sems.at[0]),
        pltpu.make_async_copy(wq_hbm, wq_ref, sems.at[1]),
        pltpu.make_async_copy(wk_hbm, wk_ref, sems.at[2]),
        pltpu.make_async_copy(wv_hbm, wv_ref, sems.at[3]),
        pltpu.make_async_copy(x_hbm.at[pl.ds(rows, rows)], x_ref.at[pl.ds(rows, rows)], sems.at[4]),
    ]
    for copy in copies:
        copy.start()
    used = lens[0]
    lane = lax.broadcasted_iota(jnp.int32, (rows, LANES), 1)
    first_half = (lane % HEAD_SIZE) < HEAD_SIZE // 2
    low = lane < HEAD_SIZE
    gain = gain_ref[...]

    def tables(first):
        row = first + lax.broadcasted_iota(jnp.int32, (rows, LANES), 0)
        position = row - jnp.where(row >= used, used, 0)
        angle = position.astype(F32) * freq_ref[...]
        sine = jnp.sin(angle)
        return jnp.cos(angle), jnp.where(first_half, -sine, sine)

    turns = [tables(i * rows) for i in range(blocks)]

    def rotate(t, turn):
        partner = jnp.where(
            first_half, pltpu.roll(t, LANES - HEAD_SIZE // 2, 1), pltpu.roll(t, HEAD_SIZE // 2, 1)
        )
        return t * turn[0] + partner * turn[1]

    def norm(i):
        x = x_ref[i * rows : (i + 1) * rows, :].astype(F32)
        return (x * lax.rsqrt(jnp.mean(x * x, axis=1, keepdims=True) + EPS) * gain).astype(BF16)

    def attend(query, first, cols):
        row = first + lax.broadcasted_iota(jnp.int32, (rows, cols), 0)
        col = lax.broadcasted_iota(jnp.int32, (rows, cols), 1)
        allowed = (col <= row) & ((row >= used) == (col >= used))
        for p in range(len(query)):
            total = jnp.zeros((rows, LANES), F32)
            for e in range(LANES // HEAD_SIZE):
                scores = dot(query[p], k_ref[e, :cols, :], 1, 1) * HEAD_SIZE ** (-0.5)
                scores = jnp.where(allowed, scores, -1e30)
                top = jnp.max(scores, axis=1, keepdims=True)
                weights = jnp.exp(scores - top)
                probs = weights * (1.0 / jnp.sum(weights, axis=1, keepdims=True))
                total = total + dot(probs.astype(BF16), v_ref[e, :cols, :], 1, 0)
            out_ref[first : first + rows, p * LANES : (p + 1) * LANES] = total.astype(BF16)

    copies[0].wait()
    for i in range(blocks):
        if i == 1:
            copies[4].wait()
        normed = norm(i)
        if i == 0:
            for copy in copies[1:4]:
                copy.wait()
        query = dot(normed, wq_ref[...], 1, 0)
        key = dot(normed, wk_ref[...], 1, 1)
        value = dot(normed, wv_ref[...], 1, 1)
        key = rotate(jnp.concatenate([key, key], axis=1), turns[i])
        value = jnp.concatenate([value, value], axis=1)
        here = slice(i * rows, (i + 1) * rows)
        k_ref[0, here, :] = jnp.where(low, key, 0.0).astype(BF16)
        k_ref[1, here, :] = jnp.where(low, 0.0, key).astype(BF16)
        v_ref[0, here, :] = jnp.where(low, value, 0.0).astype(BF16)
        v_ref[1, here, :] = jnp.where(low, 0.0, value).astype(BF16)
        turned = [
            rotate(query[:, p * LANES : (p + 1) * LANES], turns[i]).astype(BF16)
            for p in range(query.shape[1] // LANES)
        ]
        attend(turned, i * rows, (i + 1) * rows)


def front(hidden_rows, lengths, gain_attn, w_query, key_weight, value_weight):
    rows, width = hidden_rows.shape
    key_weight, value_weight = key_weight.T, value_weight.T
    gain = gain_attn[None]
    half = HEAD_SIZE // 2
    freq = np.tile(THETA ** (-np.arange(half) * 2.0 / HEAD_SIZE), LANES // half).astype(np.float32)[None]
    whole = lambda a: pl.BlockSpec(a.shape, lambda i, s: (0, 0))
    far = pl.BlockSpec(memory_space=pl.ANY)
    return pl.pallas_call(
        front_kernel,
        out_shape=jax.ShapeDtypeStruct((rows, w_query.shape[1]), BF16),
        grid_spec=pltpu.PrefetchScalarGridSpec(
            num_scalar_prefetch=1,
            grid=(1,),
            in_specs=[far, whole(gain), far, far, far, whole(freq)],
            out_specs=pl.BlockSpec((rows, w_query.shape[1]), lambda i, s: (0, 0)),
            scratch_shapes=[
                pltpu.VMEM(hidden_rows.shape, BF16),
                pltpu.VMEM(w_query.shape, BF16),
                pltpu.VMEM(key_weight.shape, BF16),
                pltpu.VMEM(value_weight.shape, BF16),
                pltpu.VMEM((2, rows, LANES), BF16),
                pltpu.VMEM((2, rows, LANES), BF16),
                pltpu.SemaphoreType.DMA((5,)),
            ],
        ),
        compiler_params=pltpu.CompilerParams(vmem_limit_bytes=58 * 2**20),
        cost_estimate=pl.CostEstimate(flops=1500000000, bytes_accessed=4000000, transcendentals=900000),
        name="front",
    )(lengths, hidden_rows, gain, w_query, key_weight, value_weight, jnp.asarray(freq))


def project_kernel(mixed_ref, w_ref, x_ref, both_ref, resid_ref, stats_ref):
    groups = mixed_ref.shape[0]
    rows, feat = resid_ref.shape
    resid = x_ref[...].astype(F32)
    for g in range(groups):
        weight = w_ref[:, g].reshape(-1, feat)
        resid = resid + dot(mixed_ref[g], weight, 1, 0).astype(BF16).astype(F32)
    resid_ref[...] = resid
    squares = dot(jnp.ones((8, feat), F32), resid * resid, 1, 1, lax.Precision.HIGHEST)
    scores = dot(jnp.broadcast_to(both_ref[...], (8, feat)), resid, 1, 1, lax.Precision.HIGHEST)
    pair = jnp.concatenate([squares[:1], scores[:1]], axis=0)
    stats_ref[...] = jnp.broadcast_to(pair[None], stats_ref.shape)


def project(mixed_all, w_parts, x_cols, both):
    n_mp, rows, heads = mixed_all.shape
    feat = w_parts.shape[-1]
    here = pl.BlockSpec(memory_space=pltpu.VMEM)
    return pl.pallas_call(
        project_kernel,
        out_shape=(
            jax.ShapeDtypeStruct((rows, feat), F32),
            jax.ShapeDtypeStruct((n_mp, 2, rows), F32),
        ),
        in_specs=[here] * 4,
        out_specs=(here, here),
        compiler_params=pltpu.CompilerParams(vmem_limit_bytes=32 * 2**20),
        cost_estimate=pl.CostEstimate(flops=550000000, bytes_accessed=4000000, transcendentals=0),
        name="project",
    )(mixed_all, w_parts, x_cols, both)


def row_terms(stats, used, width):
    sums = stats[0]
    for part in range(1, stats.shape[0]):
        sums = sums + stats[part]
    scale = lax.rsqrt(sums[:1] / width + EPS)
    score = sums[1:2] * scale
    row = lax.broadcasted_iota(jnp.int32, scale.shape, 1)
    inside = row < used
    return scale, score, inside


def reward_kernel(width, lens, stats_ref, out_ref):
    _, score, inside = row_terms(stats_ref, lens[0], width)
    total = jnp.sum(jnp.where(inside, score, 0.0), axis=1, keepdims=True)
    reward = total / lens[0].astype(F32)
    out_ref[...] = jnp.broadcast_to(reward[None], out_ref.shape)


def reward_of(lengths, stats, width, n_dp):
    return pl.pallas_call(
        functools.partial(reward_kernel, width),
        out_shape=jax.ShapeDtypeStruct((n_dp, 1, LANES), F32),
        grid_spec=pltpu.PrefetchScalarGridSpec(
            num_scalar_prefetch=1,
            grid=(1,),
            in_specs=[pl.BlockSpec(stats.shape, lambda i, s: (0, 0, 0))],
            out_specs=pl.BlockSpec((n_dp, 1, LANES), lambda i, s: (0, 0, 0)),
        ),
        compiler_params=pltpu.CompilerParams(vmem_limit_bytes=16 * 2**20),
        cost_estimate=pl.CostEstimate(flops=10000, bytes_accessed=90000, transcendentals=512),
        name="reward",
    )(lengths, stats)


def gradient_kernel(width, place, stats_ref, resid_ref, both_ref, mixed_hbm, send_ref, keep_ref, d_ref, mixed_ref, sems):
    rows, feat = resid_ref.shape
    heads = mixed_ref.shape[2]
    order = []
    for which in (1 - place[1], place[1]):
        for g in range(mixed_ref.shape[0] // NCORE):
            order.append(which * (mixed_ref.shape[0] // NCORE) + g)
    copies = [
        pltpu.make_async_copy(mixed_hbm.at[at], mixed_ref.at[i], sems.at[i]) for i, at in enumerate(order)
    ]
    for copy in copies:
        copy.start()
    groups = mixed_ref.shape[0] // NCORE
    used = place[2]
    scale, score, inside = row_terms(stats_ref, used, width)
    weight = jnp.where(inside, scale, 0.0) / used.astype(F32)
    minus = weight * scale * score * (1.0 / width)
    plus = jnp.broadcast_to(weight, (LANES, rows)).T
    minus = jnp.broadcast_to(minus, (LANES, rows)).T
    both = both_ref[...]
    pooled = []
    for part in range(feat // LANES):
        at = slice(part * LANES, (part + 1) * LANES)
        resid = resid_ref[:, at]
        d_ref[:, at] = (plus * both[:, at] - minus * resid).astype(BF16)
        pooled.append(jnp.sum(plus * resid, axis=0, keepdims=True))
    pooled = jnp.concatenate(pooled, axis=1)
    half = groups * heads
    extra = send_ref.shape[0] - half
    first = lax.broadcasted_iota(jnp.int32, (extra, feat), 0) == 0
    pooled = jnp.where(first, pooled, 0.0).astype(BF16)
    for part, out_ref in enumerate((send_ref, keep_ref)):
        for g in range(groups):
            copies[part * groups + g].wait()
            mixed = mixed_ref[part * groups + g]
            out_ref[g * heads : (g + 1) * heads, :] = dot(mixed, d_ref[...], 0, 0).astype(BF16)
        out_ref[half:, :] = pooled


def gradient_halves(place, stats, resid, both, mixed_all, half_ext, width):
    n_mp, rows, heads = mixed_all.shape
    feat = resid.shape[1]
    here = pl.BlockSpec(memory_space=pltpu.VMEM)
    half = jax.ShapeDtypeStruct((half_ext, feat), BF16)
    return pl.pallas_call(
        functools.partial(gradient_kernel, width),
        out_shape=(half, half),
        in_specs=[pl.BlockSpec(memory_space=pltpu.SMEM)] + [here] * 3 + [pl.BlockSpec(memory_space=pl.ANY)],
        out_specs=(here, here),
        scratch_shapes=[
            pltpu.VMEM((rows, feat), BF16),
            pltpu.VMEM(mixed_all.shape, BF16),
            pltpu.SemaphoreType.DMA((n_mp,)),
        ],
        compiler_params=pltpu.CompilerParams(vmem_limit_bytes=60 * 2**20),
        cost_estimate=pl.CostEstimate(flops=550000000, bytes_accessed=4000000, transcendentals=0),
        name="gradient",
    )(place, stats, resid, both, mixed_all)


def weigh_kernel(place, costs_ref, order_ref, keep_ref, got_ref, out_ref, margin_ref, row_ref):
    seqs = costs_ref.shape[0]
    rewards = -costs_ref[...].reshape(seqs, LANES)
    order = order_ref[...]
    seq = lax.broadcasted_iota(jnp.int32, (seqs, LANES), 0)
    picked = jnp.sum(jnp.where(seq == order, rewards, 0.0), axis=0, keepdims=True)
    lane = lax.broadcasted_iota(jnp.int32, (1, LANES), 1)
    chosen = lane % 2 == 0
    partner = jnp.where(chosen, pltpu.roll(picked, LANES - 1, 1), pltpu.roll(picked, 1, 1))
    margin = jnp.where(chosen, picked - partner, partner - picked)
    sig = 1.0 / (1.0 + jnp.exp(margin))
    dreward = jnp.where(chosen, -sig, sig)
    me = place[3]
    own = jnp.sum(jnp.where(order == me, dreward, 0.0), axis=1, keepdims=True)
    sib = jnp.sum(jnp.where(order == (me ^ 1), dreward, 0.0), axis=1, keepdims=True)
    out_ref[...] = (keep_ref[...].astype(F32) * own + got_ref[...].astype(F32) * sib).astype(BF16)
    margin_ref[...] = margin
    at = lax.broadcasted_iota(jnp.int32, (seqs, LANES), 1)
    row_ref[...] = jnp.sum(jnp.where(seq == at, rewards, 0.0), axis=0, keepdims=True)


def weigh(place, costs, order, keep, got):
    flat = lambda a: pl.BlockSpec(a.shape, lambda i, s: (0,) * len(a.shape))
    return pl.pallas_call(
        weigh_kernel,
        out_shape=(
            jax.ShapeDtypeStruct(keep.shape, BF16),
            jax.ShapeDtypeStruct((1, LANES), F32),
            jax.ShapeDtypeStruct((1, LANES), F32),
        ),
        grid_spec=pltpu.PrefetchScalarGridSpec(
            num_scalar_prefetch=1,
            grid=(1,),
            in_specs=[flat(costs), flat(order), flat(keep), flat(got)],
            out_specs=(flat(keep),) + (pl.BlockSpec((1, LANES), lambda i, s: (0, 0)),) * 2,
        ),
        compiler_params=pltpu.CompilerParams(vmem_limit_bytes=16 * 2**20),
        cost_estimate=pl.CostEstimate(flops=1000000, bytes_accessed=2000000, transcendentals=128),
        name="weigh",
    )(place, costs, order, keep, got)


def finish_kernel(half, place, mine_ref, other_ref, gain_ref, head_ref, grad_ref, ghead_ref, ggain_ref):
    step = pl.program_id(0)

    @pl.when(step == place[1])
    def _():
        grad_ref[...] = mine_ref[:half, :].astype(F32)

    @pl.when(step != place[1])
    def _():
        grad_ref[...] = other_ref[:half, :].astype(F32)

    pooled = mine_ref[half : half + 16, :].astype(F32)[:1]
    ghead_ref[...] = gain_ref[...] * pooled
    ggain_ref[...] = head_ref[...] * pooled


def finish(place, mine, other, gain_final, w_head, half):
    feat = mine.shape[1]
    flat = pl.BlockSpec(mine.shape, lambda i, s: (0, 0))
    share = pl.BlockSpec((1, feat), lambda i, s: (0, s[0]))
    line = pl.BlockSpec((1, feat), lambda i, s: (0, 0))
    return pl.pallas_call(
        functools.partial(finish_kernel, half),
        out_shape=(
            jax.ShapeDtypeStruct((NCORE * half, feat), F32),
            jax.ShapeDtypeStruct((1, feat), F32),
            jax.ShapeDtypeStruct((1, feat), F32),
        ),
        grid_spec=pltpu.PrefetchScalarGridSpec(
            num_scalar_prefetch=1,
            grid=(NCORE,),
            in_specs=[flat, flat, share, share],
            out_specs=(pl.BlockSpec((half, feat), lambda i, s: (i, 0)), line, line),
        ),
        compiler_params=pltpu.CompilerParams(vmem_limit_bytes=16 * 2**20),
        cost_estimate=pl.CostEstimate(flops=1000000, bytes_accessed=4000000, transcendentals=0),
        name="finish",
    )(place, mine, other, gain_final[None], w_head[None])


def body(
    hidden_rows,
    lengths,
    pair_order,
    gain_attn,
    w_query,
    key_weight,
    value_weight,
    w_out,
    gain_final,
    w_head,
):
    rows, width = hidden_rows.shape
    n_mp = lax.axis_size("mp")
    n_dp = lax.axis_size("dp")
    feat = width // n_mp
    me = lax.axis_index("dp").astype(jnp.int32)
    core = me % NCORE
    along_x, along_z, near = dp_groups()
    place = jnp.stack([lax.axis_index("mp").astype(jnp.int32), core, lengths[0], me])

    mixed = front(hidden_rows, lengths, gain_attn, w_query, key_weight, value_weight)

    mixed, w_out, hidden_rows, gain_final, w_head = lax.optimization_barrier(
        (mixed, w_out, hidden_rows, gain_final, w_head)
    )
    mixed_all = lax.all_gather(mixed, "mp", axis=0, tiled=False)
    piece_rows = w_out.shape[0] // NEAR
    my_near = (me // (NZ * NCORE)) * NCORE + core
    w_piece = lax.dynamic_slice_in_dim(w_out, my_near * piece_rows, piece_rows, 0)
    w_piece = w_piece.reshape(piece_rows, n_mp, feat).swapaxes(0, 1)
    w_piece = lax.all_to_all(w_piece, "mp", 0, 0, tiled=True)
    w_parts = swap(jnp.broadcast_to(w_piece[None], (NEAR,) + w_piece.shape), near)

    x_cols = lax.dynamic_slice_in_dim(hidden_rows, place[0] * feat, feat, 1)
    both = lax.dynamic_slice_in_dim(gain_final * w_head, place[0] * feat, feat, 0)[None]
    resid, stats = project(mixed_all, w_parts, x_cols, both)
    stats = lax.all_to_all(stats, "mp", 0, 0, tiled=True)
    reward, stats = lax.optimization_barrier((reward_of(lengths, stats, width, n_dp), stats))
    costs = -lax.all_to_all(reward, "dp", 0, 0, tiled=True)
    costs = jnp.maximum(lax.optimization_barrier(costs), jnp.finfo(F32).min)
    costs = jnp.minimum(lax.optimization_barrier(costs), jnp.finfo(F32).max)

    half = width // NCORE
    piece = -(-(half + 16) // (NX * NZ * 8)) * 8
    half_ext = piece * NX * NZ
    send, keep = gradient_halves(place, stats, resid, both, mixed_all, half_ext, width)
    got = to_sibling(send)
    seqs = pair_order.shape[0]
    order = jnp.pad(pair_order, (0, LANES - seqs), constant_values=-1)[None]
    summed, margin, reward_row = weigh(place, costs, order, keep, got)
    loss = jnp.sum(jax.nn.softplus(-margin[0, :seqs:2]))

    got = swap(summed.reshape(NX, NZ * piece, feat), along_x)
    summed = jnp.sum(got.astype(F32), axis=0).astype(BF16)
    got = swap(summed.reshape(NZ, piece, feat), along_z)
    mine = jnp.sum(got.astype(F32), axis=0).astype(BF16)
    got = swap(jnp.broadcast_to(mine[None], (NZ, piece, feat)), along_z)
    got = swap(jnp.broadcast_to(got.reshape(1, NZ * piece, feat), (NX, NZ * piece, feat)), along_x)
    got = got.reshape(half_ext, feat)
    other = to_sibling(got)
    grad_out_proj, grad_head, grad_gain = finish(place, got, other, gain_final, w_head, half)
    return (loss, reward_row[0, :seqs], grad_out_proj, grad_head[0], grad_gain[0])


def solution(mesh):
    placed = (
        P("dp", None),
        P("dp"),
        P(),
        P(),
        P(None, "mp"),
        P(None, "mp"),
        P(None, "mp"),
        P("mp", None),
        P(),
        P(),
    )
    return jax.shard_map(
        body,
        mesh=mesh,
        in_specs=placed,
        out_specs=(P(), P(), P(None, "mp"), P("mp"), P("mp")),
        check_vma=False,
    )
```

```python
import functools

import jax
import jax.numpy as jnp
import numpy as np
from jax import lax
from jax.experimental import pallas as pl
from jax.experimental.pallas import tpu as pltpu
from jax.sharding import PartitionSpec as P

QUERY_HEADS = 32
KEY_VALUE_HEADS = 8
HEAD_SIZE = 64
NX, NZ, NCORE = 4, 12, 2

EPS = 1e-05
THETA = 500000.0
LANES = 128
F32 = jnp.float32
BF16 = jnp.bfloat16


def device_of(x, z, core):
    return (x * NZ + z) * NCORE + core


def dp_groups():
    along_x = [[device_of(x, z, c) for x in range(NX)] for z in range(NZ) for c in range(NCORE)]
    along_z = [[device_of(x, z, c) for z in range(NZ)] for x in range(NX) for c in range(NCORE)]
    return along_x, along_z


def swap(parts, groups):
    return lax.all_to_all(parts, "dp", 0, 0, tiled=True, axis_index_groups=groups)


def to_sibling(x):
    pairs = [(i, i ^ 1) for i in range(NX * NZ * NCORE)]
    return lax.ppermute(x, "dp", pairs)


def dot(a, b, a_dim, b_dim, precision=None):
    return lax.dot_general(
        a, b, (((a_dim,), (b_dim,)), ((), ())), preferred_element_type=F32, precision=precision
    )


def front_kernel(lens, x_hbm, gain_ref, wq_hbm, wk_hbm, wv_hbm, freq_ref, out_ref, x_ref, wq_ref, wk_ref, wv_ref, k_ref, v_ref, sems):
    total_rows = x_ref.shape[0]
    blocks = 2
    rows = total_rows // blocks
    copies = [
        pltpu.make_async_copy(x_hbm.at[pl.ds(0, rows)], x_ref.at[pl.ds(0, rows)], sems.at[0]),
        pltpu.make_async_copy(wq_hbm, wq_ref, sems.at[1]),
        pltpu.make_async_copy(wk_hbm, wk_ref, sems.at[2]),
        pltpu.make_async_copy(wv_hbm, wv_ref, sems.at[3]),
        pltpu.make_async_copy(x_hbm.at[pl.ds(rows, rows)], x_ref.at[pl.ds(rows, rows)], sems.at[4]),
    ]
    for copy in copies:
        copy.start()
    used = lens[0]
    lane = lax.broadcasted_iota(jnp.int32, (rows, LANES), 1)
    first_half = (lane % HEAD_SIZE) < HEAD_SIZE // 2
    low = lane < HEAD_SIZE
    gain = gain_ref[...]

    def tables(first):
        row = first + lax.broadcasted_iota(jnp.int32, (rows, LANES), 0)
        position = row - jnp.where(row >= used, used, 0)
        angle = position.astype(F32) * freq_ref[...]
        sine = jnp.sin(angle)
        return jnp.cos(angle), jnp.where(first_half, -sine, sine)

    turns = [tables(i * rows) for i in range(blocks)]

    def rotate(t, turn):
        partner = jnp.where(
            first_half, pltpu.roll(t, LANES - HEAD_SIZE // 2, 1), pltpu.roll(t, HEAD_SIZE // 2, 1)
        )
        return t * turn[0] + partner * turn[1]

    def norm(i):
        x = x_ref[i * rows : (i + 1) * rows, :].astype(F32)
        return (x * lax.rsqrt(jnp.mean(x * x, axis=1, keepdims=True) + EPS) * gain).astype(BF16)

    def attend(query, first, cols):
        row = first + lax.broadcasted_iota(jnp.int32, (rows, cols), 0)
        col = lax.broadcasted_iota(jnp.int32, (rows, cols), 1)
        allowed = (col <= row) & ((row >= used) == (col >= used))
        for p in range(len(query)):
            total = jnp.zeros((rows, LANES), F32)
            for e in range(LANES // HEAD_SIZE):
                scores = dot(query[p], k_ref[e, :cols, :], 1, 1) * HEAD_SIZE ** (-0.5)
                scores = jnp.where(allowed, scores, -1e30)
                top = jnp.max(scores, axis=1, keepdims=True)
                weights = jnp.exp(scores - top)
                probs = weights * (1.0 / jnp.sum(weights, axis=1, keepdims=True))
                total = total + dot(probs.astype(BF16), v_ref[e, :cols, :], 1, 0)
            out_ref[first : first + rows, p * LANES : (p + 1) * LANES] = total.astype(BF16)

    copies[0].wait()
    for i in range(blocks):
        if i == 1:
            copies[4].wait()
        normed = norm(i)
        if i == 0:
            for copy in copies[1:4]:
                copy.wait()
        query = dot(normed, wq_ref[...], 1, 0)
        key = dot(normed, wk_ref[...], 1, 1)
        value = dot(normed, wv_ref[...], 1, 1)
        key = rotate(jnp.concatenate([key, key], axis=1), turns[i])
        value = jnp.concatenate([value, value], axis=1)
        here = slice(i * rows, (i + 1) * rows)
        k_ref[0, here, :] = jnp.where(low, key, 0.0).astype(BF16)
        k_ref[1, here, :] = jnp.where(low, 0.0, key).astype(BF16)
        v_ref[0, here, :] = jnp.where(low, value, 0.0).astype(BF16)
        v_ref[1, here, :] = jnp.where(low, 0.0, value).astype(BF16)
        turned = [
            rotate(query[:, p * LANES : (p + 1) * LANES], turns[i]).astype(BF16)
            for p in range(query.shape[1] // LANES)
        ]
        attend(turned, i * rows, (i + 1) * rows)


def front(hidden_rows, lengths, gain_attn, w_query, key_weight, value_weight):
    rows, width = hidden_rows.shape
    key_weight, value_weight = key_weight.T, value_weight.T
    gain = gain_attn[None]
    half = HEAD_SIZE // 2
    freq = np.tile(THETA ** (-np.arange(half) * 2.0 / HEAD_SIZE), LANES // half).astype(np.float32)[None]
    whole = lambda a: pl.BlockSpec(a.shape, lambda i, s: (0, 0))
    far = pl.BlockSpec(memory_space=pl.ANY)
    return pl.pallas_call(
        front_kernel,
        out_shape=jax.ShapeDtypeStruct((rows, w_query.shape[1]), BF16),
        grid_spec=pltpu.PrefetchScalarGridSpec(
            num_scalar_prefetch=1,
            grid=(1,),
            in_specs=[far, whole(gain), far, far, far, whole(freq)],
            out_specs=pl.BlockSpec((rows, w_query.shape[1]), lambda i, s: (0, 0)),
            scratch_shapes=[
                pltpu.VMEM(hidden_rows.shape, BF16),
                pltpu.VMEM(w_query.shape, BF16),
                pltpu.VMEM(key_weight.shape, BF16),
                pltpu.VMEM(value_weight.shape, BF16),
                pltpu.VMEM((2, rows, LANES), BF16),
                pltpu.VMEM((2, rows, LANES), BF16),
                pltpu.SemaphoreType.DMA((5,)),
            ],
        ),
        compiler_params=pltpu.CompilerParams(vmem_limit_bytes=58 * 2**20),
        cost_estimate=pl.CostEstimate(flops=1500000000, bytes_accessed=4000000, transcendentals=900000),
        name="front",
    )(lengths, hidden_rows, gain, w_query, key_weight, value_weight, jnp.asarray(freq))


def ring(x):
    n = lax.axis_size("mp")
    up = [(i, (i + 1) % n) for i in range(n)]
    down = [(i, (i - 1) % n) for i in range(n)]
    parts, below, above = [(0, x)], x, x
    for step in range(1, n // 2):
        below, above = lax.ppermute(below, "mp", up), lax.ppermute(above, "mp", down)
        parts += [(-step, below), (step, above)]
    half = x.shape[0] // 2
    first = lax.ppermute(below[:half], "mp", up)
    second = lax.ppermute(above[half:], "mp", down)
    return parts + [(n // 2, (first, second))]


def flatten(parts):
    return [p for _, part in parts for p in (part if isinstance(part, tuple) else (part,))]


def shard_of(refs, i):
    if i < len(refs) - 2:
        return refs[i][...]
    return jnp.concatenate([refs[-2][...], refs[-1][...]], axis=0)


def cut_kernel(place, w_hbm, out_ref, sems):
    parts, rows, cols = out_ref.shape
    mine = pl.ds(pl.multiple_of(place[1] * rows, rows), rows)
    copies = [
        pltpu.make_async_copy(w_hbm.at[mine, pl.ds(g * cols, cols)], out_ref.at[g], sems.at[g])
        for g in range(parts)
    ]
    for copy in copies:
        copy.start()
    for copy in copies:
        copy.wait()


def cut(place, w_out, n_mp):
    shape = (n_mp, w_out.shape[0] // NCORE, w_out.shape[1] // n_mp)
    return pl.pallas_call(
        cut_kernel,
        out_shape=jax.ShapeDtypeStruct(shape, BF16),
        in_specs=[pl.BlockSpec(memory_space=pltpu.SMEM), pl.BlockSpec(memory_space=pl.ANY)],
        out_specs=pl.BlockSpec(memory_space=pltpu.VMEM),
        scratch_shapes=[pltpu.SemaphoreType.DMA((n_mp,))],
        compiler_params=pltpu.CompilerParams(vmem_limit_bytes=58 * 2**20),
        cost_estimate=pl.CostEstimate(flops=0, bytes_accessed=1000000, transcendentals=0),
        name="cut",
    )(place, w_out)


def project_kernel(distances, place, *refs):
    count = len(distances) + 1
    shards = refs[:count]
    mine_ref, other_ref, x_ref, both_ref, resid_ref, stats_ref, w_ref = refs[count:]
    groups, half, feat = mine_ref.shape
    core = place[1]
    w_ref[:, pl.ds(pl.multiple_of(core * half, half), half), :] = mine_ref[...]
    w_ref[:, pl.ds(pl.multiple_of((1 - core) * half, half), half), :] = other_ref[...]
    resid = x_ref[...].astype(F32)
    for i, distance in enumerate(distances):
        group = lax.rem(place[0] + (distance + groups), groups)
        resid = resid + dot(shard_of(shards, i), w_ref[group], 1, 0).astype(BF16).astype(F32)
    resid_ref[...] = resid
    squares = dot(jnp.ones((8, feat), F32), resid * resid, 1, 1, lax.Precision.HIGHEST)
    scores = dot(jnp.broadcast_to(both_ref[...], (8, feat)), resid, 1, 1, lax.Precision.HIGHEST)
    pair = jnp.concatenate([squares[:1], scores[:1]], axis=0)
    stats_ref[...] = jnp.broadcast_to(pair[None], stats_ref.shape)


def project(place, parts, w_mine, w_other, x_cols, both):
    n_mp, half, feat = w_mine.shape
    rows = x_cols.shape[0]
    shards = flatten(parts)
    here = pl.BlockSpec(memory_space=pltpu.VMEM)
    return pl.pallas_call(
        functools.partial(project_kernel, [d for d, _ in parts]),
        out_shape=(
            jax.ShapeDtypeStruct((rows, feat), F32),
            jax.ShapeDtypeStruct((n_mp, 2, rows), F32),
        ),
        in_specs=[pl.BlockSpec(memory_space=pltpu.SMEM)] + [here] * (len(shards) + 4),
        out_specs=(here, here),
        scratch_shapes=[pltpu.VMEM((n_mp, NCORE * half, feat), BF16)],
        compiler_params=pltpu.CompilerParams(vmem_limit_bytes=32 * 2**20),
        cost_estimate=pl.CostEstimate(flops=550000000, bytes_accessed=4000000, transcendentals=0),
        name="project",
    )(place, *shards, w_mine, w_other, x_cols, both)


def row_terms(stats, used, width):
    sums = stats[0]
    for part in range(1, stats.shape[0]):
        sums = sums + stats[part]
    scale = lax.rsqrt(sums[:1] / width + EPS)
    score = sums[1:2] * scale
    row = lax.broadcasted_iota(jnp.int32, scale.shape, 1)
    inside = row < used
    return scale, score, inside


def reward_kernel(width, lens, stats_ref, out_ref):
    _, score, inside = row_terms(stats_ref, lens[0], width)
    total = jnp.sum(jnp.where(inside, score, 0.0), axis=1, keepdims=True)
    reward = total / lens[0].astype(F32)
    out_ref[...] = jnp.broadcast_to(reward[None], out_ref.shape)


def reward_of(lengths, stats, width, n_dp):
    return pl.pallas_call(
        functools.partial(reward_kernel, width),
        out_shape=jax.ShapeDtypeStruct((n_dp, 1, LANES), F32),
        grid_spec=pltpu.PrefetchScalarGridSpec(
            num_scalar_prefetch=1,
            grid=(1,),
            in_specs=[pl.BlockSpec(stats.shape, lambda i, s: (0, 0, 0))],
            out_specs=pl.BlockSpec((n_dp, 1, LANES), lambda i, s: (0, 0, 0)),
        ),
        compiler_params=pltpu.CompilerParams(vmem_limit_bytes=16 * 2**20),
        cost_estimate=pl.CostEstimate(flops=10000, bytes_accessed=90000, transcendentals=512),
        name="reward",
    )(lengths, stats)


def gradient_kernel(width, distances, place, stats_ref, resid_ref, both_ref, *refs):
    count = len(distances) + 1
    shards = refs[:count]
    send_ref, keep_ref, d_ref = refs[count:]
    rows, feat = resid_ref.shape
    heads = shards[0].shape[1]
    groups = width // heads
    used = place[2]
    scale, score, inside = row_terms(stats_ref, used, width)
    weight = jnp.where(inside, scale, 0.0) / used.astype(F32)
    minus = weight * scale * score * (1.0 / width)
    plus = jnp.broadcast_to(weight, (LANES, rows)).T
    minus = jnp.broadcast_to(minus, (LANES, rows)).T
    both = both_ref[...]
    pooled = []
    for part in range(feat // LANES):
        at = slice(part * LANES, (part + 1) * LANES)
        resid = resid_ref[:, at]
        d_ref[:, at] = (plus * both[:, at] - minus * resid).astype(BF16)
        pooled.append(jnp.sum(plus * resid, axis=0, keepdims=True))
    pooled = jnp.concatenate(pooled, axis=1)
    half = width // NCORE
    extra = send_ref.shape[0] - half
    first = lax.broadcasted_iota(jnp.int32, (extra, feat), 0) == 0
    pooled = jnp.where(first, pooled, 0.0).astype(BF16)
    send_ref[half:, :] = pooled
    keep_ref[half:, :] = pooled
    for i, distance in enumerate(distances):
        group = lax.rem(place[0] + (distance + groups), groups)
        at = pl.ds(pl.multiple_of(lax.rem(group, groups // NCORE) * heads, heads), heads)
        block = dot(shard_of(shards, i), d_ref[...], 0, 0).astype(BF16)
        stays = lax.div(group, groups // NCORE) == place[1]

        @pl.when(stays)
        def _(block=block, at=at):
            keep_ref[at, :] = block

        @pl.when(jnp.logical_not(stays))
        def _(block=block, at=at):
            send_ref[at, :] = block


def gradient_halves(place, stats, resid, both, parts, half_ext, width):
    rows, feat = resid.shape
    shards = flatten(parts)
    here = pl.BlockSpec(memory_space=pltpu.VMEM)
    half = jax.ShapeDtypeStruct((half_ext, feat), BF16)
    return pl.pallas_call(
        functools.partial(gradient_kernel, width, [d for d, _ in parts]),
        out_shape=(half, half),
        in_specs=[pl.BlockSpec(memory_space=pltpu.SMEM)] + [here] * (len(shards) + 3),
        out_specs=(here, here),
        scratch_shapes=[pltpu.VMEM((rows, feat), BF16)],
        compiler_params=pltpu.CompilerParams(vmem_limit_bytes=32 * 2**20),
        cost_estimate=pl.CostEstimate(flops=550000000, bytes_accessed=4000000, transcendentals=0),
        name="gradient",
    )(place, stats, resid, both, *shards)


def weigh_kernel(place, costs_ref, order_ref, keep_ref, got_ref, out_ref, margin_ref, row_ref):
    seqs = costs_ref.shape[0]
    rewards = -costs_ref[...].reshape(seqs, LANES)
    order = order_ref[...]
    seq = lax.broadcasted_iota(jnp.int32, (seqs, LANES), 0)
    picked = jnp.sum(jnp.where(seq == order, rewards, 0.0), axis=0, keepdims=True)
    lane = lax.broadcasted_iota(jnp.int32, (1, LANES), 1)
    chosen = lane % 2 == 0
    partner = jnp.where(chosen, pltpu.roll(picked, LANES - 1, 1), pltpu.roll(picked, 1, 1))
    margin = jnp.where(chosen, picked - partner, partner - picked)
    sig = 1.0 / (1.0 + jnp.exp(margin))
    dreward = jnp.where(chosen, -sig, sig)
    me = place[3]
    own = jnp.sum(jnp.where(order == me, dreward, 0.0), axis=1, keepdims=True)
    sib = jnp.sum(jnp.where(order == (me ^ 1), dreward, 0.0), axis=1, keepdims=True)
    out_ref[...] = (keep_ref[...].astype(F32) * own + got_ref[...].astype(F32) * sib).astype(BF16)
    margin_ref[...] = margin
    at = lax.broadcasted_iota(jnp.int32, (seqs, LANES), 1)
    row_ref[...] = jnp.sum(jnp.where(seq == at, rewards, 0.0), axis=0, keepdims=True)


def weigh(place, costs, order, keep, got):
    flat = lambda a: pl.BlockSpec(a.shape, lambda i, s: (0,) * len(a.shape))
    return pl.pallas_call(
        weigh_kernel,
        out_shape=(
            jax.ShapeDtypeStruct(keep.shape, BF16),
            jax.ShapeDtypeStruct((1, LANES), F32),
            jax.ShapeDtypeStruct((1, LANES), F32),
        ),
        grid_spec=pltpu.PrefetchScalarGridSpec(
            num_scalar_prefetch=1,
            grid=(1,),
            in_specs=[flat(costs), flat(order), flat(keep), flat(got)],
            out_specs=(flat(keep),) + (pl.BlockSpec((1, LANES), lambda i, s: (0, 0)),) * 2,
        ),
        compiler_params=pltpu.CompilerParams(vmem_limit_bytes=16 * 2**20),
        cost_estimate=pl.CostEstimate(flops=1000000, bytes_accessed=2000000, transcendentals=128),
        name="weigh",
    )(place, costs, order, keep, got)


def finish_kernel(half, place, mine_ref, other_ref, gain_ref, head_ref, grad_ref, ghead_ref, ggain_ref):
    step = pl.program_id(0)

    @pl.when(step == place[1])
    def _():
        grad_ref[...] = mine_ref[:half, :].astype(F32)

    @pl.when(step != place[1])
    def _():
        grad_ref[...] = other_ref[:half, :].astype(F32)

    pooled = mine_ref[half : half + 16, :].astype(F32)[:1]
    ghead_ref[...] = gain_ref[...] * pooled
    ggain_ref[...] = head_ref[...] * pooled


def finish(place, mine, other, gain_final, w_head, half):
    feat = mine.shape[1]
    flat = pl.BlockSpec(mine.shape, lambda i, s: (0, 0))
    share = pl.BlockSpec((1, feat), lambda i, s: (0, s[0]))
    line = pl.BlockSpec((1, feat), lambda i, s: (0, 0))
    return pl.pallas_call(
        functools.partial(finish_kernel, half),
        out_shape=(
            jax.ShapeDtypeStruct((NCORE * half, feat), F32),
            jax.ShapeDtypeStruct((1, feat), F32),
            jax.ShapeDtypeStruct((1, feat), F32),
        ),
        grid_spec=pltpu.PrefetchScalarGridSpec(
            num_scalar_prefetch=1,
            grid=(NCORE,),
            in_specs=[flat, flat, share, share],
            out_specs=(pl.BlockSpec((half, feat), lambda i, s: (i, 0)), line, line),
        ),
        compiler_params=pltpu.CompilerParams(vmem_limit_bytes=16 * 2**20),
        cost_estimate=pl.CostEstimate(flops=1000000, bytes_accessed=4000000, transcendentals=0),
        name="finish",
    )(place, mine, other, gain_final[None], w_head[None])


def body(
    hidden_rows,
    lengths,
    pair_order,
    gain_attn,
    w_query,
    key_weight,
    value_weight,
    w_out,
    gain_final,
    w_head,
):
    rows, width = hidden_rows.shape
    n_mp = lax.axis_size("mp")
    n_dp = lax.axis_size("dp")
    feat = width // n_mp
    me = lax.axis_index("dp").astype(jnp.int32)
    core = me % NCORE
    along_x, along_z = dp_groups()
    place = jnp.stack([lax.axis_index("mp").astype(jnp.int32), core, lengths[0], me])

    w_mine = lax.all_to_all(cut(place, w_out, n_mp), "mp", 0, 0, tiled=True)
    mixed = front(hidden_rows, lengths, gain_attn, w_query, key_weight, value_weight)
    mixed, w_mine, hidden_rows, gain_final, w_head = lax.optimization_barrier(
        (mixed, w_mine, hidden_rows, gain_final, w_head)
    )
    w_other = to_sibling(w_mine)

    parts = ring(mixed)
    x_cols = lax.dynamic_slice_in_dim(hidden_rows, place[0] * feat, feat, 1)
    both = lax.dynamic_slice_in_dim(gain_final * w_head, place[0] * feat, feat, 0)[None]
    resid, stats = project(place, parts, w_mine, w_other, x_cols, both)
    stats = lax.all_to_all(stats, "mp", 0, 0, tiled=True)
    reward, stats = lax.optimization_barrier((reward_of(lengths, stats, width, n_dp), stats))
    costs = -lax.all_to_all(reward, "dp", 0, 0, tiled=True)
    costs = jnp.maximum(lax.optimization_barrier(costs), jnp.finfo(F32).min)
    costs = jnp.minimum(lax.optimization_barrier(costs), jnp.finfo(F32).max)

    half = width // NCORE
    piece = -(-(half + 16) // (NX * NZ * 8)) * 8
    half_ext = piece * NX * NZ
    send, keep = gradient_halves(place, stats, resid, both, parts, half_ext, width)
    got = to_sibling(send)
    seqs = pair_order.shape[0]
    order = jnp.pad(pair_order, (0, LANES - seqs), constant_values=-1)[None]
    summed, margin, reward_row = weigh(place, costs, order, keep, got)
    loss = jnp.sum(jax.nn.softplus(-margin[0, :seqs:2]))

    got = swap(summed.reshape(NX, NZ * piece, feat), along_x)
    summed = jnp.sum(got.astype(F32), axis=0).astype(BF16)
    got = swap(summed.reshape(NZ, piece, feat), along_z)
    mine = jnp.sum(got.astype(F32), axis=0).astype(BF16)
    got = swap(jnp.broadcast_to(mine[None], (NZ, piece, feat)), along_z)
    got = swap(jnp.broadcast_to(got.reshape(1, NZ * piece, feat), (NX, NZ * piece, feat)), along_x)
    got = got.reshape(half_ext, feat)
    other = to_sibling(got)
    grad_out_proj, grad_head, grad_gain = finish(place, got, other, gain_final, w_head, half)
    return (loss, reward_row[0, :seqs], grad_out_proj, grad_head[0], grad_gain[0])


def solution(mesh):
    placed = (
        P("dp", None),
        P("dp"),
        P(),
        P(),
        P(None, "mp"),
        P(None, "mp"),
        P(None, "mp"),
        P("mp", None),
        P(),
        P(),
    )
    return jax.shard_map(
        body,
        mesh=mesh,
        in_specs=placed,
        out_specs=(P(), P(), P(None, "mp"), P("mp"), P("mp")),
        check_vma=False,
    )
```

```python
import functools

import jax
import jax.numpy as jnp
import numpy as np
from jax import lax
from jax.experimental import pallas as pl
from jax.experimental.pallas import tpu as pltpu
from jax.sharding import PartitionSpec as P

QUERY_HEADS = 32
KEY_VALUE_HEADS = 8
HEAD_SIZE = 64
NX, NZ, NCORE = 4, 12, 2
NEAR = NX * NCORE

EPS = 1e-05
THETA = 500000.0
LANES = 128
F32 = jnp.float32
BF16 = jnp.bfloat16


def device_of(x, z, core):
    return (x * NZ + z) * NCORE + core


def dp_groups():
    along_x = [[device_of(x, z, c) for x in range(NX)] for z in range(NZ) for c in range(NCORE)]
    along_z = [[device_of(x, z, c) for z in range(NZ)] for x in range(NX) for c in range(NCORE)]
    near = [[device_of(x, z, c) for x in range(NX) for c in range(NCORE)] for z in range(NZ)]
    return along_x, along_z, near


def swap(parts, groups):
    return lax.all_to_all(parts, "dp", 0, 0, tiled=True, axis_index_groups=groups)


def to_sibling(x):
    pairs = [(i, i ^ 1) for i in range(NX * NZ * NCORE)]
    return lax.ppermute(x, "dp", pairs)


def dot(a, b, a_dim, b_dim, precision=None):
    return lax.dot_general(
        a, b, (((a_dim,), (b_dim,)), ((), ())), preferred_element_type=F32, precision=precision
    )


def front_kernel(lens, x_hbm, gain_ref, wq_hbm, wk_hbm, wv_hbm, freq_ref, out_ref, x_ref, wq_ref, wk_ref, wv_ref, k_ref, v_ref, sems):
    total_rows = x_ref.shape[0]
    blocks = 2
    rows = total_rows // blocks
    copies = [
        pltpu.make_async_copy(x_hbm.at[pl.ds(0, rows)], x_ref.at[pl.ds(0, rows)], sems.at[0]),
        pltpu.make_async_copy(wq_hbm, wq_ref, sems.at[1]),
        pltpu.make_async_copy(wk_hbm, wk_ref, sems.at[2]),
        pltpu.make_async_copy(wv_hbm, wv_ref, sems.at[3]),
        pltpu.make_async_copy(x_hbm.at[pl.ds(rows, rows)], x_ref.at[pl.ds(rows, rows)], sems.at[4]),
    ]
    for copy in copies:
        copy.start()
    used = lens[0]
    lane = lax.broadcasted_iota(jnp.int32, (rows, LANES), 1)
    first_half = (lane % HEAD_SIZE) < HEAD_SIZE // 2
    low = lane < HEAD_SIZE
    gain = gain_ref[...]

    def tables(first):
        row = first + lax.broadcasted_iota(jnp.int32, (rows, LANES), 0)
        position = row - jnp.where(row >= used, used, 0)
        angle = position.astype(F32) * freq_ref[...]
        sine = jnp.sin(angle)
        return jnp.cos(angle), jnp.where(first_half, -sine, sine)

    turns = [tables(i * rows) for i in range(blocks)]

    def rotate(t, turn):
        partner = jnp.where(
            first_half, pltpu.roll(t, LANES - HEAD_SIZE // 2, 1), pltpu.roll(t, HEAD_SIZE // 2, 1)
        )
        return t * turn[0] + partner * turn[1]

    def norm(i):
        x = x_ref[i * rows : (i + 1) * rows, :].astype(F32)
        return (x * lax.rsqrt(jnp.mean(x * x, axis=1, keepdims=True) + EPS) * gain).astype(BF16)

    def attend(query, first, cols):
        row = first + lax.broadcasted_iota(jnp.int32, (rows, cols), 0)
        col = lax.broadcasted_iota(jnp.int32, (rows, cols), 1)
        allowed = (col <= row) & ((row >= used) == (col >= used))
        for p in range(len(query)):
            total = jnp.zeros((rows, LANES), F32)
            for e in range(LANES // HEAD_SIZE):
                scores = dot(query[p], k_ref[e, :cols, :], 1, 1) * HEAD_SIZE ** (-0.5)
                scores = jnp.where(allowed, scores, -1e30)
                top = jnp.max(scores, axis=1, keepdims=True)
                weights = jnp.exp(scores - top)
                probs = weights * (1.0 / jnp.sum(weights, axis=1, keepdims=True))
                total = total + dot(probs.astype(BF16), v_ref[e, :cols, :], 1, 0)
            out_ref[first : first + rows, p * LANES : (p + 1) * LANES] = total.astype(BF16)

    copies[0].wait()
    for i in range(blocks):
        if i == 1:
            copies[4].wait()
        normed = norm(i)
        if i == 0:
            for copy in copies[1:4]:
                copy.wait()
        query = dot(normed, wq_ref[...], 1, 0)
        key = dot(normed, wk_ref[...], 1, 1)
        value = dot(normed, wv_ref[...], 1, 1)
        key = rotate(jnp.concatenate([key, key], axis=1), turns[i])
        value = jnp.concatenate([value, value], axis=1)
        here = slice(i * rows, (i + 1) * rows)
        k_ref[0, here, :] = jnp.where(low, key, 0.0).astype(BF16)
        k_ref[1, here, :] = jnp.where(low, 0.0, key).astype(BF16)
        v_ref[0, here, :] = jnp.where(low, value, 0.0).astype(BF16)
        v_ref[1, here, :] = jnp.where(low, 0.0, value).astype(BF16)
        turned = [
            rotate(query[:, p * LANES : (p + 1) * LANES], turns[i]).astype(BF16)
            for p in range(query.shape[1] // LANES)
        ]
        attend(turned, i * rows, (i + 1) * rows)


def front(hidden_rows, lengths, gain_attn, w_query, key_weight, value_weight):
    rows, width = hidden_rows.shape
    key_weight, value_weight = key_weight.T, value_weight.T
    gain = gain_attn[None]
    half = HEAD_SIZE // 2
    freq = np.tile(THETA ** (-np.arange(half) * 2.0 / HEAD_SIZE), LANES // half).astype(np.float32)[None]
    whole = lambda a: pl.BlockSpec(a.shape, lambda i, s: (0, 0))
    far = pl.BlockSpec(memory_space=pl.ANY)
    return pl.pallas_call(
        front_kernel,
        out_shape=jax.ShapeDtypeStruct((rows, w_query.shape[1]), BF16),
        grid_spec=pltpu.PrefetchScalarGridSpec(
            num_scalar_prefetch=1,
            grid=(1,),
            in_specs=[far, whole(gain), far, far, far, whole(freq)],
            out_specs=pl.BlockSpec((rows, w_query.shape[1]), lambda i, s: (0, 0)),
            scratch_shapes=[
                pltpu.VMEM(hidden_rows.shape, BF16),
                pltpu.VMEM(w_query.shape, BF16),
                pltpu.VMEM(key_weight.shape, BF16),
                pltpu.VMEM(value_weight.shape, BF16),
                pltpu.VMEM((2, rows, LANES), BF16),
                pltpu.VMEM((2, rows, LANES), BF16),
                pltpu.SemaphoreType.DMA((5,)),
            ],
        ),
        compiler_params=pltpu.CompilerParams(vmem_limit_bytes=58 * 2**20),
        cost_estimate=pl.CostEstimate(flops=1500000000, bytes_accessed=4000000, transcendentals=900000),
        name="front",
    )(lengths, hidden_rows, gain, w_query, key_weight, value_weight, jnp.asarray(freq))


def ring(x):
    n = lax.axis_size("mp")
    up = [(i, (i + 1) % n) for i in range(n)]
    down = [(i, (i - 1) % n) for i in range(n)]
    parts, below, above = [(0, x)], x, x
    for step in range(1, n // 2):
        below, above = lax.ppermute(below, "mp", up), lax.ppermute(above, "mp", down)
        parts += [(-step, below), (step, above)]
    half = x.shape[0] // 2
    first = lax.ppermute(below[:half], "mp", up)
    second = lax.ppermute(above[half:], "mp", down)
    return parts + [(n // 2, (first, second))]


def flatten(parts):
    return [p for _, part in parts for p in (part if isinstance(part, tuple) else (part,))]


def shard_of(refs, i):
    if i < len(refs) - 2:
        return refs[i][...]
    return jnp.concatenate([refs[-2][...], refs[-1][...]], axis=0)


def project_kernel(distances, place, *refs):
    count = len(distances) + 1
    shards = refs[:count]
    w_ref, x_ref, both_ref, resid_ref, stats_ref = refs[count:]
    groups, feat = w_ref.shape[1], w_ref.shape[3]
    resid = x_ref[...].astype(F32)
    for i, distance in enumerate(distances):
        group = lax.rem(place[0] + (distance + groups), groups)
        weight = w_ref[:, pl.ds(group, 1)].reshape(-1, feat)
        resid = resid + dot(shard_of(shards, i), weight, 1, 0).astype(BF16).astype(F32)
    resid_ref[...] = resid
    squares = dot(jnp.ones((8, feat), F32), resid * resid, 1, 1, lax.Precision.HIGHEST)
    scores = dot(jnp.broadcast_to(both_ref[...], (8, feat)), resid, 1, 1, lax.Precision.HIGHEST)
    pair = jnp.concatenate([squares[:1], scores[:1]], axis=0)
    stats_ref[...] = jnp.broadcast_to(pair[None], stats_ref.shape)


def project(place, parts, w_parts, x_cols, both):
    n_mp, feat = w_parts.shape[1], w_parts.shape[3]
    rows = x_cols.shape[0]
    shards = flatten(parts)
    here = pl.BlockSpec(memory_space=pltpu.VMEM)
    return pl.pallas_call(
        functools.partial(project_kernel, [d for d, _ in parts]),
        out_shape=(
            jax.ShapeDtypeStruct((rows, feat), F32),
            jax.ShapeDtypeStruct((n_mp, 2, rows), F32),
        ),
        in_specs=[pl.BlockSpec(memory_space=pltpu.SMEM)] + [here] * (len(shards) + 3),
        out_specs=(here, here),
        compiler_params=pltpu.CompilerParams(vmem_limit_bytes=32 * 2**20),
        cost_estimate=pl.CostEstimate(flops=550000000, bytes_accessed=4000000, transcendentals=0),
        name="project",
    )(place, *shards, w_parts, x_cols, both)


def row_terms(stats, used, width):
    sums = stats[0]
    for part in range(1, stats.shape[0]):
        sums = sums + stats[part]
    scale = lax.rsqrt(sums[:1] / width + EPS)
    score = sums[1:2] * scale
    row = lax.broadcasted_iota(jnp.int32, scale.shape, 1)
    inside = row < used
    return scale, score, inside


def reward_kernel(width, lens, stats_ref, out_ref):
    _, score, inside = row_terms(stats_ref, lens[0], width)
    total = jnp.sum(jnp.where(inside, score, 0.0), axis=1, keepdims=True)
    reward = total / lens[0].astype(F32)
    out_ref[...] = jnp.broadcast_to(reward[None], out_ref.shape)


def reward_of(lengths, stats, width, n_dp):
    return pl.pallas_call(
        functools.partial(reward_kernel, width),
        out_shape=jax.ShapeDtypeStruct((n_dp, 1, LANES), F32),
        grid_spec=pltpu.PrefetchScalarGridSpec(
            num_scalar_prefetch=1,
            grid=(1,),
            in_specs=[pl.BlockSpec(stats.shape, lambda i, s: (0, 0, 0))],
            out_specs=pl.BlockSpec((n_dp, 1, LANES), lambda i, s: (0, 0, 0)),
        ),
        compiler_params=pltpu.CompilerParams(vmem_limit_bytes=16 * 2**20),
        cost_estimate=pl.CostEstimate(flops=10000, bytes_accessed=90000, transcendentals=512),
        name="reward",
    )(lengths, stats)


def gradient_kernel(width, distances, place, stats_ref, resid_ref, both_ref, *refs):
    count = len(distances) + 1
    shards = refs[:count]
    send_ref, keep_ref, d_ref = refs[count:]
    rows, feat = resid_ref.shape
    heads = shards[0].shape[1]
    groups = width // heads
    used = place[2]
    scale, score, inside = row_terms(stats_ref, used, width)
    weight = jnp.where(inside, scale, 0.0) / used.astype(F32)
    minus = weight * scale * score * (1.0 / width)
    plus = jnp.broadcast_to(weight, (LANES, rows)).T
    minus = jnp.broadcast_to(minus, (LANES, rows)).T
    both = both_ref[...]
    pooled = []
    for part in range(feat // LANES):
        at = slice(part * LANES, (part + 1) * LANES)
        resid = resid_ref[:, at]
        d_ref[:, at] = (plus * both[:, at] - minus * resid).astype(BF16)
        pooled.append(jnp.sum(plus * resid, axis=0, keepdims=True))
    pooled = jnp.concatenate(pooled, axis=1)
    half = width // NCORE
    extra = send_ref.shape[0] - half
    first = lax.broadcasted_iota(jnp.int32, (extra, feat), 0) == 0
    pooled = jnp.where(first, pooled, 0.0).astype(BF16)
    send_ref[half:, :] = pooled
    keep_ref[half:, :] = pooled
    for i, distance in enumerate(distances):
        group = lax.rem(place[0] + (distance + groups), groups)
        at = pl.ds(pl.multiple_of(lax.rem(group, groups // NCORE) * heads, heads), heads)
        block = dot(shard_of(shards, i), d_ref[...], 0, 0).astype(BF16)
        stays = lax.div(group, groups // NCORE) == place[1]

        @pl.when(stays)
        def _(block=block, at=at):
            keep_ref[at, :] = block

        @pl.when(jnp.logical_not(stays))
        def _(block=block, at=at):
            send_ref[at, :] = block


def gradient_halves(place, stats, resid, both, parts, half_ext, width):
    rows, feat = resid.shape
    shards = flatten(parts)
    here = pl.BlockSpec(memory_space=pltpu.VMEM)
    half = jax.ShapeDtypeStruct((half_ext, feat), BF16)
    return pl.pallas_call(
        functools.partial(gradient_kernel, width, [d for d, _ in parts]),
        out_shape=(half, half),
        in_specs=[pl.BlockSpec(memory_space=pltpu.SMEM)] + [here] * (len(shards) + 3),
        out_specs=(here, here),
        scratch_shapes=[pltpu.VMEM((rows, feat), BF16)],
        compiler_params=pltpu.CompilerParams(vmem_limit_bytes=32 * 2**20),
        cost_estimate=pl.CostEstimate(flops=550000000, bytes_accessed=4000000, transcendentals=0),
        name="gradient",
    )(place, stats, resid, both, *shards)


def weigh_kernel(place, costs_ref, order_ref, keep_ref, got_ref, out_ref, margin_ref, row_ref):
    seqs = costs_ref.shape[0]
    rewards = -costs_ref[...].reshape(seqs, LANES)
    order = order_ref[...]
    seq = lax.broadcasted_iota(jnp.int32, (seqs, LANES), 0)
    picked = jnp.sum(jnp.where(seq == order, rewards, 0.0), axis=0, keepdims=True)
    lane = lax.broadcasted_iota(jnp.int32, (1, LANES), 1)
    chosen = lane % 2 == 0
    partner = jnp.where(chosen, pltpu.roll(picked, LANES - 1, 1), pltpu.roll(picked, 1, 1))
    margin = jnp.where(chosen, picked - partner, partner - picked)
    sig = 1.0 / (1.0 + jnp.exp(margin))
    dreward = jnp.where(chosen, -sig, sig)
    me = place[3]
    own = jnp.sum(jnp.where(order == me, dreward, 0.0), axis=1, keepdims=True)
    sib = jnp.sum(jnp.where(order == (me ^ 1), dreward, 0.0), axis=1, keepdims=True)
    out_ref[...] = (keep_ref[...].astype(F32) * own + got_ref[...].astype(F32) * sib).astype(BF16)
    margin_ref[...] = margin
    at = lax.broadcasted_iota(jnp.int32, (seqs, LANES), 1)
    row_ref[...] = jnp.sum(jnp.where(seq == at, rewards, 0.0), axis=0, keepdims=True)


def weigh(place, costs, order, keep, got):
    flat = lambda a: pl.BlockSpec(a.shape, lambda i, s: (0,) * len(a.shape))
    return pl.pallas_call(
        weigh_kernel,
        out_shape=(
            jax.ShapeDtypeStruct(keep.shape, BF16),
            jax.ShapeDtypeStruct((1, LANES), F32),
            jax.ShapeDtypeStruct((1, LANES), F32),
        ),
        grid_spec=pltpu.PrefetchScalarGridSpec(
            num_scalar_prefetch=1,
            grid=(1,),
            in_specs=[flat(costs), flat(order), flat(keep), flat(got)],
            out_specs=(flat(keep),) + (pl.BlockSpec((1, LANES), lambda i, s: (0, 0)),) * 2,
        ),
        compiler_params=pltpu.CompilerParams(vmem_limit_bytes=16 * 2**20),
        cost_estimate=pl.CostEstimate(flops=1000000, bytes_accessed=2000000, transcendentals=128),
        name="weigh",
    )(place, costs, order, keep, got)


def finish_kernel(half, place, mine_ref, other_ref, gain_ref, head_ref, grad_ref, ghead_ref, ggain_ref):
    step = pl.program_id(0)

    @pl.when(step == place[1])
    def _():
        grad_ref[...] = mine_ref[:half, :].astype(F32)

    @pl.when(step != place[1])
    def _():
        grad_ref[...] = other_ref[:half, :].astype(F32)

    pooled = mine_ref[half : half + 16, :].astype(F32)[:1]
    ghead_ref[...] = gain_ref[...] * pooled
    ggain_ref[...] = head_ref[...] * pooled


def finish(place, mine, other, gain_final, w_head, half):
    feat = mine.shape[1]
    flat = pl.BlockSpec(mine.shape, lambda i, s: (0, 0))
    share = pl.BlockSpec((1, feat), lambda i, s: (0, s[0]))
    line = pl.BlockSpec((1, feat), lambda i, s: (0, 0))
    return pl.pallas_call(
        functools.partial(finish_kernel, half),
        out_shape=(
            jax.ShapeDtypeStruct((NCORE * half, feat), F32),
            jax.ShapeDtypeStruct((1, feat), F32),
            jax.ShapeDtypeStruct((1, feat), F32),
        ),
        grid_spec=pltpu.PrefetchScalarGridSpec(
            num_scalar_prefetch=1,
            grid=(NCORE,),
            in_specs=[flat, flat, share, share],
            out_specs=(pl.BlockSpec((half, feat), lambda i, s: (i, 0)), line, line),
        ),
        compiler_params=pltpu.CompilerParams(vmem_limit_bytes=16 * 2**20),
        cost_estimate=pl.CostEstimate(flops=1000000, bytes_accessed=4000000, transcendentals=0),
        name="finish",
    )(place, mine, other, gain_final[None], w_head[None])


def body(
    hidden_rows,
    lengths,
    pair_order,
    gain_attn,
    w_query,
    key_weight,
    value_weight,
    w_out,
    gain_final,
    w_head,
):
    rows, width = hidden_rows.shape
    n_mp = lax.axis_size("mp")
    n_dp = lax.axis_size("dp")
    feat = width // n_mp
    me = lax.axis_index("dp").astype(jnp.int32)
    core = me % NCORE
    along_x, along_z, near = dp_groups()
    place = jnp.stack([lax.axis_index("mp").astype(jnp.int32), core, lengths[0], me])

    mixed = front(hidden_rows, lengths, gain_attn, w_query, key_weight, value_weight)
    mixed, w_out, hidden_rows, gain_final, w_head = lax.optimization_barrier(
        (mixed, w_out, hidden_rows, gain_final, w_head)
    )
    piece_rows = w_out.shape[0] // NEAR
    my_near = (me // (NZ * NCORE)) * NCORE + core
    w_piece = lax.dynamic_slice_in_dim(w_out, my_near * piece_rows, piece_rows, 0)
    w_piece = w_piece.reshape(piece_rows, n_mp, feat).swapaxes(0, 1)
    w_piece = lax.all_to_all(w_piece, "mp", 0, 0, tiled=True)
    w_parts = swap(jnp.broadcast_to(w_piece[None], (NEAR,) + w_piece.shape), near)

    parts = ring(mixed)
    x_cols = lax.dynamic_slice_in_dim(hidden_rows, place[0] * feat, feat, 1)
    both = lax.dynamic_slice_in_dim(gain_final * w_head, place[0] * feat, feat, 0)[None]
    resid, stats = project(place, parts, w_parts, x_cols, both)
    stats = lax.all_to_all(stats, "mp", 0, 0, tiled=True)
    reward, stats = lax.optimization_barrier((reward_of(lengths, stats, width, n_dp), stats))
    costs = -lax.all_to_all(reward, "dp", 0, 0, tiled=True)
    costs = jnp.maximum(lax.optimization_barrier(costs), jnp.finfo(F32).min)
    costs = jnp.minimum(lax.optimization_barrier(costs), jnp.finfo(F32).max)

    half = width // NCORE
    piece = -(-(half + 16) // (NX * NZ * 8)) * 8
    half_ext = piece * NX * NZ
    send, keep = gradient_halves(place, stats, resid, both, parts, half_ext, width)
    got = to_sibling(send)
    seqs = pair_order.shape[0]
    order = jnp.pad(pair_order, (0, LANES - seqs), constant_values=-1)[None]
    summed, margin, reward_row = weigh(place, costs, order, keep, got)
    loss = jnp.sum(jax.nn.softplus(-margin[0, :seqs:2]))

    got = swap(summed.reshape(NX, NZ * piece, feat), along_x)
    summed = jnp.sum(got.astype(F32), axis=0).astype(BF16)
    got = swap(summed.reshape(NZ, piece, feat), along_z)
    mine = jnp.sum(got.astype(F32), axis=0).astype(BF16)
    got = swap(jnp.broadcast_to(mine[None], (NZ, piece, feat)), along_z)
    got = swap(jnp.broadcast_to(got.reshape(1, NZ * piece, feat), (NX, NZ * piece, feat)), along_x)
    got = got.reshape(half_ext, feat)
    other = to_sibling(got)
    grad_out_proj, grad_head, grad_gain = finish(place, got, other, gain_final, w_head, half)
    return (loss, reward_row[0, :seqs], grad_out_proj, grad_head[0], grad_gain[0])


def solution(mesh):
    placed = (
        P("dp", None),
        P("dp"),
        P(),
        P(),
        P(None, "mp"),
        P(None, "mp"),
        P(None, "mp"),
        P("mp", None),
        P(),
        P(),
    )
    return jax.shard_map(
        body,
        mesh=mesh,
        in_specs=placed,
        out_specs=(P(), P(), P(None, "mp"), P("mp"), P("mp")),
        check_vma=False,
    )
```

```python
import functools

import jax
import jax.numpy as jnp
import numpy as np
from jax import lax
from jax.experimental import pallas as pl
from jax.experimental.pallas import tpu as pltpu
from jax.sharding import PartitionSpec as P

QUERY_HEADS = 32
KEY_VALUE_HEADS = 8
HEAD_SIZE = 64
NX, NZ, NCORE = 4, 12, 2
NEAR = NX * NCORE

EPS = 1e-05
THETA = 500000.0
LANES = 128
F32 = jnp.float32
BF16 = jnp.bfloat16


def device_of(x, z, core):
    return (x * NZ + z) * NCORE + core


def dp_groups():
    along_x = [[device_of(x, z, c) for x in range(NX)] for z in range(NZ) for c in range(NCORE)]
    along_z = [[device_of(x, z, c) for z in range(NZ)] for x in range(NX) for c in range(NCORE)]
    return along_x, along_z


def swap(parts, groups):
    return lax.all_to_all(parts, "dp", 0, 0, tiled=True, axis_index_groups=groups)


def to_sibling(x):
    pairs = [(i, i ^ 1) for i in range(NX * NZ * NCORE)]
    return lax.ppermute(x, "dp", pairs)


def dot(a, b, a_dim, b_dim, precision=None):
    return lax.dot_general(
        a, b, (((a_dim,), (b_dim,)), ((), ())), preferred_element_type=F32, precision=precision
    )


def front_kernel(lens, x_hbm, gain_ref, wq_hbm, wk_hbm, wv_hbm, freq_ref, out_ref, x_ref, wq_ref, wk_ref, wv_ref, k_ref, v_ref, sems):
    total_rows = x_ref.shape[0]
    blocks = 2
    rows = total_rows // blocks
    copies = [
        pltpu.make_async_copy(x_hbm.at[pl.ds(0, rows)], x_ref.at[pl.ds(0, rows)], sems.at[0]),
        pltpu.make_async_copy(wq_hbm, wq_ref, sems.at[1]),
        pltpu.make_async_copy(wk_hbm, wk_ref, sems.at[2]),
        pltpu.make_async_copy(wv_hbm, wv_ref, sems.at[3]),
        pltpu.make_async_copy(x_hbm.at[pl.ds(rows, rows)], x_ref.at[pl.ds(rows, rows)], sems.at[4]),
    ]
    for copy in copies:
        copy.start()
    used = lens[0]
    lane = lax.broadcasted_iota(jnp.int32, (rows, LANES), 1)
    first_half = (lane % HEAD_SIZE) < HEAD_SIZE // 2
    low = lane < HEAD_SIZE
    gain = gain_ref[...]

    def tables(first):
        row = first + lax.broadcasted_iota(jnp.int32, (rows, LANES), 0)
        position = row - jnp.where(row >= used, used, 0)
        angle = position.astype(F32) * freq_ref[...]
        sine = jnp.sin(angle)
        return jnp.cos(angle), jnp.where(first_half, -sine, sine)

    turns = [tables(i * rows) for i in range(blocks)]

    def rotate(t, turn):
        partner = jnp.where(
            first_half, pltpu.roll(t, LANES - HEAD_SIZE // 2, 1), pltpu.roll(t, HEAD_SIZE // 2, 1)
        )
        return t * turn[0] + partner * turn[1]

    def norm(i):
        x = x_ref[i * rows : (i + 1) * rows, :].astype(F32)
        return (x * lax.rsqrt(jnp.mean(x * x, axis=1, keepdims=True) + EPS) * gain).astype(BF16)

    def attend(query, first, cols):
        row = first + lax.broadcasted_iota(jnp.int32, (rows, cols), 0)
        col = lax.broadcasted_iota(jnp.int32, (rows, cols), 1)
        allowed = (col <= row) & ((row >= used) == (col >= used))
        for p in range(len(query)):
            total = jnp.zeros((rows, LANES), F32)
            for e in range(LANES // HEAD_SIZE):
                scores = dot(query[p], k_ref[e, :cols, :], 1, 1) * HEAD_SIZE ** (-0.5)
                scores = jnp.where(allowed, scores, -1e30)
                top = jnp.max(scores, axis=1, keepdims=True)
                weights = jnp.exp(scores - top)
                probs = weights * (1.0 / jnp.sum(weights, axis=1, keepdims=True))
                total = total + dot(probs.astype(BF16), v_ref[e, :cols, :], 1, 0)
            out_ref[first : first + rows, p * LANES : (p + 1) * LANES] = total.astype(BF16)

    copies[0].wait()
    for i in range(blocks):
        if i == 1:
            copies[4].wait()
        normed = norm(i)
        if i == 0:
            for copy in copies[1:4]:
                copy.wait()
        query = dot(normed, wq_ref[...], 1, 0)
        key = dot(normed, wk_ref[...], 1, 1)
        value = dot(normed, wv_ref[...], 1, 1)
        key = rotate(jnp.concatenate([key, key], axis=1), turns[i])
        value = jnp.concatenate([value, value], axis=1)
        here = slice(i * rows, (i + 1) * rows)
        k_ref[0, here, :] = jnp.where(low, key, 0.0).astype(BF16)
        k_ref[1, here, :] = jnp.where(low, 0.0, key).astype(BF16)
        v_ref[0, here, :] = jnp.where(low, value, 0.0).astype(BF16)
        v_ref[1, here, :] = jnp.where(low, 0.0, value).astype(BF16)
        turned = [
            rotate(query[:, p * LANES : (p + 1) * LANES], turns[i]).astype(BF16)
            for p in range(query.shape[1] // LANES)
        ]
        attend(turned, i * rows, (i + 1) * rows)


def front(hidden_rows, lengths, gain_attn, w_query, key_weight, value_weight):
    rows, width = hidden_rows.shape
    key_weight, value_weight = key_weight.T, value_weight.T
    gain = gain_attn[None]
    half = HEAD_SIZE // 2
    freq = np.tile(THETA ** (-np.arange(half) * 2.0 / HEAD_SIZE), LANES // half).astype(np.float32)[None]
    whole = lambda a: pl.BlockSpec(a.shape, lambda i, s: (0, 0))
    far = pl.BlockSpec(memory_space=pl.ANY)
    return pl.pallas_call(
        front_kernel,
        out_shape=jax.ShapeDtypeStruct((rows, w_query.shape[1]), BF16),
        grid_spec=pltpu.PrefetchScalarGridSpec(
            num_scalar_prefetch=1,
            grid=(1,),
            in_specs=[far, whole(gain), far, far, far, whole(freq)],
            out_specs=pl.BlockSpec((rows, w_query.shape[1]), lambda i, s: (0, 0)),
            scratch_shapes=[
                pltpu.VMEM(hidden_rows.shape, BF16),
                pltpu.VMEM(w_query.shape, BF16),
                pltpu.VMEM(key_weight.shape, BF16),
                pltpu.VMEM(value_weight.shape, BF16),
                pltpu.VMEM((2, rows, LANES), BF16),
                pltpu.VMEM((2, rows, LANES), BF16),
                pltpu.SemaphoreType.DMA((5,)),
            ],
        ),
        compiler_params=pltpu.CompilerParams(vmem_limit_bytes=58 * 2**20),
        cost_estimate=pl.CostEstimate(flops=1500000000, bytes_accessed=4000000, transcendentals=900000),
        name="front",
    )(lengths, hidden_rows, gain, w_query, key_weight, value_weight, jnp.asarray(freq))


def ring(x):
    n = lax.axis_size("mp")
    up = [(i, (i + 1) % n) for i in range(n)]
    down = [(i, (i - 1) % n) for i in range(n)]
    parts, below, above = [(0, x)], x, x
    for step in range(1, n // 2):
        below, above = lax.ppermute(below, "mp", up), lax.ppermute(above, "mp", down)
        parts += [(-step, below), (step, above)]
    half = x.shape[0] // 2
    first = lax.ppermute(below[:half], "mp", up)
    second = lax.ppermute(above[half:], "mp", down)
    return parts + [(n // 2, (first, second))]


def flatten(parts):
    return [p for _, part in parts for p in (part if isinstance(part, tuple) else (part,))]


def shard_of(refs, i):
    if i < len(refs) - 2:
        return refs[i][...]
    return jnp.concatenate([refs[-2][...], refs[-1][...]], axis=0)


def project_kernel(distances, place, *refs):
    count = len(distances) + 1
    shards = refs[:count]
    mine_ref, other_ref, x_ref, both_ref, resid_ref, stats_ref, w_ref = refs[count:]
    groups, feat = mine_ref.shape[1], mine_ref.shape[3]
    for x in range(NX):
        for g in range(groups):
            w_ref[g, NCORE * x + place[1]] = mine_ref[x, g]
            w_ref[g, NCORE * x + 1 - place[1]] = other_ref[x, g]
    resid = x_ref[...].astype(F32)
    for i, distance in enumerate(distances):
        group = lax.rem(place[0] + (distance + groups), groups)
        weight = w_ref[group].reshape(-1, feat)
        resid = resid + dot(shard_of(shards, i), weight, 1, 0).astype(BF16).astype(F32)
    resid_ref[...] = resid
    squares = dot(jnp.ones((8, feat), F32), resid * resid, 1, 1, lax.Precision.HIGHEST)
    scores = dot(jnp.broadcast_to(both_ref[...], (8, feat)), resid, 1, 1, lax.Precision.HIGHEST)
    pair = jnp.concatenate([squares[:1], scores[:1]], axis=0)
    stats_ref[...] = jnp.broadcast_to(pair[None], stats_ref.shape)


def project(place, parts, w_mine, w_other, x_cols, both):
    _, n_mp, piece_rows, feat = w_mine.shape
    rows = x_cols.shape[0]
    shards = flatten(parts)
    here = pl.BlockSpec(memory_space=pltpu.VMEM)
    return pl.pallas_call(
        functools.partial(project_kernel, [d for d, _ in parts]),
        out_shape=(
            jax.ShapeDtypeStruct((rows, feat), F32),
            jax.ShapeDtypeStruct((n_mp, 2, rows), F32),
        ),
        in_specs=[pl.BlockSpec(memory_space=pltpu.SMEM)] + [here] * (len(shards) + 4),
        out_specs=(here, here),
        scratch_shapes=[pltpu.VMEM((n_mp, NEAR, piece_rows, feat), BF16)],
        compiler_params=pltpu.CompilerParams(vmem_limit_bytes=32 * 2**20),
        cost_estimate=pl.CostEstimate(flops=550000000, bytes_accessed=4000000, transcendentals=0),
        name="project",
    )(place, *shards, w_mine, w_other, x_cols, both)


def row_terms(stats, used, width):
    sums = stats[0]
    for part in range(1, stats.shape[0]):
        sums = sums + stats[part]
    scale = lax.rsqrt(sums[:1] / width + EPS)
    score = sums[1:2] * scale
    row = lax.broadcasted_iota(jnp.int32, scale.shape, 1)
    inside = row < used
    return scale, score, inside


def reward_kernel(width, lens, stats_ref, out_ref):
    _, score, inside = row_terms(stats_ref, lens[0], width)
    total = jnp.sum(jnp.where(inside, score, 0.0), axis=1, keepdims=True)
    reward = total / lens[0].astype(F32)
    out_ref[...] = jnp.broadcast_to(reward[None], out_ref.shape)


def reward_of(lengths, stats, width, n_dp):
    return pl.pallas_call(
        functools.partial(reward_kernel, width),
        out_shape=jax.ShapeDtypeStruct((n_dp, 1, LANES), F32),
        grid_spec=pltpu.PrefetchScalarGridSpec(
            num_scalar_prefetch=1,
            grid=(1,),
            in_specs=[pl.BlockSpec(stats.shape, lambda i, s: (0, 0, 0))],
            out_specs=pl.BlockSpec((n_dp, 1, LANES), lambda i, s: (0, 0, 0)),
        ),
        compiler_params=pltpu.CompilerParams(vmem_limit_bytes=16 * 2**20),
        cost_estimate=pl.CostEstimate(flops=10000, bytes_accessed=90000, transcendentals=512),
        name="reward",
    )(lengths, stats)


def gradient_kernel(width, distances, place, stats_ref, resid_ref, both_ref, *refs):
    count = len(distances) + 1
    shards = refs[:count]
    send_ref, keep_ref, d_ref, both_halves = refs[count:]
    rows, feat = resid_ref.shape
    heads = shards[0].shape[1]
    groups = width // heads
    used = place[2]
    scale, score, inside = row_terms(stats_ref, used, width)
    weight = jnp.where(inside, scale, 0.0) / used.astype(F32)
    minus = weight * scale * score * (1.0 / width)
    plus = jnp.broadcast_to(weight, (LANES, rows)).T
    minus = jnp.broadcast_to(minus, (LANES, rows)).T
    both = both_ref[...]
    pooled = []
    for part in range(feat // LANES):
        at = slice(part * LANES, (part + 1) * LANES)
        resid = resid_ref[:, at]
        d_ref[:, at] = (plus * both[:, at] - minus * resid).astype(BF16)
        pooled.append(jnp.sum(plus * resid, axis=0, keepdims=True))
    pooled = jnp.concatenate(pooled, axis=1)
    half = width // NCORE
    extra = send_ref.shape[0] - half
    first = lax.broadcasted_iota(jnp.int32, (extra, feat), 0) == 0
    pooled = jnp.where(first, pooled, 0.0).astype(BF16)
    send_ref[half:, :] = pooled
    keep_ref[half:, :] = pooled
    for i, distance in enumerate(distances):
        group = lax.rem(place[0] + (distance + groups), groups)
        stays = (lax.div(group, groups // NCORE) == place[1]).astype(jnp.int32)
        at = stays * half + lax.rem(group, groups // NCORE) * heads
        block = dot(shard_of(shards, i), d_ref[...], 0, 0).astype(BF16)
        both_halves[pl.ds(pl.multiple_of(at, heads), heads), :] = block
    send_ref[:half, :] = both_halves[:half, :]
    keep_ref[:half, :] = both_halves[half:, :]


def gradient_halves(place, stats, resid, both, parts, half_ext, width):
    rows, feat = resid.shape
    shards = flatten(parts)
    here = pl.BlockSpec(memory_space=pltpu.VMEM)
    half = jax.ShapeDtypeStruct((half_ext, feat), BF16)
    return pl.pallas_call(
        functools.partial(gradient_kernel, width, [d for d, _ in parts]),
        out_shape=(half, half),
        in_specs=[pl.BlockSpec(memory_space=pltpu.SMEM)] + [here] * (len(shards) + 3),
        out_specs=(here, here),
        scratch_shapes=[pltpu.VMEM((rows, feat), BF16), pltpu.VMEM((width, feat), BF16)],
        compiler_params=pltpu.CompilerParams(vmem_limit_bytes=32 * 2**20),
        cost_estimate=pl.CostEstimate(flops=550000000, bytes_accessed=4000000, transcendentals=0),
        name="gradient",
    )(place, stats, resid, both, *shards)


def weigh_kernel(place, costs_ref, order_ref, keep_ref, got_ref, out_ref, margin_ref, row_ref):
    seqs = costs_ref.shape[0]
    rewards = -costs_ref[...].reshape(seqs, LANES)
    order = order_ref[...]
    seq = lax.broadcasted_iota(jnp.int32, (seqs, LANES), 0)
    picked = jnp.sum(jnp.where(seq == order, rewards, 0.0), axis=0, keepdims=True)
    lane = lax.broadcasted_iota(jnp.int32, (1, LANES), 1)
    chosen = lane % 2 == 0
    partner = jnp.where(chosen, pltpu.roll(picked, LANES - 1, 1), pltpu.roll(picked, 1, 1))
    margin = jnp.where(chosen, picked - partner, partner - picked)
    sig = 1.0 / (1.0 + jnp.exp(margin))
    dreward = jnp.where(chosen, -sig, sig)
    me = place[3]
    own = jnp.sum(jnp.where(order == me, dreward, 0.0), axis=1, keepdims=True)
    sib = jnp.sum(jnp.where(order == (me ^ 1), dreward, 0.0), axis=1, keepdims=True)
    out_ref[...] = (keep_ref[...].astype(F32) * own + got_ref[...].astype(F32) * sib).astype(BF16)
    margin_ref[...] = margin
    at = lax.broadcasted_iota(jnp.int32, (seqs, LANES), 1)
    row_ref[...] = jnp.sum(jnp.where(seq == at, rewards, 0.0), axis=0, keepdims=True)


def weigh(place, costs, order, keep, got):
    flat = lambda a: pl.BlockSpec(a.shape, lambda i, s: (0,) * len(a.shape))
    return pl.pallas_call(
        weigh_kernel,
        out_shape=(
            jax.ShapeDtypeStruct(keep.shape, BF16),
            jax.ShapeDtypeStruct((1, LANES), F32),
            jax.ShapeDtypeStruct((1, LANES), F32),
        ),
        grid_spec=pltpu.PrefetchScalarGridSpec(
            num_scalar_prefetch=1,
            grid=(1,),
            in_specs=[flat(costs), flat(order), flat(keep), flat(got)],
            out_specs=(flat(keep),) + (pl.BlockSpec((1, LANES), lambda i, s: (0, 0)),) * 2,
        ),
        compiler_params=pltpu.CompilerParams(vmem_limit_bytes=16 * 2**20),
        cost_estimate=pl.CostEstimate(flops=1000000, bytes_accessed=2000000, transcendentals=128),
        name="weigh",
    )(place, costs, order, keep, got)


def finish_kernel(half, place, mine_ref, other_ref, gain_ref, head_ref, grad_ref, ghead_ref, ggain_ref):
    step = pl.program_id(0)

    @pl.when(step == place[1])
    def _():
        grad_ref[...] = mine_ref[:half, :].astype(F32)

    @pl.when(step != place[1])
    def _():
        grad_ref[...] = other_ref[:half, :].astype(F32)

    pooled = mine_ref[half : half + 16, :].astype(F32)[:1]
    ghead_ref[...] = gain_ref[...] * pooled
    ggain_ref[...] = head_ref[...] * pooled


def finish(place, mine, other, gain_final, w_head, half):
    feat = mine.shape[1]
    flat = pl.BlockSpec(mine.shape, lambda i, s: (0, 0))
    share = pl.BlockSpec((1, feat), lambda i, s: (0, s[0]))
    line = pl.BlockSpec((1, feat), lambda i, s: (0, 0))
    return pl.pallas_call(
        functools.partial(finish_kernel, half),
        out_shape=(
            jax.ShapeDtypeStruct((NCORE * half, feat), F32),
            jax.ShapeDtypeStruct((1, feat), F32),
            jax.ShapeDtypeStruct((1, feat), F32),
        ),
        grid_spec=pltpu.PrefetchScalarGridSpec(
            num_scalar_prefetch=1,
            grid=(NCORE,),
            in_specs=[flat, flat, share, share],
            out_specs=(pl.BlockSpec((half, feat), lambda i, s: (i, 0)), line, line),
        ),
        compiler_params=pltpu.CompilerParams(vmem_limit_bytes=16 * 2**20),
        cost_estimate=pl.CostEstimate(flops=1000000, bytes_accessed=4000000, transcendentals=0),
        name="finish",
    )(place, mine, other, gain_final[None], w_head[None])


def body(
    hidden_rows,
    lengths,
    pair_order,
    gain_attn,
    w_query,
    key_weight,
    value_weight,
    w_out,
    gain_final,
    w_head,
):
    rows, width = hidden_rows.shape
    n_mp = lax.axis_size("mp")
    n_dp = lax.axis_size("dp")
    feat = width // n_mp
    me = lax.axis_index("dp").astype(jnp.int32)
    core = me % NCORE
    along_x, along_z = dp_groups()
    place = jnp.stack([lax.axis_index("mp").astype(jnp.int32), core, lengths[0], me])

    mixed = front(hidden_rows, lengths, gain_attn, w_query, key_weight, value_weight)
    mixed, w_out, hidden_rows, gain_final, w_head = lax.optimization_barrier(
        (mixed, w_out, hidden_rows, gain_final, w_head)
    )
    piece_rows = w_out.shape[0] // NEAR
    my_near = (me // (NZ * NCORE)) * NCORE + core
    w_piece = lax.dynamic_slice_in_dim(w_out, my_near * piece_rows, piece_rows, 0)
    w_piece = w_piece.reshape(piece_rows, n_mp, feat).swapaxes(0, 1)
    w_piece = lax.all_to_all(w_piece, "mp", 0, 0, tiled=True)
    w_mine = swap(jnp.broadcast_to(w_piece[None], (NX,) + w_piece.shape), along_x)
    w_other = to_sibling(w_mine)

    parts = ring(mixed)
    x_cols = lax.dynamic_slice_in_dim(hidden_rows, place[0] * feat, feat, 1)
    both = lax.dynamic_slice_in_dim(gain_final * w_head, place[0] * feat, feat, 0)[None]
    resid, stats = project(place, parts, w_mine, w_other, x_cols, both)
    stats = lax.all_to_all(stats, "mp", 0, 0, tiled=True)
    reward, stats = lax.optimization_barrier((reward_of(lengths, stats, width, n_dp), stats))
    costs = -lax.all_to_all(reward, "dp", 0, 0, tiled=True)
    costs = jnp.maximum(lax.optimization_barrier(costs), jnp.finfo(F32).min)
    costs = jnp.minimum(lax.optimization_barrier(costs), jnp.finfo(F32).max)

    half = width // NCORE
    piece = -(-(half + 16) // (NX * NZ * 8)) * 8
    half_ext = piece * NX * NZ
    send, keep = gradient_halves(place, stats, resid, both, parts, half_ext, width)
    got = to_sibling(send)
    seqs = pair_order.shape[0]
    order = jnp.pad(pair_order, (0, LANES - seqs), constant_values=-1)[None]
    summed, margin, reward_row = weigh(place, costs, order, keep, got)
    loss = jnp.sum(jax.nn.softplus(-margin[0, :seqs:2]))

    got = swap(summed.reshape(NX, NZ * piece, feat), along_x)
    summed = jnp.sum(got.astype(F32), axis=0).astype(BF16)
    got = swap(summed.reshape(NZ, piece, feat), along_z)
    mine = jnp.sum(got.astype(F32), axis=0).astype(BF16)
    got = swap(jnp.broadcast_to(mine[None], (NZ, piece, feat)), along_z)
    got = swap(jnp.broadcast_to(got.reshape(1, NZ * piece, feat), (NX, NZ * piece, feat)), along_x)
    got = got.reshape(half_ext, feat)
    other = to_sibling(got)
    grad_out_proj, grad_head, grad_gain = finish(place, got, other, gain_final, w_head, half)
    return (loss, reward_row[0, :seqs], grad_out_proj, grad_head[0], grad_gain[0])


def solution(mesh):
    placed = (
        P("dp", None),
        P("dp"),
        P(),
        P(),
        P(None, "mp"),
        P(None, "mp"),
        P(None, "mp"),
        P("mp", None),
        P(),
        P(),
    )
    return jax.shard_map(
        body,
        mesh=mesh,
        in_specs=placed,
        out_specs=(P(), P(), P(None, "mp"), P("mp"), P("mp")),
        check_vma=False,
    )
```

```python
import functools

import jax
import jax.numpy as jnp
import numpy as np
from jax import lax
from jax.experimental import pallas as pl
from jax.experimental.pallas import tpu as pltpu
from jax.sharding import PartitionSpec as P

QUERY_HEADS = 32
KEY_VALUE_HEADS = 8
HEAD_SIZE = 64
NX, NZ, NCORE = 4, 12, 2

EPS = 1e-05
THETA = 500000.0
LANES = 128
F32 = jnp.float32
BF16 = jnp.bfloat16


def device_of(x, z, core):
    return (x * NZ + z) * NCORE + core


def dp_groups():
    along_x = [[device_of(x, z, c) for x in range(NX)] for z in range(NZ) for c in range(NCORE)]
    along_z = [[device_of(x, z, c) for z in range(NZ)] for x in range(NX) for c in range(NCORE)]
    return along_x, along_z


def swap(parts, groups):
    return lax.all_to_all(parts, "dp", 0, 0, tiled=True, axis_index_groups=groups)


def to_sibling(x):
    pairs = [(i, i ^ 1) for i in range(NX * NZ * NCORE)]
    return lax.ppermute(x, "dp", pairs)


def dot(a, b, a_dim, b_dim, precision=None):
    return lax.dot_general(
        a, b, (((a_dim,), (b_dim,)), ((), ())), preferred_element_type=F32, precision=precision
    )


def front_kernel(lens, x_hbm, gain_ref, wq_hbm, wk_hbm, wv_hbm, freq_ref, out_ref, x_ref, wq_ref, wk_ref, wv_ref, k_ref, v_ref, sems):
    total_rows = x_ref.shape[0]
    blocks = 2
    rows = total_rows // blocks
    copies = [
        pltpu.make_async_copy(x_hbm.at[pl.ds(0, rows)], x_ref.at[pl.ds(0, rows)], sems.at[0]),
        pltpu.make_async_copy(wq_hbm, wq_ref, sems.at[1]),
        pltpu.make_async_copy(wk_hbm, wk_ref, sems.at[2]),
        pltpu.make_async_copy(wv_hbm, wv_ref, sems.at[3]),
        pltpu.make_async_copy(x_hbm.at[pl.ds(rows, rows)], x_ref.at[pl.ds(rows, rows)], sems.at[4]),
    ]
    for copy in copies:
        copy.start()
    used = lens[0]
    lane = lax.broadcasted_iota(jnp.int32, (rows, LANES), 1)
    first_half = (lane % HEAD_SIZE) < HEAD_SIZE // 2
    low = lane < HEAD_SIZE
    gain = gain_ref[...]

    def tables(first):
        row = first + lax.broadcasted_iota(jnp.int32, (rows, LANES), 0)
        position = row - jnp.where(row >= used, used, 0)
        angle = position.astype(F32) * freq_ref[...]
        sine = jnp.sin(angle)
        return jnp.cos(angle), jnp.where(first_half, -sine, sine)

    turns = [tables(i * rows) for i in range(blocks)]

    def rotate(t, turn):
        partner = jnp.where(
            first_half, pltpu.roll(t, LANES - HEAD_SIZE // 2, 1), pltpu.roll(t, HEAD_SIZE // 2, 1)
        )
        return t * turn[0] + partner * turn[1]

    def norm(i):
        x = x_ref[i * rows : (i + 1) * rows, :].astype(F32)
        return (x * lax.rsqrt(jnp.mean(x * x, axis=1, keepdims=True) + EPS) * gain).astype(BF16)

    def attend(query, first, cols):
        row = first + lax.broadcasted_iota(jnp.int32, (rows, cols), 0)
        col = lax.broadcasted_iota(jnp.int32, (rows, cols), 1)
        allowed = (col <= row) & ((row >= used) == (col >= used))
        for p in range(len(query)):
            total = jnp.zeros((rows, LANES), F32)
            for e in range(LANES // HEAD_SIZE):
                scores = dot(query[p], k_ref[e, :cols, :], 1, 1) * HEAD_SIZE ** (-0.5)
                scores = jnp.where(allowed, scores, -1e30)
                top = jnp.max(scores, axis=1, keepdims=True)
                weights = jnp.exp(scores - top)
                probs = weights * (1.0 / jnp.sum(weights, axis=1, keepdims=True))
                total = total + dot(probs.astype(BF16), v_ref[e, :cols, :], 1, 0)
            out_ref[first : first + rows, p * LANES : (p + 1) * LANES] = total.astype(BF16)

    copies[0].wait()
    for i in range(blocks):
        if i == 1:
            copies[4].wait()
        normed = norm(i)
        if i == 0:
            for copy in copies[1:4]:
                copy.wait()
        query = dot(normed, wq_ref[...], 1, 0)
        key = dot(normed, wk_ref[...], 1, 1)
        value = dot(normed, wv_ref[...], 1, 1)
        key = rotate(jnp.concatenate([key, key], axis=1), turns[i])
        value = jnp.concatenate([value, value], axis=1)
        here = slice(i * rows, (i + 1) * rows)
        k_ref[0, here, :] = jnp.where(low, key, 0.0).astype(BF16)
        k_ref[1, here, :] = jnp.where(low, 0.0, key).astype(BF16)
        v_ref[0, here, :] = jnp.where(low, value, 0.0).astype(BF16)
        v_ref[1, here, :] = jnp.where(low, 0.0, value).astype(BF16)
        turned = [
            rotate(query[:, p * LANES : (p + 1) * LANES], turns[i]).astype(BF16)
            for p in range(query.shape[1] // LANES)
        ]
        attend(turned, i * rows, (i + 1) * rows)


def front(hidden_rows, lengths, gain_attn, w_query, key_weight, value_weight):
    rows, width = hidden_rows.shape
    key_weight, value_weight = key_weight.T, value_weight.T
    gain = gain_attn[None]
    half = HEAD_SIZE // 2
    freq = np.tile(THETA ** (-np.arange(half) * 2.0 / HEAD_SIZE), LANES // half).astype(np.float32)[None]
    whole = lambda a: pl.BlockSpec(a.shape, lambda i, s: (0, 0))
    far = pl.BlockSpec(memory_space=pl.ANY)
    return pl.pallas_call(
        front_kernel,
        out_shape=jax.ShapeDtypeStruct((rows, w_query.shape[1]), BF16),
        grid_spec=pltpu.PrefetchScalarGridSpec(
            num_scalar_prefetch=1,
            grid=(1,),
            in_specs=[far, whole(gain), far, far, far, whole(freq)],
            out_specs=pl.BlockSpec((rows, w_query.shape[1]), lambda i, s: (0, 0)),
            scratch_shapes=[
                pltpu.VMEM(hidden_rows.shape, BF16),
                pltpu.VMEM(w_query.shape, BF16),
                pltpu.VMEM(key_weight.shape, BF16),
                pltpu.VMEM(value_weight.shape, BF16),
                pltpu.VMEM((2, rows, LANES), BF16),
                pltpu.VMEM((2, rows, LANES), BF16),
                pltpu.SemaphoreType.DMA((5,)),
            ],
        ),
        compiler_params=pltpu.CompilerParams(vmem_limit_bytes=58 * 2**20),
        cost_estimate=pl.CostEstimate(flops=1500000000, bytes_accessed=4000000, transcendentals=900000),
        name="front",
    )(lengths, hidden_rows, gain, w_query, key_weight, value_weight, jnp.asarray(freq))


def ring(x):
    n = lax.axis_size("mp")
    up = [(i, (i + 1) % n) for i in range(n)]
    down = [(i, (i - 1) % n) for i in range(n)]
    parts, below, above = [(0, x)], x, x
    for step in range(1, n // 2):
        below, above = lax.ppermute(below, "mp", up), lax.ppermute(above, "mp", down)
        parts += [(-step, below), (step, above)]
    half = x.shape[0] // 2
    first = lax.ppermute(below[:half], "mp", up)
    second = lax.ppermute(above[half:], "mp", down)
    return parts + [(n // 2, (first, second))]


def flatten(parts):
    return [p for _, part in parts for p in (part if isinstance(part, tuple) else (part,))]


def shard_of(refs, i):
    if i < len(refs) - 2:
        return refs[i][...]
    return jnp.concatenate([refs[-2][...], refs[-1][...]], axis=0)


def cut_kernel(place, w_ref, out_ref):
    parts, rows, cols = out_ref.shape
    mine = pl.ds(pl.multiple_of(place[1] * rows, rows), rows)
    for g in range(parts):
        out_ref[g] = w_ref[mine, g * cols : (g + 1) * cols]


def cut(place, w_out, n_mp):
    shape = (n_mp, w_out.shape[0] // NCORE, w_out.shape[1] // n_mp)
    here = pl.BlockSpec(memory_space=pltpu.VMEM)
    return pl.pallas_call(
        cut_kernel,
        out_shape=jax.ShapeDtypeStruct(shape, BF16),
        in_specs=[pl.BlockSpec(memory_space=pltpu.SMEM), here],
        out_specs=here,
        compiler_params=pltpu.CompilerParams(vmem_limit_bytes=16 * 2**20),
        cost_estimate=pl.CostEstimate(flops=0, bytes_accessed=1000000, transcendentals=0),
        name="cut",
    )(place, w_out)


def project_kernel(distances, place, *refs):
    count = len(distances) + 1
    shards = refs[:count]
    mine_ref, other_ref, x_ref, both_ref, resid_ref, stats_ref, w_ref = refs[count:]
    groups, half, feat = mine_ref.shape
    w_ref[:, pl.ds(pl.multiple_of(place[1] * half, half), half), :] = mine_ref[...]
    w_ref[:, pl.ds(pl.multiple_of((1 - place[1]) * half, half), half), :] = other_ref[...]
    resid = x_ref[...].astype(F32)
    for i, distance in enumerate(distances):
        group = lax.rem(place[0] + (distance + groups), groups)
        resid = resid + dot(shard_of(shards, i), w_ref[group], 1, 0).astype(BF16).astype(F32)
    resid_ref[...] = resid
    squares = dot(jnp.ones((8, feat), F32), resid * resid, 1, 1, lax.Precision.HIGHEST)
    scores = dot(jnp.broadcast_to(both_ref[...], (8, feat)), resid, 1, 1, lax.Precision.HIGHEST)
    pair = jnp.concatenate([squares[:1], scores[:1]], axis=0)
    stats_ref[...] = jnp.broadcast_to(pair[None], stats_ref.shape)


def project(place, parts, w_mine, w_other, x_cols, both):
    n_mp, half, feat = w_mine.shape
    rows = x_cols.shape[0]
    shards = flatten(parts)
    here = pl.BlockSpec(memory_space=pltpu.VMEM)
    return pl.pallas_call(
        functools.partial(project_kernel, [d for d, _ in parts]),
        out_shape=(
            jax.ShapeDtypeStruct((rows, feat), F32),
            jax.ShapeDtypeStruct((n_mp, 2, rows), F32),
        ),
        in_specs=[pl.BlockSpec(memory_space=pltpu.SMEM)] + [here] * (len(shards) + 4),
        out_specs=(here, here),
        scratch_shapes=[pltpu.VMEM((n_mp, NCORE * half, feat), BF16)],
        compiler_params=pltpu.CompilerParams(vmem_limit_bytes=32 * 2**20),
        cost_estimate=pl.CostEstimate(flops=550000000, bytes_accessed=4000000, transcendentals=0),
        name="project",
    )(place, *shards, w_mine, w_other, x_cols, both)


def row_terms(stats, used, width):
    sums = stats[0]
    for part in range(1, stats.shape[0]):
        sums = sums + stats[part]
    scale = lax.rsqrt(sums[:1] / width + EPS)
    score = sums[1:2] * scale
    row = lax.broadcasted_iota(jnp.int32, scale.shape, 1)
    inside = row < used
    return scale, score, inside


def reward_kernel(width, lens, stats_ref, out_ref):
    _, score, inside = row_terms(stats_ref, lens[0], width)
    total = jnp.sum(jnp.where(inside, score, 0.0), axis=1, keepdims=True)
    reward = total / lens[0].astype(F32)
    out_ref[...] = jnp.broadcast_to(reward[None], out_ref.shape)


def reward_of(lengths, stats, width, n_dp):
    return pl.pallas_call(
        functools.partial(reward_kernel, width),
        out_shape=jax.ShapeDtypeStruct((n_dp, 1, LANES), F32),
        grid_spec=pltpu.PrefetchScalarGridSpec(
            num_scalar_prefetch=1,
            grid=(1,),
            in_specs=[pl.BlockSpec(stats.shape, lambda i, s: (0, 0, 0))],
            out_specs=pl.BlockSpec((n_dp, 1, LANES), lambda i, s: (0, 0, 0)),
        ),
        compiler_params=pltpu.CompilerParams(vmem_limit_bytes=16 * 2**20),
        cost_estimate=pl.CostEstimate(flops=10000, bytes_accessed=90000, transcendentals=512),
        name="reward",
    )(lengths, stats)


def gradient_kernel(width, distances, place, stats_ref, resid_ref, both_ref, *refs):
    count = len(distances) + 1
    shards = refs[:count]
    send_ref, keep_ref, d_ref, both_halves = refs[count:]
    rows, feat = resid_ref.shape
    heads = shards[0].shape[1]
    groups = width // heads
    used = place[2]
    scale, score, inside = row_terms(stats_ref, used, width)
    weight = jnp.where(inside, scale, 0.0) / used.astype(F32)
    minus = weight * scale * score * (1.0 / width)
    plus = jnp.broadcast_to(weight, (LANES, rows)).T
    minus = jnp.broadcast_to(minus, (LANES, rows)).T
    both = both_ref[...]
    pooled = []
    for part in range(feat // LANES):
        at = slice(part * LANES, (part + 1) * LANES)
        resid = resid_ref[:, at]
        d_ref[:, at] = (plus * both[:, at] - minus * resid).astype(BF16)
        pooled.append(jnp.sum(plus * resid, axis=0, keepdims=True))
    pooled = jnp.concatenate(pooled, axis=1)
    half = width // NCORE
    extra = send_ref.shape[0] - half
    first = lax.broadcasted_iota(jnp.int32, (extra, feat), 0) == 0
    pooled = jnp.where(first, pooled, 0.0).astype(BF16)
    send_ref[half:, :] = pooled
    keep_ref[half:, :] = pooled
    for i, distance in enumerate(distances):
        group = lax.rem(place[0] + (distance + groups), groups)
        stays = (lax.div(group, groups // NCORE) == place[1]).astype(jnp.int32)
        at = stays * half + lax.rem(group, groups // NCORE) * heads
        block = dot(shard_of(shards, i), d_ref[...], 0, 0).astype(BF16)
        both_halves[pl.ds(pl.multiple_of(at, heads), heads), :] = block
    send_ref[:half, :] = both_halves[:half, :]
    keep_ref[:half, :] = both_halves[half:, :]


def gradient_halves(place, stats, resid, both, parts, half_ext, width):
    rows, feat = resid.shape
    shards = flatten(parts)
    here = pl.BlockSpec(memory_space=pltpu.VMEM)
    half = jax.ShapeDtypeStruct((half_ext, feat), BF16)
    return pl.pallas_call(
        functools.partial(gradient_kernel, width, [d for d, _ in parts]),
        out_shape=(half, half),
        in_specs=[pl.BlockSpec(memory_space=pltpu.SMEM)] + [here] * (len(shards) + 3),
        out_specs=(here, here),
        scratch_shapes=[pltpu.VMEM((rows, feat), BF16), pltpu.VMEM((width, feat), BF16)],
        compiler_params=pltpu.CompilerParams(vmem_limit_bytes=32 * 2**20),
        cost_estimate=pl.CostEstimate(flops=550000000, bytes_accessed=4000000, transcendentals=0),
        name="gradient",
    )(place, stats, resid, both, *shards)


def weigh_kernel(place, costs_ref, order_ref, keep_ref, got_ref, out_ref, loss_ref, row_ref):
    seqs = costs_ref.shape[0]
    rewards = -costs_ref[...].reshape(seqs, LANES)
    order = order_ref[...]
    seq = lax.broadcasted_iota(jnp.int32, (seqs, LANES), 0)
    picked = jnp.sum(jnp.where(seq == order, rewards, 0.0), axis=0, keepdims=True)
    lane = lax.broadcasted_iota(jnp.int32, (1, LANES), 1)
    chosen = lane % 2 == 0
    partner = jnp.where(chosen, pltpu.roll(picked, LANES - 1, 1), pltpu.roll(picked, 1, 1))
    margin = jnp.where(chosen, picked - partner, partner - picked)
    sig = 1.0 / (1.0 + jnp.exp(margin))
    dreward = jnp.where(chosen, -sig, sig)
    me = place[3]
    own = jnp.sum(jnp.where(order == me, dreward, 0.0), axis=1, keepdims=True)
    sib = jnp.sum(jnp.where(order == (me ^ 1), dreward, 0.0), axis=1, keepdims=True)
    out_ref[...] = (keep_ref[...].astype(F32) * own + got_ref[...].astype(F32) * sib).astype(BF16)
    each = jnp.maximum(-margin, 0.0) + jnp.log1p(jnp.exp(-jnp.abs(margin)))
    counted = chosen & (lane < seqs)
    loss_ref[...] = jnp.sum(jnp.where(counted, each, 0.0), axis=1, keepdims=True)
    at = lax.broadcasted_iota(jnp.int32, (seqs, LANES), 1)
    row = jnp.sum(jnp.where(seq == at, rewards, 0.0), axis=0, keepdims=True)
    row_ref[...] = row[:, :seqs]


def weigh(place, costs, order, keep, got):
    flat = lambda a: pl.BlockSpec(a.shape, lambda i, s: (0,) * len(a.shape))
    return pl.pallas_call(
        weigh_kernel,
        out_shape=(
            jax.ShapeDtypeStruct(keep.shape, BF16),
            jax.ShapeDtypeStruct((1, 1), F32),
            jax.ShapeDtypeStruct((1, costs.shape[0]), F32),
        ),
        grid_spec=pltpu.PrefetchScalarGridSpec(
            num_scalar_prefetch=1,
            grid=(1,),
            in_specs=[flat(costs), flat(order), flat(keep), flat(got)],
            out_specs=(
                flat(keep),
                pl.BlockSpec((1, 1), lambda i, s: (0, 0)),
                pl.BlockSpec((1, costs.shape[0]), lambda i, s: (0, 0)),
            ),
        ),
        compiler_params=pltpu.CompilerParams(vmem_limit_bytes=16 * 2**20),
        cost_estimate=pl.CostEstimate(flops=1000000, bytes_accessed=2000000, transcendentals=128),
        name="weigh",
    )(place, costs, order, keep, got)


def finish_kernel(half, place, mine_ref, other_ref, gain_ref, head_ref, grad_ref, ghead_ref, ggain_ref):
    step = pl.program_id(0)

    @pl.when(step == place[1])
    def _():
        grad_ref[...] = mine_ref[:half, :].astype(F32)

    @pl.when(step != place[1])
    def _():
        grad_ref[...] = other_ref[:half, :].astype(F32)

    pooled = mine_ref[half : half + 16, :].astype(F32)[:1]
    ghead_ref[...] = gain_ref[...] * pooled
    ggain_ref[...] = head_ref[...] * pooled


def finish(place, mine, other, gain_final, w_head, half):
    feat = mine.shape[1]
    flat = pl.BlockSpec(mine.shape, lambda i, s: (0, 0))
    share = pl.BlockSpec((1, feat), lambda i, s: (0, s[0]))
    line = pl.BlockSpec((1, feat), lambda i, s: (0, 0))
    return pl.pallas_call(
        functools.partial(finish_kernel, half),
        out_shape=(
            jax.ShapeDtypeStruct((NCORE * half, feat), F32),
            jax.ShapeDtypeStruct((1, feat), F32),
            jax.ShapeDtypeStruct((1, feat), F32),
        ),
        grid_spec=pltpu.PrefetchScalarGridSpec(
            num_scalar_prefetch=1,
            grid=(NCORE,),
            in_specs=[flat, flat, share, share],
            out_specs=(pl.BlockSpec((half, feat), lambda i, s: (i, 0)), line, line),
        ),
        compiler_params=pltpu.CompilerParams(vmem_limit_bytes=16 * 2**20),
        cost_estimate=pl.CostEstimate(flops=1000000, bytes_accessed=4000000, transcendentals=0),
        name="finish",
    )(place, mine, other, gain_final[None], w_head[None])


def body(
    hidden_rows,
    lengths,
    pair_order,
    gain_attn,
    w_query,
    key_weight,
    value_weight,
    w_out,
    gain_final,
    w_head,
):
    rows, width = hidden_rows.shape
    n_mp = lax.axis_size("mp")
    n_dp = lax.axis_size("dp")
    feat = width // n_mp
    me = lax.axis_index("dp").astype(jnp.int32)
    core = me % NCORE
    along_x, along_z = dp_groups()
    place = jnp.stack([lax.axis_index("mp").astype(jnp.int32), core, lengths[0], me])

    mixed = front(hidden_rows, lengths, gain_attn, w_query, key_weight, value_weight)
    mixed, w_out, hidden_rows, gain_final, w_head = lax.optimization_barrier(
        (mixed, w_out, hidden_rows, gain_final, w_head)
    )
    w_mine = lax.all_to_all(cut(place, w_out, n_mp), "mp", 0, 0, tiled=True)
    w_other = to_sibling(w_mine)

    parts = ring(mixed)
    x_cols = lax.dynamic_slice_in_dim(hidden_rows, place[0] * feat, feat, 1)
    both = lax.dynamic_slice_in_dim(gain_final * w_head, place[0] * feat, feat, 0)[None]
    resid, stats = project(place, parts, w_mine, w_other, x_cols, both)
    stats = lax.all_to_all(stats, "mp", 0, 0, tiled=True)
    reward, stats = lax.optimization_barrier((reward_of(lengths, stats, width, n_dp), stats))
    costs = -lax.all_to_all(reward, "dp", 0, 0, tiled=True)
    costs = jnp.maximum(lax.optimization_barrier(costs), jnp.finfo(F32).min)
    costs = jnp.minimum(lax.optimization_barrier(costs), jnp.finfo(F32).max)

    half = width // NCORE
    piece = -(-(half + 16) // (NX * NZ * 8)) * 8
    half_ext = piece * NX * NZ
    send, keep = gradient_halves(place, stats, resid, both, parts, half_ext, width)
    got = to_sibling(send)
    seqs = pair_order.shape[0]
    order = jnp.pad(pair_order, (0, LANES - seqs), constant_values=-1)[None]
    summed, loss, reward_row = weigh(place, costs, order, keep, got)

    got = swap(summed.reshape(NX, NZ * piece, feat), along_x)
    summed = jnp.sum(got.astype(F32), axis=0).astype(BF16)
    got = swap(summed.reshape(NZ, piece, feat), along_z)
    mine = jnp.sum(got.astype(F32), axis=0).astype(BF16)
    got = swap(jnp.broadcast_to(mine[None], (NZ, piece, feat)), along_z)
    got = swap(jnp.broadcast_to(got.reshape(1, NZ * piece, feat), (NX, NZ * piece, feat)), along_x)
    got = got.reshape(half_ext, feat)
    other = to_sibling(got)
    grad_out_proj, grad_head, grad_gain = finish(place, got, other, gain_final, w_head, half)
    return (loss[0, 0], reward_row[0], grad_out_proj, grad_head[0], grad_gain[0])


def solution(mesh):
    placed = (
        P("dp", None),
        P("dp"),
        P(),
        P(),
        P(None, "mp"),
        P(None, "mp"),
        P(None, "mp"),
        P("mp", None),
        P(),
        P(),
    )
    return jax.shard_map(
        body,
        mesh=mesh,
        in_specs=placed,
        out_specs=(P(), P(), P(None, "mp"), P("mp"), P("mp")),
        check_vma=False,
    )
```

```python
import functools

import jax
import jax.numpy as jnp
import numpy as np
from jax import lax
from jax.experimental import pallas as pl
from jax.experimental.pallas import tpu as pltpu
from jax.sharding import PartitionSpec as P

QUERY_HEADS = 32
KEY_VALUE_HEADS = 8
HEAD_SIZE = 64
NX, NZ, NCORE = 4, 12, 2
NEAR = NX * NCORE

EPS = 1e-05
THETA = 500000.0
LANES = 128
F32 = jnp.float32
BF16 = jnp.bfloat16


def device_of(x, z, core):
    return (x * NZ + z) * NCORE + core


def dp_groups():
    along_x = [[device_of(x, z, c) for x in range(NX)] for z in range(NZ) for c in range(NCORE)]
    along_z = [[device_of(x, z, c) for z in range(NZ)] for x in range(NX) for c in range(NCORE)]
    return along_x, along_z


def swap(parts, groups):
    return lax.all_to_all(parts, "dp", 0, 0, tiled=True, axis_index_groups=groups)


def to_sibling(x):
    pairs = [(i, i ^ 1) for i in range(NX * NZ * NCORE)]
    return lax.ppermute(x, "dp", pairs)


def dot(a, b, a_dim, b_dim, precision=None):
    return lax.dot_general(
        a, b, (((a_dim,), (b_dim,)), ((), ())), preferred_element_type=F32, precision=precision
    )


def front_kernel(lens, x_hbm, gain_ref, wq_hbm, wk_hbm, wv_hbm, freq_ref, out_ref, x_ref, wq_ref, wk_ref, wv_ref, k_ref, v_ref, sems):
    total_rows = x_ref.shape[0]
    blocks = 2
    rows = total_rows // blocks
    copies = [
        pltpu.make_async_copy(x_hbm.at[pl.ds(0, rows)], x_ref.at[pl.ds(0, rows)], sems.at[0]),
        pltpu.make_async_copy(wq_hbm, wq_ref, sems.at[1]),
        pltpu.make_async_copy(wk_hbm, wk_ref, sems.at[2]),
        pltpu.make_async_copy(wv_hbm, wv_ref, sems.at[3]),
        pltpu.make_async_copy(x_hbm.at[pl.ds(rows, rows)], x_ref.at[pl.ds(rows, rows)], sems.at[4]),
    ]
    for copy in copies:
        copy.start()
    used = lens[0]
    lane = lax.broadcasted_iota(jnp.int32, (rows, LANES), 1)
    first_half = (lane % HEAD_SIZE) < HEAD_SIZE // 2
    low = lane < HEAD_SIZE
    gain = gain_ref[...]

    def tables(first):
        row = first + lax.broadcasted_iota(jnp.int32, (rows, LANES), 0)
        position = row - jnp.where(row >= used, used, 0)
        angle = position.astype(F32) * freq_ref[...]
        sine = jnp.sin(angle)
        return jnp.cos(angle), jnp.where(first_half, -sine, sine)

    turns = [tables(i * rows) for i in range(blocks)]

    def rotate(t, turn):
        partner = jnp.where(
            first_half, pltpu.roll(t, LANES - HEAD_SIZE // 2, 1), pltpu.roll(t, HEAD_SIZE // 2, 1)
        )
        return t * turn[0] + partner * turn[1]

    def norm(i):
        x = x_ref[i * rows : (i + 1) * rows, :].astype(F32)
        return (x * lax.rsqrt(jnp.mean(x * x, axis=1, keepdims=True) + EPS) * gain).astype(BF16)

    def attend(query, first, cols):
        row = first + lax.broadcasted_iota(jnp.int32, (rows, cols), 0)
        col = lax.broadcasted_iota(jnp.int32, (rows, cols), 1)
        allowed = (col <= row) & ((row >= used) == (col >= used))
        for p in range(len(query)):
            total = jnp.zeros((rows, LANES), F32)
            for e in range(LANES // HEAD_SIZE):
                scores = dot(query[p], k_ref[e, :cols, :], 1, 1) * HEAD_SIZE ** (-0.5)
                scores = jnp.where(allowed, scores, -1e30)
                top = jnp.max(scores, axis=1, keepdims=True)
                weights = jnp.exp(scores - top)
                probs = weights * (1.0 / jnp.sum(weights, axis=1, keepdims=True))
                total = total + dot(probs.astype(BF16), v_ref[e, :cols, :], 1, 0)
            out_ref[first : first + rows, p * LANES : (p + 1) * LANES] = total.astype(BF16)

    copies[0].wait()
    for i in range(blocks):
        if i == 1:
            copies[4].wait()
        normed = norm(i)
        if i == 0:
            for copy in copies[1:4]:
                copy.wait()
        query = dot(normed, wq_ref[...], 1, 0)
        key = dot(normed, wk_ref[...], 1, 1)
        value = dot(normed, wv_ref[...], 1, 1)
        key = rotate(jnp.concatenate([key, key], axis=1), turns[i])
        value = jnp.concatenate([value, value], axis=1)
        here = slice(i * rows, (i + 1) * rows)
        k_ref[0, here, :] = jnp.where(low, key, 0.0).astype(BF16)
        k_ref[1, here, :] = jnp.where(low, 0.0, key).astype(BF16)
        v_ref[0, here, :] = jnp.where(low, value, 0.0).astype(BF16)
        v_ref[1, here, :] = jnp.where(low, 0.0, value).astype(BF16)
        turned = [
            rotate(query[:, p * LANES : (p + 1) * LANES], turns[i]).astype(BF16)
            for p in range(query.shape[1] // LANES)
        ]
        attend(turned, i * rows, (i + 1) * rows)


def front(hidden_rows, lengths, gain_attn, w_query, key_weight, value_weight):
    rows, width = hidden_rows.shape
    key_weight, value_weight = key_weight.T, value_weight.T
    gain = gain_attn[None]
    half = HEAD_SIZE // 2
    freq = np.tile(THETA ** (-np.arange(half) * 2.0 / HEAD_SIZE), LANES // half).astype(np.float32)[None]
    whole = lambda a: pl.BlockSpec(a.shape, lambda i, s: (0, 0))
    far = pl.BlockSpec(memory_space=pl.ANY)
    return pl.pallas_call(
        front_kernel,
        out_shape=jax.ShapeDtypeStruct((rows, w_query.shape[1]), BF16),
        grid_spec=pltpu.PrefetchScalarGridSpec(
            num_scalar_prefetch=1,
            grid=(1,),
            in_specs=[far, whole(gain), far, far, far, whole(freq)],
            out_specs=pl.BlockSpec((rows, w_query.shape[1]), lambda i, s: (0, 0)),
            scratch_shapes=[
                pltpu.VMEM(hidden_rows.shape, BF16),
                pltpu.VMEM(w_query.shape, BF16),
                pltpu.VMEM(key_weight.shape, BF16),
                pltpu.VMEM(value_weight.shape, BF16),
                pltpu.VMEM((2, rows, LANES), BF16),
                pltpu.VMEM((2, rows, LANES), BF16),
                pltpu.SemaphoreType.DMA((5,)),
            ],
        ),
        compiler_params=pltpu.CompilerParams(vmem_limit_bytes=58 * 2**20),
        cost_estimate=pl.CostEstimate(flops=1500000000, bytes_accessed=4000000, transcendentals=900000),
        name="front",
    )(lengths, hidden_rows, gain, w_query, key_weight, value_weight, jnp.asarray(freq))


def ring(x):
    n = lax.axis_size("mp")
    up = [(i, (i + 1) % n) for i in range(n)]
    down = [(i, (i - 1) % n) for i in range(n)]
    parts, below, above = [(0, x)], x, x
    for step in range(1, n // 2):
        below, above = lax.ppermute(below, "mp", up), lax.ppermute(above, "mp", down)
        parts += [(-step, below), (step, above)]
    half = x.shape[0] // 2
    first = lax.ppermute(below[:half], "mp", up)
    second = lax.ppermute(above[half:], "mp", down)
    return parts + [(n // 2, (first, second))]


def flatten(parts):
    return [p for _, part in parts for p in (part if isinstance(part, tuple) else (part,))]


def shard_of(refs, i):
    if i < len(refs) - 2:
        return refs[i][...]
    return jnp.concatenate([refs[-2][...], refs[-1][...]], axis=0)


def project_kernel(distances, place, *refs):
    count = len(distances) + 1
    shards = refs[:count]
    mine_ref, other_ref, x_ref, both_ref, resid_ref, stats_ref, w_ref = refs[count:]
    groups, feat = mine_ref.shape[1], mine_ref.shape[3]
    for x in range(NX):
        for g in range(groups):
            w_ref[g, NCORE * x + place[1]] = mine_ref[x, g]
            w_ref[g, NCORE * x + 1 - place[1]] = other_ref[x, g]
    resid = x_ref[...].astype(F32)
    for i, distance in enumerate(distances):
        group = lax.rem(place[0] + (distance + groups), groups)
        weight = w_ref[group].reshape(-1, feat)
        resid = resid + dot(shard_of(shards, i), weight, 1, 0).astype(BF16).astype(F32)
    resid_ref[...] = resid
    squares = dot(jnp.ones((8, feat), F32), resid * resid, 1, 1, lax.Precision.HIGHEST)
    scores = dot(jnp.broadcast_to(both_ref[...], (8, feat)), resid, 1, 1, lax.Precision.HIGHEST)
    pair = jnp.concatenate([squares[:1], scores[:1]], axis=0)
    stats_ref[...] = jnp.broadcast_to(pair[None], stats_ref.shape)


def project(place, parts, w_mine, w_other, x_cols, both):
    _, n_mp, piece_rows, feat = w_mine.shape
    rows = x_cols.shape[0]
    shards = flatten(parts)
    here = pl.BlockSpec(memory_space=pltpu.VMEM)
    return pl.pallas_call(
        functools.partial(project_kernel, [d for d, _ in parts]),
        out_shape=(
            jax.ShapeDtypeStruct((rows, feat), F32),
            jax.ShapeDtypeStruct((n_mp, 2, rows), F32),
        ),
        in_specs=[pl.BlockSpec(memory_space=pltpu.SMEM)] + [here] * (len(shards) + 4),
        out_specs=(here, here),
        scratch_shapes=[pltpu.VMEM((n_mp, NEAR, piece_rows, feat), BF16)],
        compiler_params=pltpu.CompilerParams(vmem_limit_bytes=32 * 2**20),
        cost_estimate=pl.CostEstimate(flops=550000000, bytes_accessed=4000000, transcendentals=0),
        name="project",
    )(place, *shards, w_mine, w_other, x_cols, both)


def row_terms(stats, used, width):
    sums = stats[0]
    for part in range(1, stats.shape[0]):
        sums = sums + stats[part]
    scale = lax.rsqrt(sums[:1] / width + EPS)
    score = sums[1:2] * scale
    row = lax.broadcasted_iota(jnp.int32, scale.shape, 1)
    inside = row < used
    return scale, score, inside


def reward_kernel(width, lens, stats_ref, out_ref):
    _, score, inside = row_terms(stats_ref, lens[0], width)
    total = jnp.sum(jnp.where(inside, score, 0.0), axis=1, keepdims=True)
    reward = total / lens[0].astype(F32)
    out_ref[...] = jnp.broadcast_to(reward[None], out_ref.shape)


def reward_of(lengths, stats, width, n_dp):
    return pl.pallas_call(
        functools.partial(reward_kernel, width),
        out_shape=jax.ShapeDtypeStruct((n_dp, 1, LANES), F32),
        grid_spec=pltpu.PrefetchScalarGridSpec(
            num_scalar_prefetch=1,
            grid=(1,),
            in_specs=[pl.BlockSpec(stats.shape, lambda i, s: (0, 0, 0))],
            out_specs=pl.BlockSpec((n_dp, 1, LANES), lambda i, s: (0, 0, 0)),
        ),
        compiler_params=pltpu.CompilerParams(vmem_limit_bytes=16 * 2**20),
        cost_estimate=pl.CostEstimate(flops=10000, bytes_accessed=90000, transcendentals=512),
        name="reward",
    )(lengths, stats)


def gradient_kernel(width, distances, place, stats_ref, resid_ref, both_ref, *refs):
    count = len(distances) + 1
    shards = refs[:count]
    send_ref, keep_ref, d_ref, both_halves = refs[count:]
    rows, feat = resid_ref.shape
    heads = shards[0].shape[1]
    groups = width // heads
    used = place[2]
    scale, score, inside = row_terms(stats_ref, used, width)
    weight = jnp.where(inside, scale, 0.0) / used.astype(F32)
    minus = weight * scale * score * (1.0 / width)
    plus = jnp.broadcast_to(weight, (LANES, rows)).T
    minus = jnp.broadcast_to(minus, (LANES, rows)).T
    both = both_ref[...]
    pooled = []
    for part in range(feat // LANES):
        at = slice(part * LANES, (part + 1) * LANES)
        resid = resid_ref[:, at]
        d_ref[:, at] = (plus * both[:, at] - minus * resid).astype(BF16)
        pooled.append(jnp.sum(plus * resid, axis=0, keepdims=True))
    pooled = jnp.concatenate(pooled, axis=1)
    half = width // NCORE
    extra = send_ref.shape[0] - half
    first = lax.broadcasted_iota(jnp.int32, (extra, feat), 0) == 0
    pooled = jnp.where(first, pooled, 0.0).astype(BF16)
    send_ref[half:, :] = pooled
    keep_ref[half:, :] = pooled
    for i, distance in enumerate(distances):
        group = lax.rem(place[0] + (distance + groups), groups)
        stays = (lax.div(group, groups // NCORE) == place[1]).astype(jnp.int32)
        at = stays * half + lax.rem(group, groups // NCORE) * heads
        block = dot(shard_of(shards, i), d_ref[...], 0, 0).astype(BF16)
        both_halves[pl.ds(pl.multiple_of(at, heads), heads), :] = block
    send_ref[:half, :] = both_halves[:half, :]
    keep_ref[:half, :] = both_halves[half:, :]


def gradient_halves(place, stats, resid, both, parts, half_ext, width):
    rows, feat = resid.shape
    shards = flatten(parts)
    here = pl.BlockSpec(memory_space=pltpu.VMEM)
    half = jax.ShapeDtypeStruct((half_ext, feat), BF16)
    return pl.pallas_call(
        functools.partial(gradient_kernel, width, [d for d, _ in parts]),
        out_shape=(half, half),
        in_specs=[pl.BlockSpec(memory_space=pltpu.SMEM)] + [here] * (len(shards) + 3),
        out_specs=(here, here),
        scratch_shapes=[pltpu.VMEM((rows, feat), BF16), pltpu.VMEM((width, feat), BF16)],
        compiler_params=pltpu.CompilerParams(vmem_limit_bytes=32 * 2**20),
        cost_estimate=pl.CostEstimate(flops=550000000, bytes_accessed=4000000, transcendentals=0),
        name="gradient",
    )(place, stats, resid, both, *shards)


def weigh_kernel(place, costs_ref, order_ref, keep_ref, got_ref, out_ref, loss_ref, row_ref):
    seqs = costs_ref.shape[0]
    rewards = -costs_ref[...].reshape(seqs, LANES)
    order = order_ref[...]
    seq = lax.broadcasted_iota(jnp.int32, (seqs, LANES), 0)
    picked = jnp.sum(jnp.where(seq == order, rewards, 0.0), axis=0, keepdims=True)
    lane = lax.broadcasted_iota(jnp.int32, (1, LANES), 1)
    chosen = lane % 2 == 0
    partner = jnp.where(chosen, pltpu.roll(picked, LANES - 1, 1), pltpu.roll(picked, 1, 1))
    margin = jnp.where(chosen, picked - partner, partner - picked)
    sig = 1.0 / (1.0 + jnp.exp(margin))
    dreward = jnp.where(chosen, -sig, sig)
    me = place[3]
    own = jnp.sum(jnp.where(order == me, dreward, 0.0), axis=1, keepdims=True)
    sib = jnp.sum(jnp.where(order == (me ^ 1), dreward, 0.0), axis=1, keepdims=True)
    out_ref[...] = (keep_ref[...].astype(F32) * own + got_ref[...].astype(F32) * sib).astype(BF16)
    each = jnp.maximum(-margin, 0.0) + jnp.log1p(jnp.exp(-jnp.abs(margin)))
    counted = chosen & (lane < seqs)
    loss_ref[...] = jnp.sum(jnp.where(counted, each, 0.0), axis=1, keepdims=True)
    at = lax.broadcasted_iota(jnp.int32, (seqs, LANES), 1)
    row = jnp.sum(jnp.where(seq == at, rewards, 0.0), axis=0, keepdims=True)
    row_ref[...] = row[:, :seqs]


def weigh(place, costs, order, keep, got):
    flat = lambda a: pl.BlockSpec(a.shape, lambda i, s: (0,) * len(a.shape))
    return pl.pallas_call(
        weigh_kernel,
        out_shape=(
            jax.ShapeDtypeStruct(keep.shape, BF16),
            jax.ShapeDtypeStruct((1, 1), F32),
            jax.ShapeDtypeStruct((1, costs.shape[0]), F32),
        ),
        grid_spec=pltpu.PrefetchScalarGridSpec(
            num_scalar_prefetch=1,
            grid=(1,),
            in_specs=[flat(costs), flat(order), flat(keep), flat(got)],
            out_specs=(
                flat(keep),
                pl.BlockSpec((1, 1), lambda i, s: (0, 0)),
                pl.BlockSpec((1, costs.shape[0]), lambda i, s: (0, 0)),
            ),
        ),
        compiler_params=pltpu.CompilerParams(vmem_limit_bytes=16 * 2**20),
        cost_estimate=pl.CostEstimate(flops=1000000, bytes_accessed=2000000, transcendentals=128),
        name="weigh",
    )(place, costs, order, keep, got)


def finish_kernel(half, place, mine_ref, other_ref, gain_ref, head_ref, grad_ref, ghead_ref, ggain_ref):
    step = pl.program_id(0)

    @pl.when(step == place[1])
    def _():
        grad_ref[...] = mine_ref[:half, :].astype(F32)

    @pl.when(step != place[1])
    def _():
        grad_ref[...] = other_ref[:half, :].astype(F32)

    pooled = mine_ref[half : half + 16, :].astype(F32)[:1]
    ghead_ref[...] = gain_ref[...] * pooled
    ggain_ref[...] = head_ref[...] * pooled


def finish(place, mine, other, gain_final, w_head, half):
    feat = mine.shape[1]
    flat = pl.BlockSpec(mine.shape, lambda i, s: (0, 0))
    share = pl.BlockSpec((1, feat), lambda i, s: (0, s[0]))
    line = pl.BlockSpec((1, feat), lambda i, s: (0, 0))
    return pl.pallas_call(
        functools.partial(finish_kernel, half),
        out_shape=(
            jax.ShapeDtypeStruct((NCORE * half, feat), F32),
            jax.ShapeDtypeStruct((1, feat), F32),
            jax.ShapeDtypeStruct((1, feat), F32),
        ),
        grid_spec=pltpu.PrefetchScalarGridSpec(
            num_scalar_prefetch=1,
            grid=(NCORE,),
            in_specs=[flat, flat, share, share],
            out_specs=(pl.BlockSpec((half, feat), lambda i, s: (i, 0)), line, line),
        ),
        compiler_params=pltpu.CompilerParams(vmem_limit_bytes=16 * 2**20),
        cost_estimate=pl.CostEstimate(flops=1000000, bytes_accessed=4000000, transcendentals=0),
        name="finish",
    )(place, mine, other, gain_final[None], w_head[None])


def body(
    hidden_rows,
    lengths,
    pair_order,
    gain_attn,
    w_query,
    key_weight,
    value_weight,
    w_out,
    gain_final,
    w_head,
):
    rows, width = hidden_rows.shape
    n_mp = lax.axis_size("mp")
    n_dp = lax.axis_size("dp")
    feat = width // n_mp
    me = lax.axis_index("dp").astype(jnp.int32)
    core = me % NCORE
    along_x, along_z = dp_groups()
    place = jnp.stack([lax.axis_index("mp").astype(jnp.int32), core, lengths[0], me])

    mixed = front(hidden_rows, lengths, gain_attn, w_query, key_weight, value_weight)
    mixed, w_out, hidden_rows, gain_final, w_head = lax.optimization_barrier(
        (mixed, w_out, hidden_rows, gain_final, w_head)
    )
    piece_rows = w_out.shape[0] // NEAR
    my_near = (me // (NZ * NCORE)) * NCORE + core
    w_piece = lax.dynamic_slice_in_dim(w_out, my_near * piece_rows, piece_rows, 0)
    w_piece = w_piece.reshape(piece_rows, n_mp, feat).swapaxes(0, 1)
    w_piece = lax.all_to_all(w_piece, "mp", 0, 0, tiled=True)
    w_mine = swap(jnp.broadcast_to(w_piece[None], (NX,) + w_piece.shape), along_x)
    w_other = to_sibling(w_mine)

    parts = ring(mixed)
    x_cols = lax.dynamic_slice_in_dim(hidden_rows, place[0] * feat, feat, 1)
    both = lax.dynamic_slice_in_dim(gain_final * w_head, place[0] * feat, feat, 0)[None]
    resid, stats = project(place, parts, w_mine, w_other, x_cols, both)
    stats = lax.all_to_all(stats, "mp", 0, 0, tiled=True)
    reward, stats = lax.optimization_barrier((reward_of(lengths, stats, width, n_dp), stats))
    costs = -lax.all_to_all(reward, "dp", 0, 0, tiled=True)
    costs = jnp.maximum(lax.optimization_barrier(costs), jnp.finfo(F32).min)
    costs = jnp.minimum(lax.optimization_barrier(costs), jnp.finfo(F32).max)

    half = width // NCORE
    piece = -(-(half + 16) // (NX * NZ * 8)) * 8
    half_ext = piece * NX * NZ
    send, keep = gradient_halves(place, stats, resid, both, parts, half_ext, width)
    got = to_sibling(send)
    seqs = pair_order.shape[0]
    order = jnp.pad(pair_order, (0, LANES - seqs), constant_values=-1)[None]
    summed, loss, reward_row = weigh(place, costs, order, keep, got)

    got = swap(summed.reshape(NX, NZ * piece, feat), along_x)
    summed = jnp.sum(got.astype(F32), axis=0).astype(BF16)
    got = swap(summed.reshape(NZ, piece, feat), along_z)
    mine = jnp.sum(got.astype(F32), axis=0).astype(BF16)
    got = swap(jnp.broadcast_to(mine[None], (NZ, piece, feat)), along_z)
    got = swap(jnp.broadcast_to(got.reshape(1, NZ * piece, feat), (NX, NZ * piece, feat)), along_x)
    got = got.reshape(half_ext, feat)
    other = to_sibling(got)
    grad_out_proj, grad_head, grad_gain = finish(place, got, other, gain_final, w_head, half)
    return (loss[0, 0], reward_row[0], grad_out_proj, grad_head[0], grad_gain[0])


def solution(mesh):
    placed = (
        P("dp", None),
        P("dp"),
        P(),
        P(),
        P(None, "mp"),
        P(None, "mp"),
        P(None, "mp"),
        P("mp", None),
        P(),
        P(),
    )
    return jax.shard_map(
        body,
        mesh=mesh,
        in_specs=placed,
        out_specs=(P(), P(), P(None, "mp"), P("mp"), P("mp")),
        check_vma=False,
    )
```

```python
import functools

import jax
import jax.numpy as jnp
import numpy as np
from jax import lax
from jax.experimental import pallas as pl
from jax.experimental.pallas import tpu as pltpu
from jax.sharding import PartitionSpec as P

QUERY_HEADS = 32
KEY_VALUE_HEADS = 8
HEAD_SIZE = 64
NX, NZ, NCORE = 4, 12, 2
NEAR = NX * NCORE

EPS = 1e-05
THETA = 500000.0
LANES = 128
F32 = jnp.float32
BF16 = jnp.bfloat16


def device_of(x, z, core):
    return (x * NZ + z) * NCORE + core


def dp_groups():
    along_x = [[device_of(x, z, c) for x in range(NX)] for z in range(NZ) for c in range(NCORE)]
    along_z = [[device_of(x, z, c) for z in range(NZ)] for x in range(NX) for c in range(NCORE)]
    return along_x, along_z


def swap(parts, groups):
    return lax.all_to_all(parts, "dp", 0, 0, tiled=True, axis_index_groups=groups)


def to_sibling(x):
    pairs = [(i, i ^ 1) for i in range(NX * NZ * NCORE)]
    return lax.ppermute(x, "dp", pairs)


def dot(a, b, a_dim, b_dim, precision=None):
    return lax.dot_general(
        a, b, (((a_dim,), (b_dim,)), ((), ())), preferred_element_type=F32, precision=precision
    )


def front_kernel(lens, x_hbm, gain_ref, wq_hbm, wk_hbm, wv_hbm, freq_ref, out_ref, x_ref, wq_ref, wk_ref, wv_ref, k_ref, v_ref, sems):
    total_rows = x_ref.shape[0]
    blocks = 2
    rows = total_rows // blocks
    copies = [
        pltpu.make_async_copy(x_hbm.at[pl.ds(0, rows)], x_ref.at[pl.ds(0, rows)], sems.at[0]),
        pltpu.make_async_copy(wq_hbm, wq_ref, sems.at[1]),
        pltpu.make_async_copy(wk_hbm, wk_ref, sems.at[2]),
        pltpu.make_async_copy(wv_hbm, wv_ref, sems.at[3]),
        pltpu.make_async_copy(x_hbm.at[pl.ds(rows, rows)], x_ref.at[pl.ds(rows, rows)], sems.at[4]),
    ]
    for copy in copies:
        copy.start()
    used = lens[0]
    lane = lax.broadcasted_iota(jnp.int32, (rows, LANES), 1)
    first_half = (lane % HEAD_SIZE) < HEAD_SIZE // 2
    low = lane < HEAD_SIZE
    gain = gain_ref[...]

    def tables(first):
        row = first + lax.broadcasted_iota(jnp.int32, (rows, LANES), 0)
        position = row - jnp.where(row >= used, used, 0)
        angle = position.astype(F32) * freq_ref[...]
        sine = jnp.sin(angle)
        return jnp.cos(angle), jnp.where(first_half, -sine, sine)

    turns = [tables(i * rows) for i in range(blocks)]

    def rotate(t, turn):
        partner = jnp.where(
            first_half, pltpu.roll(t, LANES - HEAD_SIZE // 2, 1), pltpu.roll(t, HEAD_SIZE // 2, 1)
        )
        return t * turn[0] + partner * turn[1]

    def norm(i):
        x = x_ref[i * rows : (i + 1) * rows, :].astype(F32)
        return (x * lax.rsqrt(jnp.mean(x * x, axis=1, keepdims=True) + EPS) * gain).astype(BF16)

    def attend(query, first, cols):
        row = first + lax.broadcasted_iota(jnp.int32, (rows, cols), 0)
        col = lax.broadcasted_iota(jnp.int32, (rows, cols), 1)
        allowed = (col <= row) & ((row >= used) == (col >= used))
        for p in range(len(query)):
            total = jnp.zeros((rows, LANES), F32)
            for e in range(LANES // HEAD_SIZE):
                scores = dot(query[p], k_ref[e, :cols, :], 1, 1) * HEAD_SIZE ** (-0.5)
                scores = jnp.where(allowed, scores, -1e30)
                top = jnp.max(scores, axis=1, keepdims=True)
                weights = jnp.exp(scores - top)
                probs = weights * (1.0 / jnp.sum(weights, axis=1, keepdims=True))
                total = total + dot(probs.astype(BF16), v_ref[e, :cols, :], 1, 0)
            out_ref[first : first + rows, p * LANES : (p + 1) * LANES] = total.astype(BF16)

    copies[0].wait()
    for i in range(blocks):
        if i == 1:
            copies[4].wait()
        normed = norm(i)
        if i == 0:
            for copy in copies[1:4]:
                copy.wait()
        query = dot(normed, wq_ref[...], 1, 0)
        key = dot(normed, wk_ref[...], 1, 1)
        value = dot(normed, wv_ref[...], 1, 1)
        key = rotate(jnp.concatenate([key, key], axis=1), turns[i])
        value = jnp.concatenate([value, value], axis=1)
        here = slice(i * rows, (i + 1) * rows)
        k_ref[0, here, :] = jnp.where(low, key, 0.0).astype(BF16)
        k_ref[1, here, :] = jnp.where(low, 0.0, key).astype(BF16)
        v_ref[0, here, :] = jnp.where(low, value, 0.0).astype(BF16)
        v_ref[1, here, :] = jnp.where(low, 0.0, value).astype(BF16)
        turned = [
            rotate(query[:, p * LANES : (p + 1) * LANES], turns[i]).astype(BF16)
            for p in range(query.shape[1] // LANES)
        ]
        attend(turned, i * rows, (i + 1) * rows)


def front(hidden_rows, lengths, gain_attn, w_query, key_weight, value_weight):
    rows, width = hidden_rows.shape
    key_weight, value_weight = key_weight.T, value_weight.T
    gain = gain_attn[None]
    half = HEAD_SIZE // 2
    freq = np.tile(THETA ** (-np.arange(half) * 2.0 / HEAD_SIZE), LANES // half).astype(np.float32)[None]
    whole = lambda a: pl.BlockSpec(a.shape, lambda i, s: (0, 0))
    far = pl.BlockSpec(memory_space=pl.ANY)
    return pl.pallas_call(
        front_kernel,
        out_shape=jax.ShapeDtypeStruct((rows, w_query.shape[1]), BF16),
        grid_spec=pltpu.PrefetchScalarGridSpec(
            num_scalar_prefetch=1,
            grid=(1,),
            in_specs=[far, whole(gain), far, far, far, whole(freq)],
            out_specs=pl.BlockSpec((rows, w_query.shape[1]), lambda i, s: (0, 0)),
            scratch_shapes=[
                pltpu.VMEM(hidden_rows.shape, BF16),
                pltpu.VMEM(w_query.shape, BF16),
                pltpu.VMEM(key_weight.shape, BF16),
                pltpu.VMEM(value_weight.shape, BF16),
                pltpu.VMEM((2, rows, LANES), BF16),
                pltpu.VMEM((2, rows, LANES), BF16),
                pltpu.SemaphoreType.DMA((5,)),
            ],
        ),
        compiler_params=pltpu.CompilerParams(vmem_limit_bytes=58 * 2**20),
        cost_estimate=pl.CostEstimate(flops=1500000000, bytes_accessed=4000000, transcendentals=900000),
        name="front",
    )(lengths, hidden_rows, gain, w_query, key_weight, value_weight, jnp.asarray(freq))


def ring(x, beside):
    n = lax.axis_size("mp")
    up = [(i, (i + 1) % n) for i in range(n)]
    down = [(i, (i - 1) % n) for i in range(n)]
    parts, below, above = [(0, x)], x, x
    for step in range(1, n // 2):
        below, above = lax.ppermute(below, "mp", up), lax.ppermute(above, "mp", down)
        if step == 1:
            below, beside = lax.optimization_barrier((below, beside))
        parts += [(-step, below), (step, above)]
    half = x.shape[0] // 2
    first = lax.ppermute(below[:half], "mp", up)
    second = lax.ppermute(above[half:], "mp", down)
    return parts + [(n // 2, (first, second))], beside


def flatten(parts):
    return [p for _, part in parts for p in (part if isinstance(part, tuple) else (part,))]


def shard_of(refs, i):
    if i < len(refs) - 2:
        return refs[i][...]
    return jnp.concatenate([refs[-2][...], refs[-1][...]], axis=0)


def project_kernel(distances, place, *refs):
    count = len(distances) + 1
    shards = refs[:count]
    mine_ref, other_ref, x_ref, both_ref, resid_ref, stats_ref, w_ref = refs[count:]
    groups, feat = mine_ref.shape[1], mine_ref.shape[3]
    for x in range(NX):
        for g in range(groups):
            w_ref[g, NCORE * x + place[1]] = mine_ref[x, g]
            w_ref[g, NCORE * x + 1 - place[1]] = other_ref[x, g]
    resid = x_ref[...].astype(F32)
    for i, distance in enumerate(distances):
        group = lax.rem(place[0] + (distance + groups), groups)
        weight = w_ref[group].reshape(-1, feat)
        resid = resid + dot(shard_of(shards, i), weight, 1, 0).astype(BF16).astype(F32)
    resid_ref[...] = resid
    squares = dot(jnp.ones((8, feat), F32), resid * resid, 1, 1, lax.Precision.HIGHEST)
    scores = dot(jnp.broadcast_to(both_ref[...], (8, feat)), resid, 1, 1, lax.Precision.HIGHEST)
    pair = jnp.concatenate([squares[:1], scores[:1]], axis=0)
    stats_ref[...] = jnp.broadcast_to(pair[None], stats_ref.shape)


def project(place, parts, w_mine, w_other, x_cols, both):
    _, n_mp, piece_rows, feat = w_mine.shape
    rows = x_cols.shape[0]
    shards = flatten(parts)
    here = pl.BlockSpec(memory_space=pltpu.VMEM)
    return pl.pallas_call(
        functools.partial(project_kernel, [d for d, _ in parts]),
        out_shape=(
            jax.ShapeDtypeStruct((rows, feat), F32),
            jax.ShapeDtypeStruct((n_mp, 2, rows), F32),
        ),
        in_specs=[pl.BlockSpec(memory_space=pltpu.SMEM)] + [here] * (len(shards) + 4),
        out_specs=(here, here),
        scratch_shapes=[pltpu.VMEM((n_mp, NEAR, piece_rows, feat), BF16)],
        compiler_params=pltpu.CompilerParams(vmem_limit_bytes=32 * 2**20),
        cost_estimate=pl.CostEstimate(flops=550000000, bytes_accessed=4000000, transcendentals=0),
        name="project",
    )(place, *shards, w_mine, w_other, x_cols, both)


def row_terms(stats, used, width):
    sums = stats[0]
    for part in range(1, stats.shape[0]):
        sums = sums + stats[part]
    scale = lax.rsqrt(sums[:1] / width + EPS)
    score = sums[1:2] * scale
    row = lax.broadcasted_iota(jnp.int32, scale.shape, 1)
    inside = row < used
    return scale, score, inside


def reward_kernel(width, lens, stats_ref, out_ref):
    _, score, inside = row_terms(stats_ref, lens[0], width)
    total = jnp.sum(jnp.where(inside, score, 0.0), axis=1, keepdims=True)
    reward = total / lens[0].astype(F32)
    out_ref[...] = jnp.broadcast_to(reward[None], out_ref.shape)


def reward_of(lengths, stats, width, n_dp):
    return pl.pallas_call(
        functools.partial(reward_kernel, width),
        out_shape=jax.ShapeDtypeStruct((n_dp, 1, LANES), F32),
        grid_spec=pltpu.PrefetchScalarGridSpec(
            num_scalar_prefetch=1,
            grid=(1,),
            in_specs=[pl.BlockSpec(stats.shape, lambda i, s: (0, 0, 0))],
            out_specs=pl.BlockSpec((n_dp, 1, LANES), lambda i, s: (0, 0, 0)),
        ),
        compiler_params=pltpu.CompilerParams(vmem_limit_bytes=16 * 2**20),
        cost_estimate=pl.CostEstimate(flops=10000, bytes_accessed=90000, transcendentals=512),
        name="reward",
    )(lengths, stats)


def gradient_kernel(width, distances, place, stats_ref, resid_ref, both_ref, *refs):
    count = len(distances) + 1
    shards = refs[:count]
    send_ref, keep_ref, d_ref, both_halves = refs[count:]
    rows, feat = resid_ref.shape
    heads = shards[0].shape[1]
    groups = width // heads
    used = place[2]
    scale, score, inside = row_terms(stats_ref, used, width)
    weight = jnp.where(inside, scale, 0.0) / used.astype(F32)
    minus = weight * scale * score * (1.0 / width)
    plus = jnp.broadcast_to(weight, (LANES, rows)).T
    minus = jnp.broadcast_to(minus, (LANES, rows)).T
    both = both_ref[...]
    pooled = []
    for part in range(feat // LANES):
        at = slice(part * LANES, (part + 1) * LANES)
        resid = resid_ref[:, at]
        d_ref[:, at] = (plus * both[:, at] - minus * resid).astype(BF16)
        pooled.append(jnp.sum(plus * resid, axis=0, keepdims=True))
    pooled = jnp.concatenate(pooled, axis=1)
    half = width // NCORE
    extra = send_ref.shape[0] - half
    first = lax.broadcasted_iota(jnp.int32, (extra, feat), 0) == 0
    pooled = jnp.where(first, pooled, 0.0).astype(BF16)
    send_ref[half:, :] = pooled
    keep_ref[half:, :] = pooled
    for i, distance in enumerate(distances):
        group = lax.rem(place[0] + (distance + groups), groups)
        stays = (lax.div(group, groups // NCORE) == place[1]).astype(jnp.int32)
        at = stays * half + lax.rem(group, groups // NCORE) * heads
        block = dot(shard_of(shards, i), d_ref[...], 0, 0).astype(BF16)
        both_halves[pl.ds(pl.multiple_of(at, heads), heads), :] = block
    send_ref[:half, :] = both_halves[:half, :]
    keep_ref[:half, :] = both_halves[half:, :]


def gradient_halves(place, stats, resid, both, parts, half_ext, width):
    rows, feat = resid.shape
    shards = flatten(parts)
    here = pl.BlockSpec(memory_space=pltpu.VMEM)
    half = jax.ShapeDtypeStruct((half_ext, feat), BF16)
    return pl.pallas_call(
        functools.partial(gradient_kernel, width, [d for d, _ in parts]),
        out_shape=(half, half),
        in_specs=[pl.BlockSpec(memory_space=pltpu.SMEM)] + [here] * (len(shards) + 3),
        out_specs=(here, here),
        scratch_shapes=[pltpu.VMEM((rows, feat), BF16), pltpu.VMEM((width, feat), BF16)],
        compiler_params=pltpu.CompilerParams(vmem_limit_bytes=32 * 2**20),
        cost_estimate=pl.CostEstimate(flops=550000000, bytes_accessed=4000000, transcendentals=0),
        name="gradient",
    )(place, stats, resid, both, *shards)


def weigh_kernel(place, costs_ref, order_ref, keep_ref, got_ref, out_ref, loss_ref, row_ref):
    seqs = costs_ref.shape[0]
    rewards = -costs_ref[...].reshape(seqs, LANES)
    order = order_ref[...]
    seq = lax.broadcasted_iota(jnp.int32, (seqs, LANES), 0)
    picked = jnp.sum(jnp.where(seq == order, rewards, 0.0), axis=0, keepdims=True)
    lane = lax.broadcasted_iota(jnp.int32, (1, LANES), 1)
    chosen = lane % 2 == 0
    partner = jnp.where(chosen, pltpu.roll(picked, LANES - 1, 1), pltpu.roll(picked, 1, 1))
    margin = jnp.where(chosen, picked - partner, partner - picked)
    sig = 1.0 / (1.0 + jnp.exp(margin))
    dreward = jnp.where(chosen, -sig, sig)
    me = place[3]
    own = jnp.sum(jnp.where(order == me, dreward, 0.0), axis=1, keepdims=True)
    sib = jnp.sum(jnp.where(order == (me ^ 1), dreward, 0.0), axis=1, keepdims=True)
    out_ref[...] = (keep_ref[...].astype(F32) * own + got_ref[...].astype(F32) * sib).astype(BF16)
    each = jnp.maximum(-margin, 0.0) + jnp.log1p(jnp.exp(-jnp.abs(margin)))
    counted = chosen & (lane < seqs)
    loss_ref[...] = jnp.sum(jnp.where(counted, each, 0.0), axis=1, keepdims=True)
    at = lax.broadcasted_iota(jnp.int32, (seqs, LANES), 1)
    row = jnp.sum(jnp.where(seq == at, rewards, 0.0), axis=0, keepdims=True)
    row_ref[...] = row[:, :seqs]


def weigh(place, costs, order, keep, got):
    flat = lambda a: pl.BlockSpec(a.shape, lambda i, s: (0,) * len(a.shape))
    return pl.pallas_call(
        weigh_kernel,
        out_shape=(
            jax.ShapeDtypeStruct(keep.shape, BF16),
            jax.ShapeDtypeStruct((1, 1), F32),
            jax.ShapeDtypeStruct((1, costs.shape[0]), F32),
        ),
        grid_spec=pltpu.PrefetchScalarGridSpec(
            num_scalar_prefetch=1,
            grid=(1,),
            in_specs=[flat(costs), flat(order), flat(keep), flat(got)],
            out_specs=(
                flat(keep),
                pl.BlockSpec((1, 1), lambda i, s: (0, 0)),
                pl.BlockSpec((1, costs.shape[0]), lambda i, s: (0, 0)),
            ),
        ),
        compiler_params=pltpu.CompilerParams(vmem_limit_bytes=16 * 2**20),
        cost_estimate=pl.CostEstimate(flops=1000000, bytes_accessed=2000000, transcendentals=128),
        name="weigh",
    )(place, costs, order, keep, got)


def finish_kernel(half, place, mine_ref, other_ref, gain_ref, head_ref, grad_ref, ghead_ref, ggain_ref):
    step = pl.program_id(0)

    @pl.when(step == place[1])
    def _():
        grad_ref[...] = mine_ref[:half, :].astype(F32)

    @pl.when(step != place[1])
    def _():
        grad_ref[...] = other_ref[:half, :].astype(F32)

    pooled = mine_ref[half : half + 16, :].astype(F32)[:1]
    ghead_ref[...] = gain_ref[...] * pooled
    ggain_ref[...] = head_ref[...] * pooled


def finish(place, mine, other, gain_final, w_head, half):
    feat = mine.shape[1]
    flat = pl.BlockSpec(mine.shape, lambda i, s: (0, 0))
    share = pl.BlockSpec((1, feat), lambda i, s: (0, s[0]))
    line = pl.BlockSpec((1, feat), lambda i, s: (0, 0))
    return pl.pallas_call(
        functools.partial(finish_kernel, half),
        out_shape=(
            jax.ShapeDtypeStruct((NCORE * half, feat), F32),
            jax.ShapeDtypeStruct((1, feat), F32),
            jax.ShapeDtypeStruct((1, feat), F32),
        ),
        grid_spec=pltpu.PrefetchScalarGridSpec(
            num_scalar_prefetch=1,
            grid=(NCORE,),
            in_specs=[flat, flat, share, share],
            out_specs=(pl.BlockSpec((half, feat), lambda i, s: (i, 0)), line, line),
        ),
        compiler_params=pltpu.CompilerParams(vmem_limit_bytes=16 * 2**20),
        cost_estimate=pl.CostEstimate(flops=1000000, bytes_accessed=4000000, transcendentals=0),
        name="finish",
    )(place, mine, other, gain_final[None], w_head[None])


def body(
    hidden_rows,
    lengths,
    pair_order,
    gain_attn,
    w_query,
    key_weight,
    value_weight,
    w_out,
    gain_final,
    w_head,
):
    rows, width = hidden_rows.shape
    n_mp = lax.axis_size("mp")
    n_dp = lax.axis_size("dp")
    feat = width // n_mp
    me = lax.axis_index("dp").astype(jnp.int32)
    core = me % NCORE
    along_x, along_z = dp_groups()
    place = jnp.stack([lax.axis_index("mp").astype(jnp.int32), core, lengths[0], me])

    mixed = front(hidden_rows, lengths, gain_attn, w_query, key_weight, value_weight)
    mixed, w_out, hidden_rows, gain_final, w_head = lax.optimization_barrier(
        (mixed, w_out, hidden_rows, gain_final, w_head)
    )
    piece_rows = w_out.shape[0] // NEAR
    my_near = (me // (NZ * NCORE)) * NCORE + core
    w_piece = lax.dynamic_slice_in_dim(w_out, my_near * piece_rows, piece_rows, 0)
    w_piece = w_piece.reshape(piece_rows, n_mp, feat).swapaxes(0, 1)
    parts, w_piece = ring(mixed, w_piece)
    w_piece = lax.all_to_all(w_piece, "mp", 0, 0, tiled=True)
    w_mine = swap(jnp.broadcast_to(w_piece[None], (NX,) + w_piece.shape), along_x)
    w_other = to_sibling(w_mine)

    x_cols = lax.dynamic_slice_in_dim(hidden_rows, place[0] * feat, feat, 1)
    both = lax.dynamic_slice_in_dim(gain_final * w_head, place[0] * feat, feat, 0)[None]
    resid, stats = project(place, parts, w_mine, w_other, x_cols, both)
    stats = lax.all_to_all(stats, "mp", 0, 0, tiled=True)
    reward, stats = lax.optimization_barrier((reward_of(lengths, stats, width, n_dp), stats))
    costs = -lax.all_to_all(reward, "dp", 0, 0, tiled=True)
    costs = jnp.maximum(lax.optimization_barrier(costs), jnp.finfo(F32).min)
    costs = jnp.minimum(lax.optimization_barrier(costs), jnp.finfo(F32).max)

    half = width // NCORE
    piece = -(-(half + 16) // (NX * NZ * 8)) * 8
    half_ext = piece * NX * NZ
    send, keep = gradient_halves(place, stats, resid, both, parts, half_ext, width)
    got = to_sibling(send)
    seqs = pair_order.shape[0]
    order = jnp.pad(pair_order, (0, LANES - seqs), constant_values=-1)[None]
    summed, loss, reward_row = weigh(place, costs, order, keep, got)

    got = swap(summed.reshape(NX, NZ * piece, feat), along_x)
    summed = jnp.sum(got.astype(F32), axis=0).astype(BF16)
    got = swap(summed.reshape(NZ, piece, feat), along_z)
    mine = jnp.sum(got.astype(F32), axis=0).astype(BF16)
    got = swap(jnp.broadcast_to(mine[None], (NZ, piece, feat)), along_z)
    got = swap(jnp.broadcast_to(got.reshape(1, NZ * piece, feat), (NX, NZ * piece, feat)), along_x)
    got = got.reshape(half_ext, feat)
    other = to_sibling(got)
    grad_out_proj, grad_head, grad_gain = finish(place, got, other, gain_final, w_head, half)
    return (loss[0, 0], reward_row[0], grad_out_proj, grad_head[0], grad_gain[0])


def solution(mesh):
    placed = (
        P("dp", None),
        P("dp"),
        P(),
        P(),
        P(None, "mp"),
        P(None, "mp"),
        P(None, "mp"),
        P("mp", None),
        P(),
        P(),
    )
    return jax.shard_map(
        body,
        mesh=mesh,
        in_specs=placed,
        out_specs=(P(), P(), P(None, "mp"), P("mp"), P("mp")),
        check_vma=False,
    )
```
